32 devices in a mesh: tok: 8 (over z, y), tp: 4 (over x, core).
Axes of the slice: x: 2, y: 2, z: 4, core: 2. Of those that a mesh axis runs over, the one named last changes fastest.
Arguments:
- block_input: bfloat16 [24, 1152, 1024], P('tok', 'tp'), may hold values from -6 to 6
- condition: bfloat16 [24, 1152], P('tok'), may hold values from -6 to 6
- timesteps: int32 [24], P('tok'), may hold values from 0 to 999
- head_mask: int32 [24, 16], P('tok', 'tp'), may hold values from 0 to 1, as said below
- group_mask: int32 [24, 16], P('tok', 'tp'), may hold values from 0 to 1, as said below
- w_ada: bfloat16 [1152, 6, 1152], P('tok', None, 'tp'), may hold values from -0.176776695 to 0.176776695
- b_ada: bfloat16 [6, 1152], P(None, 'tp'), may hold values from -2 to 2
- w_qkv: bfloat16 [1152, 3, 1152], P('tok', None, 'tp'), may hold values from -0.176776695 to 0.176776695
- b_qv: bfloat16 [2, 1152], P(None, 'tp'), may hold values from -2 to 2
- w_out: bfloat16 [1152, 1152], P('tp', 'tok'), may hold values from -0.70710678 to 0.70710678
- b_out: bfloat16 [1152], P('tp'), may hold values from -2 to 2
- w_up: bfloat16 [1152, 4608], P('tok', 'tp'), may hold values from -0.176776695 to 0.176776695
- b_up: bfloat16 [4608], P('tp'), may hold values from -2 to 2
- w_down: bfloat16 [4608, 1152], P('tp', 'tok'), may hold values from -0.176776695 to 0.176776695
- b_down: bfloat16 [1152], P('tp'), may hold values from -2 to 2
- w_head: bfloat16 [256, 16], P('tok', 'tp'), may hold values from -0.375 to 0.375
- b_head: bfloat16 [16], P('tp'), may hold values from -2.5 to 2.5
- w_group: bfloat16 [256, 16], P('tok', 'tp'), may hold values from -0.375 to 0.375
- b_group: bfloat16 [16], P('tp'), may hold values from -2.5 to 2.5
- cotangent: bfloat16 [24, 1152, 1024], P('tok', 'tp'), may hold values from -6 to 6
Outputs:
- block_output: bfloat16 [24, 1152, 1024], P('tok', 'tp')
- grad_input: float32 [24, 1152, 1024], P('tok', 'tp')
- grad_condition: float32 [24, 1152], P('tok')
- grad_w_ada: float32 [1152, 6, 1152], P('tok', None, 'tp')
- grad_b_ada: float32 [6, 1152], P(None, 'tp')
- grad_w_qkv: float32 [1152, 3, 1152], P('tok', None, 'tp')
- grad_b_qv: float32 [2, 1152], P(None, 'tp')
- grad_w_out: float32 [1152, 1152], P('tp', 'tok')
- grad_b_out: float32 [1152], P('tp')
- grad_w_up: float32 [1152, 4608], P('tok', 'tp')
- grad_b_up: float32 [4608], P('tp')
- grad_w_down: float32 [4608, 1152], P('tp', 'tok')
- grad_b_down: float32 [1152], P('tp')
- grad_w_head: float32 [256, 16], P('tok', 'tp')
- grad_b_head: float32 [16], P('tp')
- grad_w_group: float32 [256, 16], P('tok', 'tp')
- grad_b_group: float32 [16], P('tp')
The draws below stay inside these ranges and needn't reach their ends.
Inputs may be any that keep to these rules, and one draw needn't show every extreme that they name: `head_mask`: an image with timestep t keeps exactly 16 - (3 * 16 * t) // 4000 heads; which ones varies from image to image. `group_mask`: an image with timestep t keeps exactly 16 - (3 * 16 * t) // 4000 channel groups; which ones varies from image to image.
All inputs are finite; a program needn't handle non-finite values.
Results may differ from the reference program's by a relative error of at most 0.009.
Values may be sent and summed in bfloat16 or wider, within the bound.
A program may use at most 192 MiB of HBM per device.

```python
import math
import jax
import jax.numpy as jnp
from jax import lax

D = 1152
H = 16
HD = 72
FF = 4608
FREQ = 256
GROUPS = 16
LEN = 1024
IMAGES = 24


def timing(key):
    first = jax.random.randint(jax.random.fold_in(key, 11), (IMAGES,), 0, 1000)
    second = jax.random.randint(jax.random.fold_in(key, 12), (IMAGES,), 0, 1000)
    return 999 - first * second // 999


def kept_units(key, steps, units):
    keys_all = jax.random.split(key, IMAGES)
    ranks = jax.vmap(lambda single: jax.random.permutation(single, units))(keys_all)
    active = units - 3 * units * steps // 4000
    return (ranks < active[:, None]).astype(jnp.int32)


def normal_part(key, shape, scale):
    return jnp.clip(jax.random.normal(key, shape, jnp.float32), -6.0, 6.0) * scale


def draw_timesteps(key, part):
    return timing(key).astype(jnp.int32)


def draw_head_mask(key, part):
    steps = timing(key)
    key = jax.random.fold_in(key, 2)
    return kept_units(key, steps, H)


def draw_group_mask(key, part):
    steps = timing(key)
    key = jax.random.fold_in(key, 3)
    return kept_units(key, steps, GROUPS)


def draw_block_input(key, part):
    key = jax.random.fold_in(key, 21)
    return normal_part(key, (IMAGES, D, LEN), 1.0).astype(jnp.bfloat16)


def draw_cotangent(key, part):
    key = jax.random.fold_in(key, 22)
    return normal_part(key, (IMAGES, D, LEN), 1.0).astype(jnp.bfloat16)


def draw_condition(key, part):
    key = jax.random.fold_in(key, 23)
    return normal_part(key, (IMAGES, D), 1.0).astype(jnp.bfloat16)


def draw_w_ada(key, part):
    key = jax.random.fold_in(key, 24)
    return normal_part(key, (D, 6, D), D ** (-0.5)).astype(jnp.bfloat16)


def draw_w_qkv(key, part):
    key = jax.random.fold_in(key, 25)
    return normal_part(key, (D, 3, D), D ** (-0.5)).astype(jnp.bfloat16)


def draw_w_out(key, part):
    key = jax.random.fold_in(key, 26)
    return normal_part(key, (D, D), (D // 16) ** (-0.5)).astype(jnp.bfloat16)


def draw_w_up(key, part):
    key = jax.random.fold_in(key, 27)
    return normal_part(key, (D, FF), D ** (-0.5)).astype(jnp.bfloat16)


def draw_w_down(key, part):
    key = jax.random.fold_in(key, 28)
    return normal_part(key, (FF, D), (FF // 4) ** (-0.5)).astype(jnp.bfloat16)


def shard_levels(rng, dims, shards, low, high):
    factor_of, own = 1.0, jax.random.fold_in(rng, 6)
    for dim, shards_of in shards:
        draws = jnp.exp(jax.random.uniform(jax.random.fold_in(own, dim), (shards_of,), jnp.float32, low / len(shards), high / len(shards)))
        factor_of = factor_of * jnp.repeat(draws, dims[dim] // shards_of).reshape([-1 if axis == dim else 1 for axis in range(len(dims))])
    return factor_of


def gaussian(stream_key, shape, scale, most, pieces=(), kind=jnp.bfloat16):
    values = jax.random.normal(stream_key, shape, jnp.float32) * scale
    if len(pieces) > 0:
        values = shard_levels(stream_key, shape, pieces, -0.22, 0.18) * values
    return jnp.clip(values, min=-most, max=most).astype(kind)


def setup_inputs(seed: int = 0) -> dict:
    key_of = jax.random.split(jax.random.key(seed), 21)
    return {
        "block_input": draw_block_input(jax.random.fold_in(key_of[20], 71), 0),
        "condition": draw_condition(jax.random.fold_in(key_of[20], 71), 0),
        "timesteps": draw_timesteps(jax.random.fold_in(key_of[20], 71), 0),
        "head_mask": draw_head_mask(jax.random.fold_in(key_of[20], 71), 0),
        "group_mask": draw_group_mask(jax.random.fold_in(key_of[20], 71), 0),
        "w_ada": draw_w_ada(jax.random.fold_in(key_of[20], 71), 0),
        "b_ada": gaussian(key_of[6], (6, D), 0.3, 2.0, ((1, 4),)),
        "w_qkv": draw_w_qkv(jax.random.fold_in(key_of[20], 71), 0),
        "b_qv": gaussian(key_of[8], (2, D), 0.3, 2.0, ((1, 4),)),
        "w_out": draw_w_out(jax.random.fold_in(key_of[20], 71), 0),
        "b_out": gaussian(key_of[10], (D,), 0.3, 2.0, ((0, 4),)),
        "w_up": draw_w_up(jax.random.fold_in(key_of[20], 71), 0),
        "b_up": gaussian(key_of[12], (FF,), 0.3, 2.0, ((0, 4),)),
        "w_down": draw_w_down(jax.random.fold_in(key_of[20], 71), 0),
        "b_down": gaussian(key_of[14], (D,), 0.3, 2.0, ((0, 4),)),
        "w_head": gaussian(key_of[15], (FREQ, H), FREQ ** -0.5, 0.375, ((0, 8), (1, 4))),
        "b_head": gaussian(key_of[16], (H,), 0.3, 2.5, ((0, 4),)),
        "w_group": gaussian(key_of[17], (FREQ, GROUPS), FREQ ** -0.5, 0.375, ((0, 8), (1, 4))),
        "b_group": gaussian(key_of[18], (GROUPS,), 0.3, 2.5, ((0, 4),)),
        "cotangent": draw_cotangent(jax.random.fold_in(key_of[20], 71), 0),
    }


@jax.custom_vjp
def low(v):
    return lax.optimization_barrier(v.astype(jnp.bfloat16)).astype(jnp.float32)

@jax.custom_vjp
def low_back(v):
    return v

def low_keep(v):
    return (low(v), None)

def low_pass(kept, grad):
    return (grad,)

def back_keep(v):
    return (v, None)

def back_low(kept, grad):
    return (low(grad),)
low.defvjp(low_keep, low_pass)
low_back.defvjp(back_keep, back_low)
eps_norm = 1e-06
exact_mode = lax.Precision.HIGHEST

def embed_time(timesteps):
    half_width = FREQ // 2
    indices = jnp.arange(half_width, dtype=jnp.float32)
    freq_rates = jnp.exp(-math.log(10000.0) * indices / half_width)
    angles = timesteps.astype(jnp.float32)[:, None] * freq_rates[None, :]
    return jnp.concatenate([jnp.cos(angles), jnp.sin(angles)], axis=1)

def pick_mod(modulation, index):
    return modulation[:, index][:, None, :]

def layer_norm(values):
    centre = lax.optimization_barrier(jnp.mean(values, axis=-1, keepdims=True))
    spread = lax.optimization_barrier(jnp.mean(values * values, axis=-1, keepdims=True)) - centre * centre
    return (values - centre) * lax.rsqrt(spread + eps_norm)

def attend_image(inputs):
    queries, keys_in, values_in, gates = inputs
    query_heads = queries.reshape(LEN, H, HD)
    key_heads = keys_in.reshape(LEN, H, HD)
    value_heads = values_in.reshape(LEN, H, HD)
    scores = jnp.einsum('qhe,khe->hqk', query_heads, key_heads, precision=exact_mode) * HD ** (-0.5)
    scores = low_back(scores)
    weights = jax.nn.softmax(scores, axis=-1)
    mixed = jnp.einsum('hqk,khe->qhe', low(weights), value_heads, precision=exact_mode)
    mixed = low_back(mixed)
    return low(mixed * gates[None, :, None]).reshape(LEN, D)

def reference(block_input, condition, timesteps, head_mask, group_mask, w_ada, b_ada, w_qkv, b_qv, w_out, b_out, w_up, b_up, w_down, b_down, w_head, b_head, w_group, b_group, cotangent):
    time_feat = low(embed_time(timesteps))
    head_on = head_mask.astype(jnp.float32)
    group_on = group_mask.astype(jnp.float32)

    def forward(input_rows, cond_in, ada_w, ada_b, qkv_w, qv_b, out_w, out_b, up_w, up_b, down_w, down_b, head_w, head_b, group_w, group_b):
        cond_act = low(jax.nn.silu(cond_in))
        modulation = jnp.einsum('bd,dke->bke', cond_act, ada_w, precision=exact_mode) + ada_b
        head_gate = head_on * jax.nn.sigmoid(jnp.dot(time_feat, head_w, precision=exact_mode) + head_b)
        group_gate = group_on * jax.nn.sigmoid(jnp.dot(time_feat, group_w, precision=exact_mode) + group_b)
        row_data = jnp.transpose(input_rows, (0, 2, 1))
        attn_in = low(layer_norm(row_data) * (1.0 + pick_mod(modulation, 1)) + pick_mod(modulation, 0))
        projected = jnp.einsum('bld,dke->blke', attn_in, qkv_w, precision=exact_mode)
        queries = low(low_back(projected[:, :, 0] + qv_b[0]))
        keys_in = low(low_back(projected[:, :, 1]))
        values_in = low(low_back(projected[:, :, 2] + qv_b[1]))
        concat = lax.map(jax.checkpoint(attend_image), (queries, keys_in, values_in, head_gate))
        branch_one = low_back(jnp.einsum('bld,de->ble', concat, out_w, precision=exact_mode) + out_b)
        mid_rows = row_data + pick_mod(modulation, 2) * branch_one
        mlp_in = low(layer_norm(mid_rows) * (1.0 + pick_mod(modulation, 4)) + pick_mod(modulation, 3))
        hidden_pre = low_back(jnp.einsum('bld,df->blf', mlp_in, up_w, precision=exact_mode) + up_b)
        group_cols = jnp.repeat(group_gate, FF // GROUPS, axis=1)
        hidden = low(jax.nn.gelu(hidden_pre, approximate=True) * group_cols[:, None, :])
        branch_two = low_back(jnp.einsum('blf,fe->ble', hidden, down_w, precision=exact_mode) + down_b)
        return jnp.transpose(mid_rows + pick_mod(modulation, 5) * branch_two, (0, 2, 1))
    primals = tuple((array.astype(jnp.float32) for array in (block_input, condition, w_ada, b_ada, w_qkv, b_qv, w_out, b_out, w_up, b_up, w_down, b_down, w_head, b_head, w_group, b_group)))
    output, pullback = jax.vjp(forward, *primals)
    grads = pullback(cotangent.astype(jnp.float32))
    return (output.astype(jnp.bfloat16), grads[0], grads[1], grads[2], grads[3], grads[4], grads[5], grads[6], grads[7], grads[8], grads[9], grads[10], grads[11], grads[12], grads[13], grads[14], grads[15])
```

```python
import functools
import math

import jax
import jax.numpy as jnp
from jax import lax
from jax.experimental import pallas as pl
from jax.experimental.pallas import tpu as pltpu
from jax.sharding import PartitionSpec as P

D = 1152
HD = 72
HP = 80
FF = 4608
FREQ = 256
GROUPS = 16
GW = FF // GROUPS
LEN = 1024
EPS = 1e-06
SCALE = HD**-0.5
SCALE2 = SCALE / math.log(2.0)

f32 = jnp.float32
bf16 = jnp.bfloat16
exact_mode = lax.Precision.HIGHEST


def dot(a, b, ca, cb):
    return lax.dot_general(a, b, (((ca,), (cb,)), ((), ())), preferred_element_type=f32)


def embed_time(timesteps):
    half_width = FREQ // 2
    indices = jnp.arange(half_width, dtype=f32)
    freq_rates = jnp.exp(-math.log(10000.0) * indices / half_width)
    angles = timesteps.astype(f32)[:, None] * freq_rates[None, :]
    return jnp.concatenate([jnp.cos(angles), jnp.sin(angles)], axis=1)


def attn_fwd_kernel(gate_ref, q_ref, k_ref, v_ref, mixed_ref, concat_ref, lse_ref):
    gate = gate_ref[pl.program_id(0)]
    keys = k_ref[0].T
    s = jnp.dot(keys, q_ref[0], preferred_element_type=f32)
    top = jnp.max(s, axis=0, keepdims=True)
    p = jnp.exp2((s - top) * SCALE2).astype(bf16)
    out = jnp.dot(v_ref[0], p, preferred_element_type=f32)
    total = out[HD : HD + 1]
    mixed = out * (1.0 / total)
    mixed_ref[0] = mixed
    concat_ref[0] = (mixed * gate).astype(bf16)
    lse_ref[0] = top * SCALE2 + jnp.log2(total)


def attn_fwd(gate, qkv):
    heads = gate.shape[0]
    spec = pl.BlockSpec((1, HP, LEN), lambda i: (i, 0, 0))
    row = pl.BlockSpec((1, 1, LEN), lambda i: (i, 0, 0))
    return pl.pallas_call(
        attn_fwd_kernel,
        grid=(heads,),
        in_specs=[pl.BlockSpec(memory_space=pltpu.SMEM)]
        + [pl.BlockSpec((1, HP, LEN), lambda i, k=k: (i + k * heads, 0, 0)) for k in range(3)],
        out_specs=[spec, spec, row],
        out_shape=[
            jax.ShapeDtypeStruct((heads, HP, LEN), f32),
            jax.ShapeDtypeStruct((heads, HP, LEN), bf16),
            jax.ShapeDtypeStruct((heads, 1, LEN), f32),
        ],
        compiler_params=pltpu.CompilerParams(vmem_limit_bytes=48 * 2**20),
        cost_estimate=pl.CostEstimate(
            flops=heads * 4 * LEN * LEN * 256,
            bytes_accessed=heads * HP * LEN * 14,
            transcendentals=heads * LEN * LEN,
        ),
        name="attn_fwd",
    )(gate, qkv, qkv, qkv)


def attn_bwd_kernel(
    chunk, gate_ref, q_ref, k_ref, v_ref, gc_ref, mixed_ref, lse_ref, dq_ref, dk_ref, dv_ref, hg_ref
):
    gate = gate_ref[pl.program_id(0)]
    keys_t = k_ref[0]
    keys = keys_t.T
    values = v_ref[0].T
    gc = gc_ref[0]
    inner = jnp.sum(mixed_ref[0] * gc, axis=0, keepdims=True)
    hg_ref[0] = inner
    delta = gate * inner
    grad = (gate * gc).astype(bf16)
    dv = jnp.zeros((LEN, HP), f32)
    dk = jnp.zeros((LEN, HP), f32)
    for j in range(LEN // chunk):
        part = slice(j * chunk, (j + 1) * chunk)
        q = q_ref[0, :, part]
        do = grad[:, part]
        s = jnp.dot(keys, q, preferred_element_type=f32)
        p = jnp.exp2(s * SCALE2 - lse_ref[0, :, part])
        dp = jnp.dot(values, do, preferred_element_type=f32)
        ds = (p * (dp - delta[:, part])).astype(bf16)
        dv = dv + jnp.dot(p.astype(bf16), do.T, preferred_element_type=f32)
        dk = dk + jnp.dot(ds, q.T, preferred_element_type=f32)
        dq = jnp.dot(keys_t, ds, preferred_element_type=f32)
        dq_ref[0, :, part] = (dq * SCALE).astype(bf16)
    dk_ref[0] = (dk * SCALE).T.astype(bf16)
    dv_ref[0] = dv.T.astype(bf16)


def attn_bwd(gate, qkv, gc, mixed, lse):
    heads = gate.shape[0]
    spec = pl.BlockSpec((1, HP, LEN), lambda i: (i, 0, 0))
    row = pl.BlockSpec((1, 1, LEN), lambda i: (i, 0, 0))
    grads = jax.ShapeDtypeStruct((heads, HP, LEN), bf16)
    return pl.pallas_call(
        functools.partial(attn_bwd_kernel, 256),
        grid=(heads,),
        in_specs=[pl.BlockSpec(memory_space=pltpu.SMEM)]
        + [pl.BlockSpec((1, HP, LEN), lambda i, k=k: (i + k * heads, 0, 0)) for k in range(3)]
        + [spec, spec, row],
        out_specs=[spec, spec, spec, row],
        out_shape=[grads, grads, grads, jax.ShapeDtypeStruct((heads, 1, LEN), f32)],
        compiler_params=pltpu.CompilerParams(vmem_limit_bytes=48 * 2**20),
        cost_estimate=pl.CostEstimate(
            flops=heads * 10 * LEN * LEN * 256,
            bytes_accessed=heads * HP * LEN * 20,
            transcendentals=heads * LEN * LEN,
        ),
        name="attn_bwd",
    )(gate, qkv, qkv, qkv, gc, mixed, lse)


def make_body(NT, NP):
    NX = NP // 2
    SUB = NT // NP
    RB = D // NT
    CB = D // NP
    T = LEN // NX
    wide = 4 if NT >= 16 else 2
    tall = NT // wide
    cycle = [r * wide for r in reversed(range(tall))]
    for r in range(tall):
        cols = list(range(1, wide))
        cycle += [r * wide + c for c in (cols if r % 2 == 0 else cols[::-1])]
    place = [cycle.index(t) for t in range(NT)]
    right_pairs = [(cycle[i], cycle[(i + 1) % NT]) for i in range(NT)]
    left_pairs = [(b, a) for a, b in right_pairs]
    n_right = NT // 2
    n_left = NT - 1 - n_right

    def hop(v, right):
        return lax.ppermute(v, "tok", right_pairs if right else left_pairs)

    def tp_xor(v, r):
        return lax.ppermute(v, "tp", [(p, p ^ r) for p in range(NP)])

    def tok_shift(v, k):
        return lax.ppermute(v, "tok", [(t, (t + k) % NT) for t in range(NT)])

    def swap_tokens(v, k, axis):
        if k == 0:
            return v
        parts = [lax.slice_in_dim(v, (j ^ k) * T, (j ^ k) * T + T, axis=axis) for j in range(NX)]
        return jnp.concatenate(parts, axis=axis)

    def body(
        block_input,
        condition,
        timesteps,
        head_mask,
        group_mask,
        w_ada,
        b_ada,
        w_qkv,
        b_qv,
        w_out,
        b_out,
        w_up,
        b_up,
        w_down,
        b_down,
        w_head,
        b_head,
        w_group,
        b_group,
        cotangent,
    ):
        I = condition.shape[0]
        HL = head_mask.shape[1]
        GL = group_mask.shape[1]
        FL = w_up.shape[1]
        FR = FREQ // NT
        t = lax.axis_index("tok")
        p = lax.axis_index("tp")
        xi = p // 2
        my_place = jnp.array(place, jnp.int32)[t]
        ring = jnp.array(cycle, jnp.int32)

        def block_of(d):
            tt = ring[(my_place + d + NT) % NT]
            return jnp.bitwise_xor(tt // SUB, p) * SUB + tt % SUB

        def gather_rows(shard):
            pieces = [(0, shard)]
            v = shard
            for d in range(1, n_right + 1):
                v = hop(v, True)
                pieces.append((-d, v))
            v = shard
            for d in range(1, n_left + 1):
                v = hop(v, False)
                pieces.append((d, v))
            full = jnp.zeros((NT,) + shard.shape, shard.dtype)
            for d, v in pieces:
                full = lax.dynamic_update_slice(full, v[None], (block_of(d), 0, 0))
            return full.reshape(D, -1)

        def scatter_rows(full):
            blocks = full.reshape(NT, RB, -1)

            def own(d):
                return lax.dynamic_index_in_dim(blocks, block_of(d), 0, keepdims=False)

            total = own(0)
            for count, right in ((n_right, True), (n_left, False)):
                v = None
                for d in range(count, 0, -1):
                    term = own(d if right else -d)
                    v = hop((term if v is None else term + v.astype(f32)).astype(bf16), right)
                total = total + v.astype(f32)
            return total

        def own_order(v, axis):
            parts = [
                lax.dynamic_slice_in_dim(v, jnp.bitwise_xor(j, xi) * T, T, axis=axis)
                for j in range(NX)
            ]
            return jnp.concatenate(parts, axis=axis)

        xin = own_order(block_input, 2)
        cot_in = own_order(cotangent, 2)

        def gather_features(own):
            blocks = [None] * NP
            for k in range(NX):
                v = own if k == 0 else swap_tokens(tp_xor(own, 2 * k), k, 1)
                blocks[2 * k] = v
                blocks[2 * k + 1] = tp_xor(v, 1)
            return blocks

        rows_blocks = [gather_features(xin[i]) for i in range(I)]
        rows_full = [jnp.concatenate(b, axis=0) for b in rows_blocks]

        time_feat = embed_time(timesteps).astype(bf16)
        cond_wide = condition.astype(f32)
        cond_act = jax.nn.silu(cond_wide).astype(bf16)
        message = jnp.concatenate(
            [cond_act.reshape(I, NT, RB), time_feat.reshape(I, NT, FR)], axis=2
        ).transpose(1, 0, 2)
        rolled = lax.dynamic_slice_in_dim(
            jnp.concatenate([message, message], axis=0), t, NT, axis=0
        )
        feats = jnp.stack([rolled[0]] + [tok_shift(rolled[k], k) for k in range(1, NT)])
        feats = feats.reshape(NT * I, RB + FR)
        cond_rows, time_rows = feats[:, :RB], feats[:, RB:]
        w_gates = jnp.concatenate([w_head, w_group], axis=1)
        part = jnp.concatenate(
            [dot(cond_rows, w_ada.reshape(RB, 6 * CB), 1, 0), dot(time_rows, w_gates, 1, 0)],
            axis=1,
        ).reshape(NT, I, -1)
        summed = part[0]
        for k in range(1, NT):
            summed = summed + tok_shift(part[k], NT - k)
        modulation = summed[:, : 6 * CB].reshape(I, 6, CB) + b_ada.astype(f32)
        head_sig = jax.nn.sigmoid(summed[:, 6 * CB : 6 * CB + HL] + b_head.astype(f32))
        group_sig = jax.nn.sigmoid(summed[:, 6 * CB + HL :] + b_group.astype(f32))
        head_gate = head_mask.astype(f32) * head_sig
        group_gate = group_mask.astype(f32) * group_sig
        tp_message = jnp.concatenate(
            [
                modulation.reshape(-1),
                b_out.astype(f32),
                b_down.astype(f32),
                group_gate.reshape(-1),
                b_up.astype(f32),
            ]
        )
        others = [tp_message] + [tp_xor(tp_message, r) for r in range(1, NP)]
        n_mod = I * 6 * CB
        vectors = jnp.stack(
            [m[: n_mod + 2 * CB].reshape(I * 6 + 2, CB) for m in others], axis=1
        ).reshape(I * 6 + 2, D)
        columns = vectors.T

        def mod(i, k):
            return lax.slice_in_dim(columns, i * 6 + k, i * 6 + k + 1, axis=1)

        out_bias = columns[:, I * 6 : I * 6 + 1]
        down_bias = columns[:, I * 6 + 1 : I * 6 + 2]
        base = n_mod + 2 * CB
        gates_x = jnp.concatenate(
            [others[2 * k][base : base + I * GL].reshape(I, GL) for k in range(NX)], axis=1
        )
        gate_cols = jnp.repeat(gates_x, GW, axis=1).T
        up_bias = jnp.concatenate([others[2 * k][base + I * GL :] for k in range(NX)])[:, None]

        qkv_shard = jnp.pad(
            w_qkv.reshape(RB, 3, HL, HD), ((0, 0), (0, 0), (0, 0), (0, HP - HD))
        ).reshape(RB, 3 * HL * HP)
        out_shard = jnp.pad(w_out.T.reshape(RB, HL, HD), ((0, 0), (0, 0), (0, HP - HD))).reshape(
            RB, HL * HP
        )
        up_shard = jnp.concatenate(
            [w_up] + [tp_xor(w_up, 2 * k) for k in range(1, NX)], axis=1
        )
        down_shard = w_down.T
        down_shard = jnp.concatenate(
            [down_shard] + [tp_xor(down_shard, 2 * k) for k in range(1, NX)], axis=1
        )
        qkv_full = gather_rows(qkv_shard)
        out_full = gather_rows(out_shard)
        up_full = gather_rows(up_shard)
        down_full = gather_rows(down_shard)
        qv = b_qv.astype(f32).reshape(2, HL, HD)
        qv_bias = jnp.stack(
            [
                jnp.pad(qv[0], ((0, 0), (0, HP - HD))),
                jnp.zeros((HL, HP), f32),
                jnp.concatenate(
                    [qv[1], jnp.ones((HL, 1), f32), jnp.zeros((HL, HP - HD - 1), f32)], axis=1
                ),
            ]
        ).reshape(3 * HL * HP, 1)

        def stats(v):
            centre = jnp.sum(v, axis=0, keepdims=True) * (1.0 / D)
            square = jnp.sum(v * v, axis=0, keepdims=True) * (1.0 / D)
            return centre, lax.rsqrt(square - centre * centre + EPS)

        fwd = []
        for i in range(I):
            wide_rows = rows_full[i].astype(f32)
            centre, inverse = stats(wide_rows)
            attn_in = ((wide_rows - centre) * inverse * (1.0 + mod(i, 1)) + mod(i, 0)).astype(bf16)
            qkv = (dot(qkv_full, attn_in, 0, 0) + qv_bias).astype(bf16).reshape(3 * HL, HP, LEN)
            mixed, concat, lse = attn_fwd(head_gate[i], qkv)
            concat = concat.reshape(HL * HP, LEN)
            part = dot(out_full, concat, 1, 0).reshape(NX, 2, CB, LEN)
            got = tp_xor(part[:, 1].astype(bf16), 1)
            both = part[:, 0] + got.astype(f32)
            total = both[:, :, :T]
            for k in range(1, NX):
                got = tp_xor(both[:, :, k * T : (k + 1) * T].astype(bf16), 2 * k).astype(f32)
                total = total + jnp.stack([got[j ^ k] for j in range(NX)])
            total_other = tp_xor(total, 1)
            branch_one = jnp.stack([total, total_other], axis=1).reshape(D, T) + out_bias
            fwd.append((centre, inverse, attn_in, qkv, mixed, concat, lse, branch_one))

        mids = []
        for i in range(I):
            branch_one = fwd[i][-1]
            cot_blocks = []
            for k in range(NX):
                v = (
                    cot_in[i, :, :T]
                    if k == 0
                    else tp_xor(cot_in[i, :, k * T : (k + 1) * T], 2 * k)
                )
                cot_blocks += [v, tp_xor(v, 1)]
            cot = jnp.concatenate(cot_blocks, axis=0).astype(f32)
            mid_rows = rows_full[i][:, :T].astype(f32) + mod(i, 2) * branch_one
            centre, inverse = stats(mid_rows)
            normed = (mid_rows - centre) * inverse
            mlp_in = (normed * (1.0 + mod(i, 4)) + mod(i, 3)).astype(bf16)
            grad_two = (mod(i, 5) * cot).astype(bf16)
            pre = dot(up_full, mlp_in, 0, 0) + up_bias
            grad_hid = dot(down_full, grad_two, 0, 0)
            gate = gate_cols[:, i : i + 1]
            inner = jnp.tanh(math.sqrt(2.0 / math.pi) * (pre + 0.044715 * pre * pre * pre))
            act = 0.5 * pre * (1.0 + inner)
            slope = 0.5 * (1.0 + inner) + 0.5 * pre * (1.0 - inner * inner) * math.sqrt(
                2.0 / math.pi
            ) * (1.0 + 3.0 * 0.044715 * pre * pre)
            hidden = (act * gate).astype(bf16)
            grad_pre = (slope * gate * grad_hid).astype(bf16)
            gate_sums = jnp.sum(jnp.sum(grad_hid * act, axis=1).reshape(NX * GL, GW), axis=1)
            up_sums = jnp.sum(grad_pre.astype(f32), axis=1)
            gpart = dot(up_full, grad_pre, 1, 0)
            got = tp_xor(gpart.astype(bf16), 1).reshape(NX, 2, CB, T)
            got = jnp.stack([got[:, 1], got[:, 0]], axis=1).reshape(D, T)
            gnorm = gpart + got.astype(f32)
            shift_sums = jnp.sum(gnorm, axis=1)
            scale_sums = jnp.sum(gnorm * normed, axis=1)
            g = gnorm * (1.0 + mod(i, 4))
            mean_g = jnp.sum(g, axis=0, keepdims=True) * (1.0 / D)
            mean_gn = jnp.sum(g * normed, axis=0, keepdims=True) * (1.0 / D)
            grad_mid = cot + inverse * (g - mean_g - normed * mean_gn)
            gate_one_sums = jnp.sum(grad_mid * branch_one, axis=1)
            grad_one = (mod(i, 2) * grad_mid).astype(bf16)
            out_sums = jnp.sum(grad_one.astype(f32), axis=1)
            own_half = grad_one.reshape(NX, 2, CB, T)[:, 0]
            tok_blocks = [grad_one]
            for k in range(1, NX):
                got = tp_xor(own_half, 2 * k)
                got = jnp.stack([got[j ^ k] for j in range(NX)])
                tok_blocks.append(jnp.stack([got, tp_xor(got, 1)], axis=1).reshape(D, T))
            grad_one_full = jnp.concatenate(tok_blocks, axis=1)
            mid_blocks = [grad_mid[:CB]]
            for k in range(1, NX):
                mid_blocks.append(
                    tp_xor(grad_mid[2 * k * CB : (2 * k + 1) * CB].astype(bf16), 2 * k).astype(f32)
                )
            grad_mid_own = jnp.concatenate(mid_blocks, axis=1)
            bpart = dot(down_full, hidden, 1, 0).reshape(NX, 2, CB, T)
            branch_two = (
                bpart[:, 0]
                + tp_xor(bpart[:, 1].astype(bf16), 1).astype(f32)
                + down_bias.reshape(NX, 2, CB, 1)[:, 0]
            )
            half = lambda v: v.reshape(NX, 2, CB, -1)[:, 0]
            gate_two_sums = jnp.sum(half(cot) * branch_two, axis=2)
            out_half = (half(mid_rows) + half(mod(i, 5)) * branch_two).astype(bf16)
            out_blocks = [out_half[0]] + [tp_xor(out_half[k], 2 * k) for k in range(1, NX)]
            out_own = jnp.concatenate(out_blocks, axis=1)
            down_sums = jnp.sum(grad_two.astype(f32), axis=1)
            mids.append(
                dict(
                    grad_two=grad_two,
                    hidden=hidden,
                    grad_pre=grad_pre,
                    mlp_in=mlp_in,
                    grad_one_full=grad_one_full,
                    grad_mid_own=grad_mid_own,
                    out_own=out_own,
                    sums=(gate_one_sums, shift_sums, scale_sums),
                    gate_two_sums=gate_two_sums,
                    gate_sums=gate_sums,
                    up_sums=up_sums,
                    out_sums=out_sums,
                    down_sums=down_sums,
                )
            )

        block_output = own_order(jnp.stack([m["out_own"] for m in mids]), 2)

        grad_down = sum(dot(m["grad_two"], m["hidden"], 1, 1) for m in mids)
        grad_up = sum(dot(m["mlp_in"], m["grad_pre"], 1, 1) for m in mids)
        grad_down = scatter_rows(grad_down)
        grad_up = scatter_rows(grad_up)

        def x_sum(v):
            total = v[:, :FL]
            for k in range(1, NX):
                got = tp_xor(v[:, k * FL : (k + 1) * FL].astype(bf16), 2 * k)
                total = total + got.astype(f32)
            return total

        grad_down = x_sum(grad_down)
        grad_up = x_sum(grad_up)

        def x_message(k):
            parts = []
            for m in mids:
                for v in m["sums"]:
                    parts.append(v[2 * k * CB : (2 * k + 1) * CB])
                parts.append(m["gate_two_sums"][k])
                parts.append(m["gate_sums"][k * GL : (k + 1) * GL])
            for name, size in (("out_sums", 2 * k * CB), ("down_sums", 2 * k * CB)):
                parts.append(sum(m[name] for m in mids)[size : size + CB])
            parts.append(sum(m["up_sums"] for m in mids)[k * FL : (k + 1) * FL])
            return jnp.concatenate(parts)

        x_total = x_message(0)
        for k in range(1, NX):
            x_total = x_total + tp_xor(x_message(k), 2 * k)
        per = 4 * CB + GL
        per_image = x_total[: I * per].reshape(I, per)
        late_mods = per_image[:, : 4 * CB].reshape(I, 4, CB)
        grad_group_gate = per_image[:, 4 * CB :]
        bias_sums = x_total[I * per :]

        backs = []
        for i in range(I):
            centre, inverse, attn_in, qkv, mixed, concat, lse, _ = fwd[i]
            m = mids[i]
            gc = dot(out_full, m["grad_one_full"], 0, 0).reshape(HL, HP, LEN)
            dq, dk, dv, inner = attn_bwd(head_gate[i], qkv, gc, mixed, lse)
            dqkv = jnp.concatenate([dq, dk, dv], axis=0).reshape(3 * HL * HP, LEN)
            part = dot(qkv_full, dqkv, 1, 0).reshape(NX, 2, CB, LEN)
            got = tp_xor(part[:, 1].astype(bf16), 1)
            both = part[:, 0] + got.astype(f32)
            gnorm = both[0]
            for k in range(1, NX):
                got = tp_xor(both[k].astype(bf16), 2 * k).astype(f32)
                gnorm = gnorm + swap_tokens(got, k, 1)
            normed = (xin[i].astype(f32) - centre) * inverse
            own_cols = columns[:CB]
            g = gnorm * (1.0 + own_cols[:, i * 6 + 1 : i * 6 + 2])
            sums = jnp.stack([jnp.sum(g, axis=0), jnp.sum(g * normed, axis=0)])
            total = sums
            for r in range(1, NP):
                total = total + swap_tokens(tp_xor(sums, r), r // 2, 1)
            grad_in = m["grad_mid_own"] + inverse * (
                g - total[0:1] * (1.0 / D) - normed * (total[1:2] * (1.0 / D))
            )
            backs.append(
                dict(
                    dqkv=dqkv,
                    grad_in=grad_in,
                    shift=jnp.sum(gnorm, axis=1),
                    scale=jnp.sum(gnorm * normed, axis=1),
                    heads=jnp.sum(inner, axis=(1, 2)),
                    q_sums=jnp.sum(dq.astype(f32), axis=2)[:, :HD].reshape(-1),
                    v_sums=jnp.sum(dv.astype(f32), axis=2)[:, :HD].reshape(-1),
                )
            )
        grad_input = own_order(jnp.stack([b["grad_in"] for b in backs]), 2)

        grad_out = sum(
            dot(m["grad_one_full"], f[5], 1, 1) for m, f in zip(mids, fwd)
        )
        grad_out = scatter_rows(grad_out)
        grad_qkv = sum(dot(f[2], b["dqkv"], 1, 1) for f, b in zip(fwd, backs))
        grad_qkv = scatter_rows(grad_qkv)

        grad_mod = jnp.stack(
            [
                jnp.stack([b["shift"] for b in backs]),
                jnp.stack([b["scale"] for b in backs]),
                late_mods[:, 0],
                late_mods[:, 1],
                late_mods[:, 2],
                late_mods[:, 3],
            ],
            axis=1,
        )
        grad_head_gate = jnp.stack([b["heads"] for b in backs])
        head_logit = grad_head_gate * head_mask.astype(f32) * head_sig * (1.0 - head_sig)
        group_logit = grad_group_gate * group_mask.astype(f32) * group_sig * (1.0 - group_sig)
        last = jnp.concatenate(
            [
                jnp.concatenate([grad_mod.reshape(I, -1), head_logit, group_logit], axis=1).reshape(
                    -1
                ),
                sum(b["q_sums"] for b in backs),
                sum(b["v_sums"] for b in backs),
                bias_sums,
            ]
        )
        lasts = jnp.stack([last] + [tok_shift(last, k) for k in range(1, NT)])
        n_head = I * (6 * CB + HL + GL)
        per_all = lasts[:, :n_head].reshape(NT * I, -1)
        mods_all = per_all[:, : 6 * CB]
        logits_all = per_all[:, 6 * CB :]
        biases = jnp.sum(lasts[:, n_head:], axis=0)
        cond_f = cond_rows.astype(f32)
        grad_w_ada = lax.dot_general(
            cond_f, mods_all, (((0,), (0,)), ((), ())), precision=exact_mode
        ).reshape(RB, 6, CB)
        grad_b_ada = jnp.sum(mods_all, axis=0).reshape(6, CB)
        grad_w_gates = lax.dot_general(
            time_rows.astype(f32), logits_all, (((0,), (0,)), ((), ())), precision=exact_mode
        )
        grad_b_gates = jnp.sum(logits_all, axis=0)
        cond_part = lax.dot_general(
            mods_all,
            w_ada.reshape(RB, 6 * CB).astype(f32),
            (((1,), (1,)), ((), ())),
            precision=exact_mode,
        ).reshape(NT, I, RB)
        cond_parts = jnp.stack(
            [cond_part[0]] + [tok_shift(cond_part[k], NT - k) for k in range(1, NT)]
        )
        cond_parts = lax.dynamic_slice_in_dim(
            jnp.concatenate([cond_parts, cond_parts], axis=0), (NT - t) % NT, NT, axis=0
        )
        cond_sum = cond_parts.transpose(1, 0, 2).reshape(I, D)
        cond_total = cond_sum
        for r in range(1, NP):
            cond_total = cond_total + tp_xor(cond_sum, r)
        grad_condition = jax.vjp(jax.nn.silu, cond_wide)[1](cond_total)[0]

        n_qv = 2 * HL * HD
        return (
            block_output,
            grad_input,
            grad_condition,
            grad_w_ada,
            grad_b_ada,
            grad_qkv.reshape(RB, 3, HL, HP)[..., :HD].reshape(RB, 3, HL * HD),
            biases[:n_qv].reshape(2, HL * HD),
            grad_out.reshape(RB, HL, HP)[..., :HD].reshape(RB, HL * HD).T,
            biases[n_qv : n_qv + CB],
            grad_up,
            biases[n_qv + 2 * CB :],
            grad_down.T,
            biases[n_qv + CB : n_qv + 2 * CB],
            grad_w_gates[:, :HL],
            grad_b_gates[:HL],
            grad_w_gates[:, HL:],
            grad_b_gates[HL:],
        )

    return body


def solution(mesh):
    return jax.shard_map(
        make_body(mesh.shape["tok"], mesh.shape["tp"]),
        mesh=mesh,
        in_specs=(
            P("tok", "tp", None),
            P("tok", None),
            P("tok"),
            P("tok", "tp"),
            P("tok", "tp"),
            P("tok", None, "tp"),
            P(None, "tp"),
            P("tok", None, "tp"),
            P(None, "tp"),
            P("tp", "tok"),
            P("tp"),
            P("tok", "tp"),
            P("tp"),
            P("tp", "tok"),
            P("tp"),
            P("tok", "tp"),
            P("tp"),
            P("tok", "tp"),
            P("tp"),
            P("tok", "tp", None),
        ),
        out_specs=(
            P("tok", "tp", None),
            P("tok", "tp", None),
            P("tok", None),
            P("tok", None, "tp"),
            P(None, "tp"),
            P("tok", None, "tp"),
            P(None, "tp"),
            P("tp", "tok"),
            P("tp"),
            P("tok", "tp"),
            P("tp"),
            P("tp", "tok"),
            P("tp"),
            P("tok", "tp"),
            P("tp"),
            P("tok", "tp"),
            P("tp"),
        ),
        check_vma=False,
    )
```

```python
import functools
import math

import jax
import jax.numpy as jnp
from jax import lax
from jax.experimental import pallas as pl
from jax.experimental.pallas import tpu as pltpu
from jax.sharding import PartitionSpec as P

D = 1152
HD = 72
HP = 80
FF = 4608
FREQ = 256
GROUPS = 16
GW = FF // GROUPS
LEN = 1024
EPS = 1e-06
SCALE = HD**-0.5
SCALE2 = SCALE / math.log(2.0)

f32 = jnp.float32
bf16 = jnp.bfloat16
exact_mode = lax.Precision.HIGHEST


def dot(a, b, ca, cb):
    return lax.dot_general(a, b, (((ca,), (cb,)), ((), ())), preferred_element_type=f32)


def embed_time(timesteps):
    half_width = FREQ // 2
    indices = jnp.arange(half_width, dtype=f32)
    freq_rates = jnp.exp(-math.log(10000.0) * indices / half_width)
    angles = timesteps.astype(f32)[:, None] * freq_rates[None, :]
    return jnp.concatenate([jnp.cos(angles), jnp.sin(angles)], axis=1)


def attn_fwd_kernel(gate_ref, q_ref, k_ref, v_ref, mixed_ref, concat_ref, lse_ref):
    gate = gate_ref[pl.program_id(0)]
    keys = k_ref[0].T
    s = jnp.dot(keys, q_ref[0], preferred_element_type=f32)
    top = jnp.max(s, axis=0, keepdims=True)
    p = jnp.exp2((s - top) * SCALE2).astype(bf16)
    out = jnp.dot(v_ref[0], p, preferred_element_type=f32)
    total = out[HD : HD + 1]
    mixed = out * (1.0 / total)
    mixed_ref[0] = mixed
    concat_ref[0] = (mixed * gate).astype(bf16)
    lse_ref[0] = top * SCALE2 + jnp.log2(total)


def attn_fwd(gate, qkv):
    heads = gate.shape[0]
    spec = pl.BlockSpec((1, HP, LEN), lambda i: (i, 0, 0))
    row = pl.BlockSpec((1, 1, LEN), lambda i: (i, 0, 0))
    return pl.pallas_call(
        attn_fwd_kernel,
        grid=(heads,),
        in_specs=[pl.BlockSpec(memory_space=pltpu.SMEM)]
        + [pl.BlockSpec((1, HP, LEN), lambda i, k=k: (i + k * heads, 0, 0)) for k in range(3)],
        out_specs=[spec, spec, row],
        out_shape=[
            jax.ShapeDtypeStruct((heads, HP, LEN), f32),
            jax.ShapeDtypeStruct((heads, HP, LEN), bf16),
            jax.ShapeDtypeStruct((heads, 1, LEN), f32),
        ],
        compiler_params=pltpu.CompilerParams(vmem_limit_bytes=48 * 2**20),
        cost_estimate=pl.CostEstimate(
            flops=heads * 4 * LEN * LEN * 256,
            bytes_accessed=heads * HP * LEN * 14,
            transcendentals=heads * LEN * LEN,
        ),
        name="attn_fwd",
    )(gate, qkv, qkv, qkv)


def attn_bwd_kernel(
    chunk, gate_ref, q_ref, k_ref, v_ref, gc_ref, mixed_ref, lse_ref, dq_ref, dk_ref, dv_ref, hg_ref
):
    gate = gate_ref[pl.program_id(0)]
    keys_t = k_ref[0]
    keys = keys_t.T
    values = v_ref[0].T
    gc = gc_ref[0]
    inner = jnp.sum(mixed_ref[0] * gc, axis=0, keepdims=True)
    hg_ref[0] = inner
    delta = gate * inner
    grad = (gate * gc).astype(bf16)
    dv = jnp.zeros((LEN, HP), f32)
    dk = jnp.zeros((LEN, HP), f32)
    for j in range(LEN // chunk):
        part = slice(j * chunk, (j + 1) * chunk)
        q = q_ref[0, :, part]
        do = grad[:, part]
        s = jnp.dot(keys, q, preferred_element_type=f32)
        p = jnp.exp2(s * SCALE2 - lse_ref[0, :, part])
        dp = jnp.dot(values, do, preferred_element_type=f32)
        ds = (p * (dp - delta[:, part])).astype(bf16)
        dv = dv + jnp.dot(p.astype(bf16), do.T, preferred_element_type=f32)
        dk = dk + jnp.dot(ds, q.T, preferred_element_type=f32)
        dq = jnp.dot(keys_t, ds, preferred_element_type=f32)
        dq_ref[0, :, part] = (dq * SCALE).astype(bf16)
    dk_ref[0] = (dk * SCALE).T.astype(bf16)
    dv_ref[0] = dv.T.astype(bf16)


def attn_bwd(gate, qkv, gc, mixed, lse):
    heads = gate.shape[0]
    spec = pl.BlockSpec((1, HP, LEN), lambda i: (i, 0, 0))
    row = pl.BlockSpec((1, 1, LEN), lambda i: (i, 0, 0))
    grads = jax.ShapeDtypeStruct((heads, HP, LEN), bf16)
    return pl.pallas_call(
        functools.partial(attn_bwd_kernel, 256),
        grid=(heads,),
        in_specs=[pl.BlockSpec(memory_space=pltpu.SMEM)]
        + [pl.BlockSpec((1, HP, LEN), lambda i, k=k: (i + k * heads, 0, 0)) for k in range(3)]
        + [spec, spec, row],
        out_specs=[spec, spec, spec, row],
        out_shape=[grads, grads, grads, jax.ShapeDtypeStruct((heads, 1, LEN), f32)],
        compiler_params=pltpu.CompilerParams(vmem_limit_bytes=48 * 2**20),
        cost_estimate=pl.CostEstimate(
            flops=heads * 10 * LEN * LEN * 256,
            bytes_accessed=heads * HP * LEN * 20,
            transcendentals=heads * LEN * LEN,
        ),
        name="attn_bwd",
    )(gate, qkv, qkv, qkv, gc, mixed, lse)


MESH = pl.DeviceIdType.MESH
ML = 384


def xor(v, k):
    out, bit = 0, 1
    while bit <= k or bit <= 8:
        b = (v // bit) % 2
        out = out + bit * (1 - b if k & bit else b)
        bit *= 2
    return out


class Ring:
    def __init__(self, NT):
        self.NT, self.tall = NT, NT // 2

    def place(self, t):
        b = t % 2
        return (1 - b) * (self.tall - 1 - t // 2) + b * (self.tall + t // 2)

    def tok(self, q):
        q = (q + 2 * self.NT) % self.NT
        b = q // self.tall
        return (1 - b) * 2 * (self.tall - 1 - q) + b * (2 * (q - self.tall) + 1)


def copy_to(src, dst, send, recv, device):
    return pltpu.make_async_remote_copy(
        src_ref=src, dst_ref=dst, send_sem=send, recv_sem=recv, device_id=device, device_id_type=MESH
    )


def greet(t, p, NT, NP):
    barrier = pltpu.get_barrier_semaphore()
    for r in range(1, NP):
        pl.semaphore_signal(barrier, inc=1, device_id=(t, xor(p, r)), device_id_type=MESH)
    for k in range(1, NT):
        pl.semaphore_signal(barrier, inc=1, device_id=((t + k) % NT, p), device_id_type=MESH)
    pl.semaphore_wait(barrier, NP - 1 + NT - 1)


def start_kernel(
    NT, NP, x_ref, w_ref, msg_ref, ada_ref, gates_ref, bias_ref, mask_ref,
    rows_ref, full_ref, mods_ref, sig_ref, cond_ref,
    part_ref, got_ref, x_send, x_recv, c_send, c_recv, r_send, r_recv, s_send, s_recv, local_sem,
):
    NX, SUB = NP // 2, NT // NP
    I, _, length = x_ref.shape
    T = length // NX
    WN = w_ref.shape[1]
    half = WN // 256 * 128
    t, p = lax.axis_index("tok"), lax.axis_index("tp")
    xi = p // 2
    core = (t, xor(p, 1))
    ring = Ring(NT)
    q = ring.place(t)
    right, left = (ring.tok(q + 1), p), (ring.tok(q - 1), p)

    def where(tt):
        out = 0
        for r in range(NP):
            out = out + jnp.where(p == r, xor(tt // SUB, r), 0)
        return out * SUB + tt % SUB

    greet(t, p, NT, NP)

    small = []
    for k in range(1, NT):
        peer = (t + k) % NT
        small.append(copy_to(msg_ref.at[peer], cond_ref.at[k], s_send.at[0, k], s_recv.at[0, k], (peer, p)))
        small[-1].start()

    def hop(d, to_right):
        side = 0 if to_right else 1
        block = where(ring.tok(q - (d - 1) if to_right else q + (d - 1)))
        src = w_ref if d == 1 else full_ref.at[block]
        dst = full_ref.at[block]
        if d == NT // 2:
            cols = pl.ds(0, half) if to_right else pl.ds(half, WN - half)
            src, dst = src.at[:, cols], dst.at[:, cols]
        return copy_to(src, dst, r_send.at[side, d], r_recv.at[side, d], right if to_right else left)

    hops = {}

    def start_hop(d):
        for to_right in (True, False):
            hops[d, to_right] = hop(d, to_right)
            hops[d, to_right].start()

    def land_hop(d):
        for to_right in (True, False):
            hops[d, to_right].wait_recv()

    sent = {}

    def start_image(i):
        for k in range(1, NX):
            peer = xor(xi, k)
            for j in range(NX):
                at = pl.ds(pl.multiple_of(xor(peer, j) * T, T), T)
                cp = copy_to(
                    x_ref.at[i, :, pl.ds(j * T, T)], rows_ref.at[i, 2 * k, :, at],
                    x_send.at[i, k, j], x_recv.at[i, k, j], (t, xor(p, 2 * k)),
                )
                sent[i, k, j] = cp
                cp.start()

    locals_, own = [], []
    start_image(0)
    start_hop(1)
    for i in range(1, I):
        start_image(i)
    for i in range(I):
        for j in range(NX):
            at = pl.ds(pl.multiple_of(xor(xi, j) * T, T), T)
            src = x_ref.at[i, :, pl.ds(j * T, T)]
            cp = pltpu.make_async_copy(src, rows_ref.at[i, 0, :, at], local_sem.at[i, j])
            cp.start()
            locals_.append(cp)
            cp = copy_to(src, rows_ref.at[i, 1, :, at], c_send.at[i, 0, j], c_recv.at[i, 0, j], core)
            cp.start()
            own.append(cp)
    cp = pltpu.make_async_copy(w_ref, full_ref.at[where(t)], local_sem.at[I, 0])
    cp.start()
    locals_.append(cp)

    cond_ref[0] = msg_ref[t]
    for cp in small:
        cp.wait_recv()
    rb, fr = ada_ref.shape[1], gates_ref.shape[0]
    feats = cond_ref[...].reshape(NT * 8, -1).astype(bf16)
    for k in range(6):
        part = jnp.dot(feats[:, :rb], ada_ref[k], preferred_element_type=f32)
        part_ref[:, :, k * ML : (k + 1) * ML] = part.reshape(NT, 8, ML)
    part = jnp.dot(feats[:, 256 : 256 + fr], gates_ref[...], preferred_element_type=f32)
    part_ref[:, :, 6 * ML :] = part.reshape(NT, 8, 128)
    for k in range(1, NT):
        peer = (t + NT - k) % NT
        cp = copy_to(part_ref.at[k], got_ref.at[k], s_send.at[1, k], s_recv.at[1, k], (peer, p))
        cp.start()
        small.append(cp)
    land_hop(1)
    start_hop(2)
    for cp in small[NT - 1 :]:
        cp.wait_recv()
    total = part_ref[0]
    for k in range(1, NT):
        total = total + got_ref[k]
    total = total + bias_ref[...]
    sig = 1.0 / (1.0 + jnp.exp(-total[:, 6 * ML :]))
    sig_ref[...] = sig
    mods_ref[0, :, : 6 * ML] = total[:, : 6 * ML]
    mods_ref[0, :, 6 * ML :] = sig * mask_ref[...]
    mods = []
    for r in range(1, NP):
        cp = copy_to(mods_ref.at[0], mods_ref.at[r], s_send.at[2, r], s_recv.at[2, r], (t, xor(p, r)))
        cp.start()
        mods.append(cp)

    passed = []

    def land_image(i):
        for k in range(1, NX):
            for j in range(NX):
                sent[i, k, j].wait_recv()
            cp = copy_to(
                rows_ref.at[i, 2 * k], rows_ref.at[i, 2 * k + 1],
                c_send.at[i, k, 0], c_recv.at[i, k, 0], core,
            )
            cp.start()
            passed.append(cp)

    ring_left = list(range(2, NT // 2 + 1))
    images_left = list(range(I))
    while ring_left or images_left:
        if images_left:
            land_image(images_left.pop(0))
        if ring_left:
            d = ring_left.pop(0)
            land_hop(d)
            if d < NT // 2:
                start_hop(d + 1)
    for cp in own + passed + mods:
        cp.wait_recv()
    for cp in locals_:
        cp.wait()
    for cp in small + mods + own + passed + list(sent.values()) + list(hops.values()):
        cp.wait_send()


def start_call(NT, NP, x, w, msg, ada, gates, bias, mask):
    I, CB, length = x.shape
    NX = NP // 2
    RB, WN = w.shape
    wide = 6 * ML + 128
    hbm, vmem = pl.BlockSpec(memory_space=pl.ANY), pl.BlockSpec(memory_space=pltpu.VMEM)
    dma = pltpu.SemaphoreType.DMA
    return pl.pallas_call(
        functools.partial(start_kernel, NT, NP),
        in_specs=[hbm, hbm] + [vmem] * 5,
        out_specs=[hbm, hbm, vmem, vmem, vmem],
        out_shape=[
            jax.ShapeDtypeStruct((I, NP, CB, length), bf16),
            jax.ShapeDtypeStruct((NT, RB, WN), bf16),
            jax.ShapeDtypeStruct((NP, 8, wide), f32),
            jax.ShapeDtypeStruct((8, 128), f32),
            jax.ShapeDtypeStruct((NT, 8, ML), f32),
        ],
        scratch_shapes=[
            pltpu.VMEM((NT, 8, wide), f32),
            pltpu.VMEM((NT, 8, wide), f32),
            dma((I, NX, NX)),
            dma((I, NX, NX)),
            dma((I, NX, NX)),
            dma((I, NX, NX)),
            dma((2, NT // 2 + 1)),
            dma((2, NT // 2 + 1)),
            dma((3, max(NT, NP))),
            dma((3, max(NT, NP))),
            dma((I + 1, NX)),
        ],
        compiler_params=pltpu.CompilerParams(
            collective_id=0, has_side_effects=True, vmem_limit_bytes=32 * 2**20
        ),
        name="start",
    )(x, w, msg, ada, gates, bias, mask)


def tail_kernel(
    NT, NP, g_ref, last_ref, ada_ref,
    out_ref, lasts_ref, cond_ref,
    part_ref, sum_ref, send_ref, recv_ref, r_send, r_recv, s_send, s_recv,
):
    SUB = NT // NP
    t, p = lax.axis_index("tok"), lax.axis_index("tp")
    ring = Ring(NT)
    q = ring.place(t)
    right, left = (ring.tok(q + 1), p), (ring.tok(q - 1), p)
    WN = g_ref.shape[2]
    half = (WN // 2 + 127) // 128 * 128
    cols = (slice(0, half), slice(half, WN))

    def where(tt):
        out = 0
        for r in range(NP):
            out = out + jnp.where(p == r, xor(tt // SUB, r), 0)
        return out * SUB + tt % SUB

    greet(t, p, NT, NP)
    lasts = []
    for k in range(1, NT):
        peer = (t + k) % NT
        cp = copy_to(last_ref, lasts_ref.at[k], s_send.at[0, k], s_recv.at[0, k], (peer, p))
        cp.start()
        lasts.append(cp)
    lasts_ref[0] = last_ref[...]

    chains = []
    for side in range(2):
        for s in range(2):
            chains.append((side, s, NT // 2 if side == s else NT // 2 - 1))
    flying = {}

    def step(h):
        for n, (side, s, count) in enumerate(chains):
            if h >= count:
                continue
            d = count - h
            block = where(ring.tok(q + d if side == 0 else q - d))
            width = cols[s].stop - cols[s].start
            v = g_ref[block, :, cols[s]]
            if h:
                flying[n, h - 1].wait_recv()
                v = v + recv_ref[n, h - 1, :, :width].astype(f32)
            send_ref[n, h, :, :width] = v.astype(bf16)
            cp = copy_to(
                send_ref.at[n, h], recv_ref.at[n, h], r_send.at[n, h], r_recv.at[n, h],
                right if side == 0 else left,
            )
            cp.start()
            flying[n, h] = cp

    step(0)
    for cp in lasts:
        cp.wait_recv()
    grads = lasts_ref[...].reshape(NT * 8, -1)
    total = 0.0
    for k in range(6):
        g = grads[:, k * ML : (k + 1) * ML]
        high = g.astype(bf16)
        low = (g - high.astype(f32)).astype(bf16)
        w = ada_ref[k]
        total = total + dot(high, w, 1, 1) + dot(low, w, 1, 1)
    part_ref[:, :, : total.shape[1]] = total.reshape(NT, 8, -1)
    parts = []
    for k in range(1, NT):
        peer = (t + NT - k) % NT
        cp = copy_to(part_ref.at[k], sum_ref.at[0, t], s_send.at[1, k], s_recv.at[1, k], (peer, p))
        cp.start()
        parts.append(cp)
    sum_ref[0, t] = part_ref[0]
    step(1)
    for cp in parts:
        cp.wait_recv()
    sums = []
    for r in range(1, NP):
        cp = copy_to(sum_ref.at[0], sum_ref.at[r], s_send.at[2, r], s_recv.at[2, r], (t, xor(p, r)))
        cp.start()
        sums.append(cp)
    for h in range(2, NT // 2):
        step(h)
    for cp in sums:
        cp.wait_recv()
    total = sum_ref[0]
    for r in range(1, NP):
        total = total + sum_ref[r]
    cond_ref[...] = total
    mine = where(t)
    for s in range(2):
        v = g_ref[mine, :, cols[s]]
        for n, (side, ss, count) in enumerate(chains):
            if ss == s:
                flying[n, count - 1].wait_recv()
                v = v + recv_ref[n, count - 1, :, : cols[s].stop - cols[s].start].astype(f32)
        out_ref[:, cols[s]] = v
    for cp in lasts + parts + sums + list(flying.values()):
        cp.wait_send()


def tail_call(NT, NP, g, last, ada):
    _, RB, WN = g.shape
    half = (WN // 2 + 127) // 128 * 128
    vmem = pl.BlockSpec(memory_space=pltpu.VMEM)
    dma = pltpu.SemaphoreType.DMA
    hops = NT // 2
    return pl.pallas_call(
        functools.partial(tail_kernel, NT, NP),
        in_specs=[vmem] * 3,
        out_specs=[vmem] * 3,
        out_shape=[
            jax.ShapeDtypeStruct((RB, WN), f32),
            jax.ShapeDtypeStruct((NT,) + last.shape, f32),
            jax.ShapeDtypeStruct((NT, 8, 256), f32),
        ],
        scratch_shapes=[
            pltpu.VMEM((NT, 8, 256), f32),
            pltpu.VMEM((NP, NT, 8, 256), f32),
            pltpu.VMEM((4, hops, RB, half), bf16),
            pltpu.VMEM((4, hops, RB, half), bf16),
            dma((4, hops)),
            dma((4, hops)),
            dma((3, max(NT, NP))),
            dma((3, max(NT, NP))),
        ],
        compiler_params=pltpu.CompilerParams(
            collective_id=1, has_side_effects=True, vmem_limit_bytes=40 * 2**20
        ),
        name="tail",
    )(g, last, ada)


def make_body(NT, NP):
    NX = NP // 2
    SUB = NT // NP
    RB = D // NT
    CB = D // NP
    T = LEN // NX
    table = Ring(NT)
    cycle = [table.tok(q) for q in range(NT)]
    right_pairs = [(cycle[i], cycle[(i + 1) % NT]) for i in range(NT)]
    left_pairs = [(b, a) for a, b in right_pairs]
    n_right = NT // 2
    n_left = NT - 1 - n_right

    def hop(v, right):
        return lax.ppermute(v, "tok", right_pairs if right else left_pairs)

    def tp_xor(v, r):
        return lax.ppermute(v, "tp", [(p, p ^ r) for p in range(NP)])

    def swap_tokens(v, k, axis):
        if k == 0:
            return v
        parts = [lax.slice_in_dim(v, (j ^ k) * T, (j ^ k) * T + T, axis=axis) for j in range(NX)]
        return jnp.concatenate(parts, axis=axis)

    def body(
        block_input,
        condition,
        timesteps,
        head_mask,
        group_mask,
        w_ada,
        b_ada,
        w_qkv,
        b_qv,
        w_out,
        b_out,
        w_up,
        b_up,
        w_down,
        b_down,
        w_head,
        b_head,
        w_group,
        b_group,
        cotangent,
    ):
        I = condition.shape[0]
        HL = head_mask.shape[1]
        GL = group_mask.shape[1]
        FL = w_up.shape[1]
        FR = FREQ // NT
        t = lax.axis_index("tok")
        p = lax.axis_index("tp")
        xi = p // 2
        my_place = table.place(t)

        def block_of(d):
            tt = table.tok(my_place + d)
            return jnp.bitwise_xor(tt // SUB, p) * SUB + tt % SUB

        def gather_rows(shard):
            pieces = [(0, shard)]
            v = shard
            for d in range(1, n_right + 1):
                v = hop(v, True)
                pieces.append((-d, v))
            v = shard
            for d in range(1, n_left + 1):
                v = hop(v, False)
                pieces.append((d, v))
            full = jnp.zeros((2, NT) + shard.shape[1:], shard.dtype)
            for d, v in pieces:
                full = lax.dynamic_update_slice(full, v[:, None], (0, block_of(d), 0, 0))
            return full.reshape(2, D, -1)

        def scatter_rows(full):
            blocks = full.reshape(NT, RB, -1)

            def own(d):
                return lax.dynamic_index_in_dim(blocks, block_of(d), 0, keepdims=False)

            total = own(0)
            for count, right in ((n_right, True), (n_left, False)):
                v = None
                for d in range(count, 0, -1):
                    term = own(d if right else -d)
                    v = hop((term if v is None else term + v.astype(f32)).astype(bf16), right)
                total = total + v.astype(f32)
            return total

        def own_order(v, axis):
            parts = [
                lax.dynamic_slice_in_dim(v, jnp.bitwise_xor(j, xi) * T, T, axis=axis)
                for j in range(NX)
            ]
            return jnp.concatenate(parts, axis=axis)

        qkv_shard = jnp.pad(
            w_qkv.reshape(RB, 3, HL, HD), ((0, 0), (0, 0), (0, 0), (0, HP - HD))
        ).reshape(RB, 3 * HL * HP)
        out_shard = jnp.pad(w_out.T.reshape(RB, HL, HD), ((0, 0), (0, 0), (0, HP - HD))).reshape(
            RB, HL * HP
        )
        time_feat = embed_time(timesteps).astype(bf16)
        cond_wide = condition.astype(f32)
        cond_act = jax.nn.silu(cond_wide).astype(bf16)
        pad8 = lambda v, width: jnp.pad(v, ((0, 8 - v.shape[0]), (0, width - v.shape[1])))
        message = jnp.concatenate(
            [
                jnp.pad(cond_act.reshape(I, NT, RB), ((0, 0), (0, 0), (0, 256 - RB))),
                jnp.pad(time_feat.reshape(I, NT, FR), ((0, 0), (0, 0), (0, ML - 256 - FR))),
            ],
            axis=2,
        )
        message = jnp.pad(message.transpose(1, 0, 2).astype(f32), ((0, 0), (0, 8 - I), (0, 0)))
        ada = jnp.pad(w_ada.transpose(1, 0, 2), ((0, 0), (0, 0), (0, ML - CB)))
        gates = jnp.concatenate([w_head, w_group], axis=1)
        gates = jnp.pad(gates, ((0, 0), (0, 128 - HL - GL)))
        wide = 6 * ML + 128
        mod_bias = jnp.concatenate(
            [jnp.pad(b_ada, ((0, 0), (0, ML - CB))).reshape(6 * ML), b_head, b_group]
        ).astype(f32)
        bias = jnp.concatenate(
            [
                jnp.broadcast_to(pad8(mod_bias[None], wide)[:1], (I, wide)),
                pad8(jnp.concatenate([jnp.pad(b_out, (0, ML - CB)), b_down]).astype(f32)[None], wide)[:1],
                pad8(b_up.astype(f32)[None], wide)[: 8 - I - 1],
            ],
            axis=0,
        )
        mask = pad8(jnp.concatenate([head_mask, group_mask], axis=1).astype(f32), 128)
        rows_all, early_full, mods, sig, cond_all = start_call(
            NT,
            NP,
            block_input,
            jnp.concatenate([qkv_shard, out_shard], axis=1),
            message,
            ada,
            gates,
            bias,
            mask,
        )
        rows_full = [rows_all[i].reshape(D, LEN) for i in range(I)]
        early_full = early_full.reshape(D, -1)
        qkv_full, out_full = early_full[:, : 3 * HL * HP], early_full[:, 3 * HL * HP :]
        head_sig, group_sig = sig[:I, :HL], sig[:I, HL : HL + GL]
        head_gate = mods[0, :I, 6 * ML : 6 * ML + HL]
        vectors = mods[:, :I, : 6 * ML].reshape(NP, I * 6, ML)[:, :, :CB]
        biases_two = mods[:, I, : 2 * ML].reshape(NP, 2, ML)[:, :, :CB]
        columns = jnp.concatenate([vectors, biases_two], axis=1).transpose(0, 2, 1).reshape(D, -1)

        def mod(i, k):
            return lax.slice_in_dim(columns, i * 6 + k, i * 6 + k + 1, axis=1)

        out_bias = columns[:, I * 6 : I * 6 + 1]
        down_bias = columns[:, I * 6 + 1 : I * 6 + 2]
        gates_x = jnp.concatenate(
            [mods[2 * k, :I, 6 * ML + HL : 6 * ML + HL + GL] for k in range(NX)], axis=1
        )
        gate_cols = jnp.repeat(gates_x, GW, axis=1).T
        up_bias = jnp.concatenate([mods[2 * k, I + 1, :FL] for k in range(NX)])[:, None]

        cot_in = own_order(cotangent, 2)
        cot_blocks = []
        for k in range(NX):
            v = cot_in[:, :, k * T : (k + 1) * T]
            v = v if k == 0 else tp_xor(v, 2 * k)
            cot_blocks.append(v)
        cot_half = jnp.stack(cot_blocks, axis=1)
        cot_full = jnp.stack([cot_half, tp_xor(cot_half, 1)], axis=2).reshape(I, D, T)

        late_shard = jnp.stack([w_up, w_down.T])
        late_parts = [late_shard] + [tp_xor(late_shard, 2 * k) for k in range(1, NX)]
        late_parts = [gather_rows(v) for v in late_parts]
        up_full = jnp.concatenate([v[0] for v in late_parts], axis=1)
        down_full = jnp.concatenate([v[1] for v in late_parts], axis=1)
        qv = b_qv.astype(f32).reshape(2, HL, HD)
        qv_bias = jnp.stack(
            [
                jnp.pad(qv[0], ((0, 0), (0, HP - HD))),
                jnp.zeros((HL, HP), f32),
                jnp.concatenate(
                    [qv[1], jnp.ones((HL, 1), f32), jnp.zeros((HL, HP - HD - 1), f32)], axis=1
                ),
            ]
        ).reshape(3 * HL * HP, 1)

        def stats(v):
            centre = jnp.sum(v, axis=0, keepdims=True) * (1.0 / D)
            square = jnp.sum(v * v, axis=0, keepdims=True) * (1.0 / D)
            return centre, lax.rsqrt(square - centre * centre + EPS)

        fwd = []
        for i in range(I):
            wide_rows = rows_full[i].astype(f32)
            centre, inverse = stats(wide_rows)
            attn_in = ((wide_rows - centre) * inverse * (1.0 + mod(i, 1)) + mod(i, 0)).astype(bf16)
            qkv = (dot(qkv_full, attn_in, 0, 0) + qv_bias).astype(bf16).reshape(3 * HL, HP, LEN)
            mixed, concat, lse = attn_fwd(head_gate[i], qkv)
            concat = concat.reshape(HL * HP, LEN)
            part = dot(out_full, concat, 1, 0).reshape(NX, 2, CB, LEN)
            got = tp_xor(part[:, 1].astype(bf16), 1)
            both = part[:, 0] + got.astype(f32)
            total = both[:, :, :T]
            for k in range(1, NX):
                got = tp_xor(both[:, :, k * T : (k + 1) * T].astype(bf16), 2 * k).astype(f32)
                total = total + jnp.stack([got[j ^ k] for j in range(NX)])
            total_other = tp_xor(total, 1)
            branch_one = jnp.stack([total, total_other], axis=1).reshape(D, T) + out_bias
            fwd.append((centre, inverse, attn_in, qkv, mixed, concat, lse, branch_one))

        mids = []
        for i in range(I):
            branch_one = fwd[i][-1]
            cot = cot_full[i].astype(f32)
            mid_rows = rows_full[i][:, :T].astype(f32) + mod(i, 2) * branch_one
            centre, inverse = stats(mid_rows)
            normed = (mid_rows - centre) * inverse
            mlp_in = (normed * (1.0 + mod(i, 4)) + mod(i, 3)).astype(bf16)
            grad_two = (mod(i, 5) * cot).astype(bf16)
            pre = dot(up_full, mlp_in, 0, 0) + up_bias
            grad_hid = dot(down_full, grad_two, 0, 0)
            gate = gate_cols[:, i : i + 1]
            inner = jnp.tanh(math.sqrt(2.0 / math.pi) * (pre + 0.044715 * pre * pre * pre))
            act = 0.5 * pre * (1.0 + inner)
            slope = 0.5 * (1.0 + inner) + 0.5 * pre * (1.0 - inner * inner) * math.sqrt(
                2.0 / math.pi
            ) * (1.0 + 3.0 * 0.044715 * pre * pre)
            hidden = (act * gate).astype(bf16)
            grad_pre = (slope * gate * grad_hid).astype(bf16)
            gate_sums = jnp.sum(jnp.sum(grad_hid * act, axis=1).reshape(NX * GL, GW), axis=1)
            up_sums = jnp.sum(grad_pre.astype(f32), axis=1)
            gpart = dot(up_full, grad_pre, 1, 0)
            got = tp_xor(gpart.astype(bf16), 1).reshape(NX, 2, CB, T)
            got = jnp.stack([got[:, 1], got[:, 0]], axis=1).reshape(D, T)
            gnorm = gpart + got.astype(f32)
            shift_sums = jnp.sum(gnorm, axis=1)
            scale_sums = jnp.sum(gnorm * normed, axis=1)
            g = gnorm * (1.0 + mod(i, 4))
            mean_g = jnp.sum(g, axis=0, keepdims=True) * (1.0 / D)
            mean_gn = jnp.sum(g * normed, axis=0, keepdims=True) * (1.0 / D)
            grad_mid = cot + inverse * (g - mean_g - normed * mean_gn)
            gate_one_sums = jnp.sum(grad_mid * branch_one, axis=1)
            grad_one = (mod(i, 2) * grad_mid).astype(bf16)
            out_sums = jnp.sum(grad_one.astype(f32), axis=1)
            own_half = grad_one.reshape(NX, 2, CB, T)[:, 0]
            tok_blocks = [grad_one]
            for k in range(1, NX):
                got = tp_xor(own_half, 2 * k)
                got = jnp.stack([got[j ^ k] for j in range(NX)])
                tok_blocks.append(jnp.stack([got, tp_xor(got, 1)], axis=1).reshape(D, T))
            grad_one_full = jnp.concatenate(tok_blocks, axis=1)
            mid_blocks = [grad_mid[:CB]]
            for k in range(1, NX):
                mid_blocks.append(
                    tp_xor(grad_mid[2 * k * CB : (2 * k + 1) * CB].astype(bf16), 2 * k).astype(f32)
                )
            grad_mid_own = jnp.concatenate(mid_blocks, axis=1)
            bpart = dot(down_full, hidden, 1, 0).reshape(NX, 2, CB, T)
            branch_two = (
                bpart[:, 0]
                + tp_xor(bpart[:, 1].astype(bf16), 1).astype(f32)
                + down_bias.reshape(NX, 2, CB, 1)[:, 0]
            )
            half = lambda v: v.reshape(NX, 2, CB, -1)[:, 0]
            gate_two_sums = jnp.sum(half(cot) * branch_two, axis=2)
            out_half = (half(mid_rows) + half(mod(i, 5)) * branch_two).astype(bf16)
            out_blocks = [out_half[0]] + [tp_xor(out_half[k], 2 * k) for k in range(1, NX)]
            out_own = jnp.concatenate(out_blocks, axis=1)
            down_sums = jnp.sum(grad_two.astype(f32), axis=1)
            mids.append(
                dict(
                    grad_two=grad_two,
                    hidden=hidden,
                    grad_pre=grad_pre,
                    mlp_in=mlp_in,
                    grad_one_full=grad_one_full,
                    grad_mid_own=grad_mid_own,
                    out_own=out_own,
                    sums=(gate_one_sums, shift_sums, scale_sums),
                    gate_two_sums=gate_two_sums,
                    gate_sums=gate_sums,
                    up_sums=up_sums,
                    out_sums=out_sums,
                    down_sums=down_sums,
                )
            )

        block_output = own_order(jnp.stack([m["out_own"] for m in mids]), 2)

        grad_down = sum(dot(m["grad_two"], m["hidden"], 1, 1) for m in mids)
        grad_up = sum(dot(m["mlp_in"], m["grad_pre"], 1, 1) for m in mids)
        late = scatter_rows(jnp.concatenate([grad_up, grad_down], axis=1))
        late = late.reshape(RB, 2, NX, FL)
        total = late[:, :, 0]
        for k in range(1, NX):
            total = total + tp_xor(late[:, :, k].astype(bf16), 2 * k).astype(f32)
        grad_up, grad_down = total[:, 0], total[:, 1]

        def x_message(k):
            parts = []
            for m in mids:
                for v in m["sums"]:
                    parts.append(v[2 * k * CB : (2 * k + 1) * CB])
                parts.append(m["gate_two_sums"][k])
                parts.append(m["gate_sums"][k * GL : (k + 1) * GL])
            for name, size in (("out_sums", 2 * k * CB), ("down_sums", 2 * k * CB)):
                parts.append(sum(m[name] for m in mids)[size : size + CB])
            parts.append(sum(m["up_sums"] for m in mids)[k * FL : (k + 1) * FL])
            return jnp.concatenate(parts)

        x_total = x_message(0)
        for k in range(1, NX):
            x_total = x_total + tp_xor(x_message(k), 2 * k)
        per = 4 * CB + GL
        per_image = x_total[: I * per].reshape(I, per)
        late_mods = per_image[:, : 4 * CB].reshape(I, 4, CB)
        grad_group_gate = per_image[:, 4 * CB :]
        bias_sums = x_total[I * per :]

        backs = []
        for i in range(I):
            centre, inverse, attn_in, qkv, mixed, concat, lse, _ = fwd[i]
            m = mids[i]
            gc = dot(out_full, m["grad_one_full"], 0, 0).reshape(HL, HP, LEN)
            dq, dk, dv, inner = attn_bwd(head_gate[i], qkv, gc, mixed, lse)
            dqkv = jnp.concatenate([dq, dk, dv], axis=0).reshape(3 * HL * HP, LEN)
            part = dot(qkv_full, dqkv, 1, 0).reshape(NX, 2, CB, LEN)
            got = tp_xor(part[:, 1].astype(bf16), 1)
            both = part[:, 0] + got.astype(f32)
            gnorm = both[0]
            for k in range(1, NX):
                got = tp_xor(both[k].astype(bf16), 2 * k).astype(f32)
                gnorm = gnorm + swap_tokens(got, k, 1)
            normed = (rows_full[i][:CB].astype(f32) - centre) * inverse
            own_cols = columns[:CB]
            g = gnorm * (1.0 + own_cols[:, i * 6 + 1 : i * 6 + 2])
            sums = jnp.stack([jnp.sum(g, axis=0), jnp.sum(g * normed, axis=0)])
            total = sums
            for r in range(1, NP):
                total = total + swap_tokens(tp_xor(sums, r), r // 2, 1)
            grad_in = m["grad_mid_own"] + inverse * (
                g - total[0:1] * (1.0 / D) - normed * (total[1:2] * (1.0 / D))
            )
            backs.append(
                dict(
                    dqkv=dqkv,
                    grad_in=grad_in,
                    shift=jnp.sum(gnorm, axis=1),
                    scale=jnp.sum(gnorm * normed, axis=1),
                    heads=jnp.sum(inner, axis=(1, 2)),
                    q_sums=jnp.sum(dq.astype(f32), axis=2)[:, :HD].reshape(-1),
                    v_sums=jnp.sum(dv.astype(f32), axis=2)[:, :HD].reshape(-1),
                )
            )
        grad_input = own_order(jnp.stack([b["grad_in"] for b in backs]), 2)

        grad_out = sum(
            dot(m["grad_one_full"], f[5], 1, 1) for m, f in zip(mids, fwd)
        )
        grad_out = scatter_rows(grad_out)
        grad_qkv = sum(dot(f[2], b["dqkv"], 1, 1) for f, b in zip(fwd, backs))

        grad_mod = jnp.stack(
            [
                jnp.stack([b["shift"] for b in backs]),
                jnp.stack([b["scale"] for b in backs]),
                late_mods[:, 0],
                late_mods[:, 1],
                late_mods[:, 2],
                late_mods[:, 3],
            ],
            axis=1,
        )
        grad_head_gate = jnp.stack([b["heads"] for b in backs])
        head_logit = grad_head_gate * head_mask.astype(f32) * head_sig * (1.0 - head_sig)
        group_logit = grad_group_gate * group_mask.astype(f32) * group_sig * (1.0 - group_sig)
        image_rows = jnp.concatenate(
            [
                jnp.pad(grad_mod, ((0, 0), (0, 0), (0, ML - CB))).reshape(I, 6 * ML),
                head_logit,
                group_logit,
                jnp.zeros((I, 128 - HL - GL), f32),
            ],
            axis=1,
        )
        widen = lambda v: jnp.pad(v, (0, wide - v.shape[0]))[None]
        last = jnp.concatenate(
            [
                image_rows,
                widen(sum(b["q_sums"] for b in backs)),
                widen(sum(b["v_sums"] for b in backs)),
                widen(bias_sums[: 2 * CB]),
                widen(bias_sums[2 * CB :]),
                jnp.zeros((8 - I - 4, wide), f32),
            ],
            axis=0,
        )
        grad_qkv, lasts, cond_sum = tail_call(NT, NP, grad_qkv.reshape(NT, RB, -1), last, ada)
        mods_all = (
            lasts[:, :I, : 6 * ML].reshape(NT * I, 6, ML)[:, :, :CB].reshape(NT * I, 6 * CB)
        )
        logits_all = lasts[:, :I, 6 * ML : 6 * ML + HL + GL].reshape(NT * I, HL + GL)
        bias_rows = jnp.sum(lasts[:, I : I + 4], axis=0)
        cond_f = cond_all[:, :I, :RB].reshape(NT * I, RB)
        time_f = cond_all[:, :I, 256 : 256 + FR].reshape(NT * I, FR)
        grad_w_ada = lax.dot_general(
            cond_f, mods_all, (((0,), (0,)), ((), ())), precision=exact_mode
        ).reshape(RB, 6, CB)
        grad_b_ada = jnp.sum(mods_all, axis=0).reshape(6, CB)
        grad_w_gates = lax.dot_general(
            time_f, logits_all, (((0,), (0,)), ((), ())), precision=exact_mode
        )
        grad_b_gates = jnp.sum(logits_all, axis=0)
        cond_total = cond_sum[:, :I, :RB].transpose(1, 0, 2).reshape(I, D)
        grad_condition = jax.vjp(jax.nn.silu, cond_wide)[1](cond_total)[0]

        return (
            block_output,
            grad_input,
            grad_condition,
            grad_w_ada,
            grad_b_ada,
            grad_qkv.reshape(RB, 3, HL, HP)[..., :HD].reshape(RB, 3, HL * HD),
            bias_rows[:2, : HL * HD],
            grad_out.reshape(RB, HL, HP)[..., :HD].reshape(RB, HL * HD).T,
            bias_rows[2, :CB],
            grad_up,
            bias_rows[3, :FL],
            grad_down.T,
            bias_rows[2, CB : 2 * CB],
            grad_w_gates[:, :HL],
            grad_b_gates[:HL],
            grad_w_gates[:, HL:],
            grad_b_gates[HL:],
        )

    return body


def solution(mesh):
    return jax.shard_map(
        make_body(mesh.shape["tok"], mesh.shape["tp"]),
        mesh=mesh,
        in_specs=(
            P("tok", "tp", None),
            P("tok", None),
            P("tok"),
            P("tok", "tp"),
            P("tok", "tp"),
            P("tok", None, "tp"),
            P(None, "tp"),
            P("tok", None, "tp"),
            P(None, "tp"),
            P("tp", "tok"),
            P("tp"),
            P("tok", "tp"),
            P("tp"),
            P("tp", "tok"),
            P("tp"),
            P("tok", "tp"),
            P("tp"),
            P("tok", "tp"),
            P("tp"),
            P("tok", "tp", None),
        ),
        out_specs=(
            P("tok", "tp", None),
            P("tok", "tp", None),
            P("tok", None),
            P("tok", None, "tp"),
            P(None, "tp"),
            P("tok", None, "tp"),
            P(None, "tp"),
            P("tp", "tok"),
            P("tp"),
            P("tok", "tp"),
            P("tp"),
            P("tp", "tok"),
            P("tp"),
            P("tok", "tp"),
            P("tp"),
            P("tok", "tp"),
            P("tp"),
        ),
        check_vma=False,
    )
```

```python
import functools
import math

import jax
import jax.numpy as jnp
from jax import lax
from jax.experimental import pallas as pl
from jax.experimental.pallas import tpu as pltpu
from jax.sharding import PartitionSpec as P

D = 1152
HD = 72
HP = 80
FF = 4608
FREQ = 256
GROUPS = 16
GW = FF // GROUPS
LEN = 1024
EPS = 1e-06
SCALE = HD**-0.5
SCALE2 = SCALE / math.log(2.0)

f32 = jnp.float32
bf16 = jnp.bfloat16
exact_mode = lax.Precision.HIGHEST


def dot(a, b, ca, cb):
    return lax.dot_general(a, b, (((ca,), (cb,)), ((), ())), preferred_element_type=f32)


def embed_time(timesteps):
    half_width = FREQ // 2
    indices = jnp.arange(half_width, dtype=f32)
    freq_rates = jnp.exp(-math.log(10000.0) * indices / half_width)
    angles = timesteps.astype(f32)[:, None] * freq_rates[None, :]
    return jnp.concatenate([jnp.cos(angles), jnp.sin(angles)], axis=1)


MESH = pl.DeviceIdType.MESH
ML = 384


def xor(v, k):
    out, bit = 0, 1
    while bit <= k or bit <= 8:
        b = (v // bit) % 2
        out = out + bit * (1 - b if k & bit else b)
        bit *= 2
    return out


class Ring:
    def __init__(self, NT):
        self.NT, self.tall = NT, NT // 2

    def place(self, t):
        b = t % 2
        return (1 - b) * (self.tall - 1 - t // 2) + b * (self.tall + t // 2)

    def tok(self, q):
        q = (q + 2 * self.NT) % self.NT
        b = q // self.tall
        return (1 - b) * 2 * (self.tall - 1 - q) + b * (2 * (q - self.tall) + 1)


def copy_to(src, dst, send, recv, device):
    return pltpu.make_async_remote_copy(
        src_ref=src, dst_ref=dst, send_sem=send, recv_sem=recv, device_id=device, device_id_type=MESH
    )


def greet(t, p, NT, NP):
    barrier = pltpu.get_barrier_semaphore()
    for r in range(1, NP):
        pl.semaphore_signal(barrier, inc=1, device_id=(t, xor(p, r)), device_id_type=MESH)
    for k in range(1, NT):
        pl.semaphore_signal(barrier, inc=1, device_id=((t + k) % NT, p), device_id_type=MESH)
    pl.semaphore_wait(barrier, NP - 1 + NT - 1)


def start_kernel(
    NT, NP, x_ref, w_ref, msg_ref, ada_ref, gates_ref, bias_ref, mask_ref,
    rows_ref, full_ref, mods_ref, sig_ref, cond_ref,
    part_ref, got_ref, x_send, x_recv, c_send, c_recv, r_send, r_recv, s_send, s_recv, local_sem,
):
    NX, SUB = NP // 2, NT // NP
    I, _, length = x_ref.shape
    T = length // NX
    WN = w_ref.shape[1]
    half = WN // 256 * 128
    t, p = lax.axis_index("tok"), lax.axis_index("tp")
    xi = p // 2
    core = (t, xor(p, 1))
    ring = Ring(NT)
    q = ring.place(t)
    right, left = (ring.tok(q + 1), p), (ring.tok(q - 1), p)

    def where(tt):
        out = 0
        for r in range(NP):
            out = out + jnp.where(p == r, xor(tt // SUB, r), 0)
        return out * SUB + tt % SUB

    greet(t, p, NT, NP)

    small = []
    for k in range(1, NT):
        peer = (t + k) % NT
        small.append(copy_to(msg_ref.at[peer], cond_ref.at[k], s_send.at[0, k], s_recv.at[0, k], (peer, p)))
        small[-1].start()

    def hop(d, to_right):
        side = 0 if to_right else 1
        block = where(ring.tok(q - (d - 1) if to_right else q + (d - 1)))
        src = w_ref if d == 1 else full_ref.at[block]
        dst = full_ref.at[block]
        if d == NT // 2:
            cols = pl.ds(0, half) if to_right else pl.ds(half, WN - half)
            src, dst = src.at[:, cols], dst.at[:, cols]
        return copy_to(src, dst, r_send.at[side, d], r_recv.at[side, d], right if to_right else left)

    hops = {}

    def start_hop(d):
        for to_right in (True, False):
            hops[d, to_right] = hop(d, to_right)
            hops[d, to_right].start()

    def land_hop(d):
        for to_right in (True, False):
            hops[d, to_right].wait_recv()

    sent = {}

    def start_image(i):
        for k in range(1, NX):
            peer = xor(xi, k)
            for j in range(NX):
                at = pl.ds(pl.multiple_of(xor(peer, j) * T, T), T)
                cp = copy_to(
                    x_ref.at[i, :, pl.ds(j * T, T)], rows_ref.at[i, 2 * k, :, at],
                    x_send.at[i, k, j], x_recv.at[i, k, j], (t, xor(p, 2 * k)),
                )
                sent[i, k, j] = cp
                cp.start()

    locals_, own = [], []
    start_image(0)
    start_hop(1)
    for i in range(1, I):
        start_image(i)
    for i in range(I):
        for j in range(NX):
            at = pl.ds(pl.multiple_of(xor(xi, j) * T, T), T)
            src = x_ref.at[i, :, pl.ds(j * T, T)]
            cp = pltpu.make_async_copy(src, rows_ref.at[i, 0, :, at], local_sem.at[i, j])
            cp.start()
            locals_.append(cp)
            cp = copy_to(src, rows_ref.at[i, 1, :, at], c_send.at[i, 0, j], c_recv.at[i, 0, j], core)
            cp.start()
            own.append(cp)
    cp = pltpu.make_async_copy(w_ref, full_ref.at[where(t)], local_sem.at[I, 0])
    cp.start()
    locals_.append(cp)

    cond_ref[0] = msg_ref[t]
    for cp in small:
        cp.wait_recv()
    rb, fr = ada_ref.shape[1], gates_ref.shape[0]
    feats = cond_ref[...].reshape(NT * 8, -1).astype(bf16)
    for k in range(6):
        part = jnp.dot(feats[:, :rb], ada_ref[k], preferred_element_type=f32)
        part_ref[:, :, k * ML : (k + 1) * ML] = part.reshape(NT, 8, ML)
    part = jnp.dot(feats[:, 256 : 256 + fr], gates_ref[...], preferred_element_type=f32)
    part_ref[:, :, 6 * ML :] = part.reshape(NT, 8, 128)
    for k in range(1, NT):
        peer = (t + NT - k) % NT
        cp = copy_to(part_ref.at[k], got_ref.at[k], s_send.at[1, k], s_recv.at[1, k], (peer, p))
        cp.start()
        small.append(cp)
    land_hop(1)
    start_hop(2)
    for cp in small[NT - 1 :]:
        cp.wait_recv()
    total = part_ref[0]
    for k in range(1, NT):
        total = total + got_ref[k]
    total = total + bias_ref[...]
    sig = 1.0 / (1.0 + jnp.exp(-total[:, 6 * ML :]))
    sig_ref[...] = sig
    mods_ref[0, :, : 6 * ML] = total[:, : 6 * ML]
    mods_ref[0, :, 6 * ML :] = sig * mask_ref[...]
    mods = []
    for r in range(1, NP):
        cp = copy_to(mods_ref.at[0], mods_ref.at[r], s_send.at[2, r], s_recv.at[2, r], (t, xor(p, r)))
        cp.start()
        mods.append(cp)

    passed = []

    def land_image(i):
        for k in range(1, NX):
            for j in range(NX):
                sent[i, k, j].wait_recv()
            cp = copy_to(
                rows_ref.at[i, 2 * k], rows_ref.at[i, 2 * k + 1],
                c_send.at[i, k, 0], c_recv.at[i, k, 0], core,
            )
            cp.start()
            passed.append(cp)

    ring_left = list(range(2, NT // 2 + 1))
    images_left = list(range(I))
    while ring_left or images_left:
        if images_left:
            land_image(images_left.pop(0))
        if ring_left:
            d = ring_left.pop(0)
            land_hop(d)
            if d < NT // 2:
                start_hop(d + 1)
    for cp in own + passed + mods:
        cp.wait_recv()
    for cp in locals_:
        cp.wait()
    for cp in small + mods + own + passed + list(sent.values()) + list(hops.values()):
        cp.wait_send()


def start_call(NT, NP, x, w, msg, ada, gates, bias, mask):
    I, CB, length = x.shape
    NX = NP // 2
    RB, WN = w.shape
    wide = 6 * ML + 128
    hbm, vmem = pl.BlockSpec(memory_space=pl.ANY), pl.BlockSpec(memory_space=pltpu.VMEM)
    dma = pltpu.SemaphoreType.DMA
    return pl.pallas_call(
        functools.partial(start_kernel, NT, NP),
        in_specs=[hbm, hbm] + [vmem] * 5,
        out_specs=[hbm, hbm, vmem, vmem, vmem],
        out_shape=[
            jax.ShapeDtypeStruct((I, NP, CB, length), bf16),
            jax.ShapeDtypeStruct((NT, RB, WN), bf16),
            jax.ShapeDtypeStruct((NP, 8, wide), f32),
            jax.ShapeDtypeStruct((8, 128), f32),
            jax.ShapeDtypeStruct((NT, 8, ML), f32),
        ],
        scratch_shapes=[
            pltpu.VMEM((NT, 8, wide), f32),
            pltpu.VMEM((NT, 8, wide), f32),
            dma((I, NX, NX)),
            dma((I, NX, NX)),
            dma((I, NX, NX)),
            dma((I, NX, NX)),
            dma((2, NT // 2 + 1)),
            dma((2, NT // 2 + 1)),
            dma((3, max(NT, NP))),
            dma((3, max(NT, NP))),
            dma((I + 1, NX)),
        ],
        compiler_params=pltpu.CompilerParams(
            collective_id=0, has_side_effects=True, vmem_limit_bytes=32 * 2**20
        ),
        name="start",
    )(x, w, msg, ada, gates, bias, mask)


def fwd_kernel(
    NT, NP, gate_ref, rows_ref, w_ref, mod_ref, bias_ref, late_ref,
    attn_ref, qkv_ref, mixed_ref, concat_ref, lse_ref, stats_ref, branch_ref, full_ref,
    wt_ref, own_ref, core_out, core_in, x_out, x_in, total_ref,
    l_send, l_recv, c_send, c_recv, x_send, x_recv, b_send, b_recv, local_sem,
):
    NX, SUB = NP // 2, NT // NP
    I, CB, T = total_ref.shape[0], total_ref.shape[2], total_ref.shape[3]
    HL = gate_ref.shape[0] // I
    QKV = 3 * HL * HP
    steps = HL + 2
    i, s = pl.program_id(0), pl.program_id(1)
    flat = i * steps + s
    t, p = lax.axis_index("tok"), lax.axis_index("tp")
    ring = Ring(NT)
    q = ring.place(t)
    right, left = (ring.tok(q + 1), p), (ring.tok(q - 1), p)
    core = (t, xor(p, 1))

    def at(n):
        return pl.when(flat == n)

    def where(tt):
        out = 0
        for r in range(NP):
            out = out + jnp.where(p == r, xor(tt // SUB, r), 0)
        return out * SUB + tt % SUB

    def hop(k, d, side):
        block = where(ring.tok(q - (d - 1) if side == 0 else q + (d - 1)))
        dst = full_ref.at[k, :, block]
        src = late_ref.at[k] if d == 1 else dst
        if d == NT // 2:
            src, dst = src.at[side], dst.at[side]
        return copy_to(src, dst, l_send.at[k, side, d], l_recv.at[k, side, d], left if side else right)

    def keep(k):
        return pltpu.make_async_copy(late_ref.at[k], full_ref.at[k, :, where(t)], local_sem.at[k])

    def start_hop(k, d):
        for side in range(2):
            hop(k, d, side).start()

    def land_hop(k, d):
        for side in range(2):
            hop(k, d, side).wait_recv()
        if d < NT // 2:
            start_hop(k, d + 1)

    def core_copy(i):
        return copy_to(core_out.at[i], core_in.at[i], c_send.at[i], c_recv.at[i], core)

    def x_copy(i, k):
        return copy_to(
            x_out.at[i, k], x_in.at[i, k], x_send.at[i, k], x_recv.at[i, k], (t, xor(p, 2 * k))
        )

    def back_copy(i):
        return copy_to(total_ref.at[i], branch_ref.at[i, 1], b_send.at[i], b_recv.at[i], core)

    def back_keep(i):
        return pltpu.make_async_copy(total_ref.at[i], branch_ref.at[i, 0], local_sem.at[NX + i])

    def add_core(i):
        core_copy(i).wait_recv()
        for f in range(NX):
            for k in range(NX):
                cols = slice(k * T, (k + 1) * T)
                v = own_ref[f, :, cols] + core_in[i, f, :, cols].astype(f32)
                if k == 0:
                    total_ref[i, f] = v
                else:
                    x_out[i, k, f] = v.astype(bf16)
        for k in range(1, NX):
            x_copy(i, k).start()

    def add_x(i):
        for k in range(1, NX):
            x_copy(i, k).wait_recv()
        for f in range(NX):
            v = total_ref[i, f]
            for k in range(1, NX):
                v = v + x_in[i, k, f ^ k].astype(f32)
            total_ref[i, f] = v
        back_copy(i).start()
        back_keep(i).start()

    @at(0)
    def _():
        barrier = pltpu.get_barrier_semaphore()
        peers = [right, left, core] + [(t, xor(p, 2 * k)) for k in range(1, NX)]
        for peer in peers:
            pl.semaphore_signal(barrier, inc=1, device_id=peer, device_id_type=MESH)
        pl.semaphore_wait(barrier, len(peers))
        for k in range(NX):
            start_hop(k, 1)
        for k in range(NX):
            keep(k).start()
        wt_ref[...] = w_ref[:, :QKV].T

    @pl.when(s == 0)
    def _():
        width = 256
        for j in range(LEN // width):
            cols = slice(j * width, (j + 1) * width)
            v = rows_ref[0, :, cols].astype(f32)
            centre = jnp.sum(v, axis=0, keepdims=True) * (1.0 / D)
            square = jnp.sum(v * v, axis=0, keepdims=True) * (1.0 / D)
            inverse = lax.rsqrt(square - centre * centre + EPS)
            stats_ref[0, 0:1, cols] = centre
            stats_ref[0, 1:2, cols] = inverse
            n = (v - centre) * inverse
            a = (n * (1.0 + mod_ref[0, :, 1:2]) + mod_ref[0, :, 0:1]).astype(bf16)
            attn_ref[0, :, cols] = a
            out = jnp.dot(wt_ref[...], a, preferred_element_type=f32) + bias_ref[...]
            qkv_ref[0, :, cols] = out.astype(bf16)

    @pl.when((s > 0) & (s <= HL))
    def _():
        h = s - 1
        gate = gate_ref[i * HL + h]

        def head(k):
            return pl.ds(pl.multiple_of((k * HL + h) * HP, HP), HP)

        keys = qkv_ref[0, head(1)].T
        sc = jnp.dot(keys, qkv_ref[0, head(0)], preferred_element_type=f32)
        top = jnp.max(sc, axis=0, keepdims=True)
        pr = jnp.exp2((sc - top) * SCALE2).astype(bf16)
        out = jnp.dot(qkv_ref[0, head(2)], pr, preferred_element_type=f32)
        total = out[HD : HD + 1]
        mixed = out * (1.0 / total)
        mixed_ref[0, head(0)] = mixed
        concat_ref[0, head(0)] = (mixed * gate).astype(bf16)
        lse_ref[0, pl.ds(h, 1)] = top * SCALE2 + jnp.log2(total)

    @pl.when(s == HL + 1)
    def _():
        for r in range(NP):
            w = w_ref[r * CB : (r + 1) * CB, w_ref.shape[1] - HL * HP :]
            part = jnp.dot(w, concat_ref[0], preferred_element_type=f32)
            if r % 2 == 0:
                own_ref[r // 2] = part
            else:
                core_out[i, r // 2] = part.astype(bf16)
        core_copy(i).start()

    for n in range(I - 1):
        at((n + 1) * steps + 1)(functools.partial(add_core, n))
        at((n + 1) * steps + HL)(functools.partial(add_x, n))

    events = [(k, d) for d in range(1, NT // 2 + 1) for k in range(NX)]
    early = [steps + HL, 2 * steps - 1][: len(events)] if I > 1 else []
    for n, (k, d) in zip(early, events):
        at(n)(functools.partial(land_hop, k, d))

    @at(I * steps - 1)
    def _():
        add_core(I - 1)
        rest = events[len(early) :]
        for n, (k, d) in enumerate(rest):
            land_hop(k, d)
            if n == 0:
                add_x(I - 1)
        for n in range(I):
            back_copy(n).wait_recv()
        for n in range(I):
            core_copy(n).wait_send()
            back_copy(n).wait_send()
            back_keep(n).wait()
            for k in range(1, NX):
                x_copy(n, k).wait_send()
        for k in range(NX):
            keep(k).wait()
            for d in range(1, NT // 2 + 1):
                for side in range(2):
                    hop(k, d, side).wait_send()


def fwd_call(NT, NP, gate, rows, w, mods, bias, late):
    I, _, length = rows.shape
    NX = NP // 2
    CB, T = D // NP, length // NX
    HL = gate.shape[0] // I
    QKV = 3 * HL * HP
    RB, FL = late.shape[2:]
    hbm = pl.BlockSpec(memory_space=pl.ANY)
    dma = pltpu.SemaphoreType.DMA

    def image(*shape):
        return pl.BlockSpec((1,) + shape, lambda i, s: (i,) + (0,) * len(shape))

    def whole(*shape):
        return pl.BlockSpec(shape, lambda i, s: (0,) * len(shape))

    return pl.pallas_call(
        functools.partial(fwd_kernel, NT, NP),
        grid=(I, HL + 2),
        in_specs=[
            pl.BlockSpec(memory_space=pltpu.SMEM),
            image(D, length),
            whole(*w.shape),
            image(D, mods.shape[2]),
            whole(*bias.shape),
            hbm,
        ],
        out_specs=[
            image(D, length),
            image(QKV, length),
            image(HL * HP, length),
            image(HL * HP, length),
            image(HL, length),
            image(8, length),
            hbm,
            hbm,
        ],
        out_shape=[
            jax.ShapeDtypeStruct((I, D, length), bf16),
            jax.ShapeDtypeStruct((I, QKV, length), bf16),
            jax.ShapeDtypeStruct((I, HL * HP, length), f32),
            jax.ShapeDtypeStruct((I, HL * HP, length), bf16),
            jax.ShapeDtypeStruct((I, HL, length), f32),
            jax.ShapeDtypeStruct((I, 8, length), f32),
            jax.ShapeDtypeStruct((I, 2, NX, CB, T), f32),
            jax.ShapeDtypeStruct((NX, 2, NT, RB, FL), bf16),
        ],
        scratch_shapes=[
            pltpu.VMEM((QKV, D), bf16),
            pltpu.VMEM((NX, CB, length), f32),
            pltpu.VMEM((I, NX, CB, length), bf16),
            pltpu.VMEM((I, NX, CB, length), bf16),
            pltpu.VMEM((I, NX, NX, CB, T), bf16),
            pltpu.VMEM((I, NX, NX, CB, T), bf16),
            pltpu.VMEM((I, NX, CB, T), f32),
            dma((NX, 2, NT // 2 + 1)),
            dma((NX, 2, NT // 2 + 1)),
            dma((I,)),
            dma((I,)),
            dma((I, NX)),
            dma((I, NX)),
            dma((I,)),
            dma((I,)),
            dma((NX + I,)),
        ],
        compiler_params=pltpu.CompilerParams(
            collective_id=2, has_side_effects=True, vmem_limit_bytes=60 * 2**20
        ),
        name="forward",
    )(gate, rows, w, mods, bias, late)


def bwd_kernel(
    NT, NP, gate_ref, go_ref, gms_ref, gm_ref, qkv_ref, mixed_ref, lse_ref, concat_ref, attn_ref,
    rows_ref, stats_ref, scale_ref, w_ref, late_ref, base_ref, factor_ref, ada_ref,
    gin_ref, late_out, gqkv_ref, gout_ref, lasts_ref, cond_ref, gox_ref,
    go_buf, gmx_ref, own_ref, core_out, core_in, x_out, x_in, gn_ref, accq_ref, acco_ref, wt_ref,
    gc_ref, dqkv_ref, rows_buf, gin_buf, st_out, st_in, msg_ref, heads_ref, qv_ref,
    l_own, l_out, l_in, lx_out, lx_in, q_out, q_in, part_ref, sum_ref, lasts_buf,
    g_send, g_recv, c_send, c_recv, x_send, x_recv, t_send, t_recv, l_send, l_recv, lx_send, lx_recv,
    q_send, q_recv, s_send, s_recv, m_send, m_recv, local_sem, own_sem,
):
    NX, SUB = NP // 2, NT // NP
    I, CB, T = gm_ref.shape
    HL = gate_ref.shape[0] // I
    QKV, HO = 3 * HL * HP, HL * HP
    RB = D // NT
    HOPS = NT // 2
    steps = HL + 2
    i, s = pl.program_id(0), pl.program_id(1)
    flat = i * steps + s
    t, p = lax.axis_index("tok"), lax.axis_index("tp")
    xi = p // 2
    ring = Ring(NT)
    q = ring.place(t)
    right, left = (ring.tok(q + 1), p), (ring.tok(q - 1), p)
    core = (t, xor(p, 1))

    def at(n):
        return pl.when(flat == n)

    def partner(k):
        return (t, xor(p, 2 * k))

    def where(tt):
        out = 0
        for r in range(NP):
            out = out + jnp.where(p == r, xor(tt // SUB, r), 0)
        return out * SUB + tt % SUB

    def go_x(n, k, f):
        return copy_to(
            go_ref.at[n, f, 0], gox_ref.at[n, k, f ^ k, 0], g_send.at[0, n, k, f],
            g_recv.at[0, n, k, f], partner(k),
        )

    def go_core(n, k, f):
        return copy_to(
            gox_ref.at[n, k, f, 0], gox_ref.at[n, k, f, 1], g_send.at[1, n, k, f],
            g_recv.at[1, n, k, f], core,
        )

    def gm_x(n, k):
        return copy_to(gms_ref.at[n, k], gmx_ref.at[n, k - 1], m_send.at[n, k], m_recv.at[n, k], partner(k))

    def send_go(n):
        for k in range(1, NX):
            for f in range(NX):
                go_x(n, k, f).start()

    def pass_go(n):
        for k in range(1, NX):
            for f in range(NX):
                go_x(n, k, f ^ k).wait_recv()
                go_core(n, k, f).start()
        if n + 1 < I:
            send_go(n + 1)
        for m in [n - 1] if n + 1 < I else [n - 1, n]:
            if m >= 0:
                for k in range(1, NX):
                    gm_x(m, k).start()

    def load_go(n):
        def load(k):
            src = go_ref.at[n] if k == 0 else gox_ref.at[n, k]
            return pltpu.make_async_copy(src, go_buf.at[k], local_sem.at[k])

        load(0).start()
        for k in range(1, NX):
            for f in range(NX):
                go_core(n, k, f).wait_recv()
            load(k).start()
        for k in range(NX):
            load(k).wait()

    def rows_copy(n):
        return pltpu.make_async_copy(rows_ref.at[n, 0], rows_buf.at[n], local_sem.at[NX + n])

    def core_copy(n):
        return copy_to(core_out, core_in.at[n % 2], c_send.at[n], c_recv.at[n], core)

    def x_copy(n, k):
        return copy_to(
            x_out.at[n % 2, k - 1], x_in.at[n % 2, k - 1], x_send.at[n, k], x_recv.at[n, k], partner(k)
        )

    def st_copy(n, r):
        return copy_to(
            st_out.at[n], st_in.at[n, r], t_send.at[n, r], t_recv.at[n, r], (t, xor(p, r))
        )

    def gin_copy(n, j):
        to = pl.ds(pl.multiple_of(xor(xi, j) * T, T), T)
        return pltpu.make_async_copy(
            gin_buf.at[n % 2, :, pl.ds(j * T, T)], gin_ref.at[n, :, to], local_sem.at[NX + I + n * NX + j]
        )

    def add_core(n):
        core_copy(n).wait_recv()
        if n >= 2:
            for k in range(1, NX):
                x_copy(n - 2, k).wait_send()
        for f in range(NX):
            v = own_ref[f] + core_in[n % 2, f].astype(f32)
            if f == 0:
                gn_ref[...] = v
            else:
                x_out[n % 2, f - 1] = v.astype(bf16)
        for k in range(1, NX):
            x_copy(n, k).start()

    def tokens(v):
        total = v[:, :128]
        for j in range(1, LEN // 128):
            total = total + v[:, j * 128 : (j + 1) * 128]
        return jnp.sum(total.T, axis=0, keepdims=True)

    def normed(n):
        return (rows_buf[n].astype(f32) - stats_ref[n, 0:1]) * stats_ref[n, 1:2]

    def add_x(n):
        for k in range(1, NX):
            x_copy(n, k).wait_recv()
        for j in range(NX):
            v = gn_ref[:, j * T : (j + 1) * T]
            for k in range(1, NX):
                v = v + x_in[n % 2, k - 1, :, (j ^ k) * T : ((j ^ k) + 1) * T].astype(f32)
            gn_ref[:, j * T : (j + 1) * T] = v
        v = gn_ref[...]
        vn = v * normed(n)
        scale = 1.0 + scale_ref[n]
        st_out[n, 0:1] = jnp.sum(v * scale, axis=0, keepdims=True)
        st_out[n, 1:2] = jnp.sum(vn * scale, axis=0, keepdims=True)
        for r in range(1, NP):
            st_copy(n, r).start()
        msg_ref[n : n + 1, :CB] = tokens(v)
        msg_ref[n : n + 1, ML : ML + CB] = tokens(vn)

    def add_stats(n):
        for r in range(1, NP):
            st_copy(n, r).wait_recv()
        if n >= 2:
            for j in range(NX):
                gin_copy(n - 2, j).wait()
        for k in range(1, NX):
            gm_x(n, k).wait_recv()
        for j in range(NX):
            cols = slice(j * T, (j + 1) * T)
            a, b = st_out[n, 0:1, cols], st_out[n, 1:2, cols]
            for r in range(1, NP):
                m = j ^ (r // 2)
                a = a + st_in[n, r, 0:1, m * T : (m + 1) * T]
                b = b + st_in[n, r, 1:2, m * T : (m + 1) * T]
            centre, inverse = stats_ref[n, 0:1, cols], stats_ref[n, 1:2, cols]
            nrm = (rows_buf[n, :, cols].astype(f32) - centre) * inverse
            g = gn_ref[:, cols] * (1.0 + scale_ref[n])
            mid = gm_ref[n] if j == 0 else gmx_ref[n, j - 1].astype(f32)
            gin_buf[n % 2, :, cols] = mid + inverse * (g - a * (1.0 / D) - nrm * (b * (1.0 / D)))
        for j in range(NX):
            gin_copy(n, j).start()

    def l_block(side, h):
        d = HOPS - h
        return where(ring.tok(q + d if side == 0 else q - d))

    def l_load(k, side, h):
        return pltpu.make_async_copy(
            late_ref.at[k, :, l_block(side, h)], l_own.at[k, side], own_sem.at[k, side]
        )

    def l_hop(k, side, h):
        to = left if side else right
        if h == 0:
            return copy_to(
                late_ref.at[k, side, l_block(side, 0)], l_in.at[k, side, 0, side],
                l_send.at[k, side, h], l_recv.at[k, side, h], to,
            )
        return copy_to(
            l_out.at[k, side], l_in.at[k, side, h % 2], l_send.at[k, side, h], l_recv.at[k, side, h], to
        )

    def l_event(k, h):
        for side in range(2):
            l_hop(k, side, h - 1).wait_recv()
        for side in range(2):
            if h < HOPS or side == 0:
                l_load(k, side, h).wait()
            if 1 < h < HOPS:
                l_hop(k, side, h - 1).wait_send()
        if h < HOPS:
            for side in range(2):
                for u in range(2):
                    v = l_own[k, side, u]
                    if h > 1 or u == side:
                        v = (v.astype(f32) + l_in[k, side, (h - 1) % 2, u].astype(f32)).astype(bf16)
                    l_out[k, side, u] = v
            for side in range(2):
                l_hop(k, side, h).start()
                if h + 1 < HOPS or side == 0:
                    l_load(k, side, h + 1).start()
        else:
            for u in range(2):
                v = l_own[k, 0, u].astype(f32)
                for side in range(2):
                    if HOPS > 1 or u == side:
                        v = v + l_in[k, side, (h - 1) % 2, u].astype(f32)
                if k == 0:
                    late_out[u] = v
                else:
                    lx_out[k - 1, u] = v.astype(bf16)
            if k:
                lx_copy(k).start()

    def lx_copy(k):
        return copy_to(lx_out.at[k - 1], lx_in.at[k - 1], lx_send.at[k], lx_recv.at[k], partner(k))

    half = (QKV // 2 + 127) // 128 * 128

    def q_block(side, h):
        return l_block(side, h)

    def q_hop(side, h):
        to = left if side else right
        return copy_to(
            q_out.at[side], q_in.at[side, h % 2], q_send.at[side, h], q_recv.at[side, h], to
        )

    def q_event(h):
        if h:
            for side in range(2):
                q_hop(side, h - 1).wait_recv()
        if h < HOPS:
            for side in range(2):
                if h:
                    q_hop(side, h - 1).wait_send()
                block = q_block(side, h)
                a, b = accq_ref[block], acco_ref[block]
                if h:
                    a = a + q_in[side, (h - 1) % 2, :, :QKV].astype(f32)
                    b = b + q_in[side, (h - 1) % 2, :, QWIDE:].astype(f32)
                else:
                    lane = lax.broadcasted_iota(jnp.int32, a.shape, 1)
                    a = jnp.where((lane < half) if side == 0 else (lane >= half), a, 0.0)
                    b = b if side == 0 else jnp.zeros_like(b)
                q_out[side, :, :QKV] = a.astype(bf16)
                q_out[side, :, QWIDE:] = b.astype(bf16)
            for side in range(2):
                q_hop(side, h).start()
        else:
            a, b = accq_ref[q_block(0, h)], acco_ref[q_block(0, h)]
            for side in range(2):
                a = a + q_in[side, (h - 1) % 2, :, :QKV].astype(f32)
                b = b + q_in[side, (h - 1) % 2, :, QWIDE:].astype(f32)
            gqkv_ref[...] = a
            gout_ref[...] = b

    QWIDE = (QKV + 127) // 128 * 128

    def last_copy(k):
        return copy_to(msg_ref, lasts_buf.at[k], s_send.at[0, k], s_recv.at[0, k], ((t + k) % NT, p))

    def part_copy(k):
        return copy_to(
            part_ref.at[k], sum_ref.at[0, t], s_send.at[1, k], s_recv.at[1, k], ((t + NT - k) % NT, p)
        )

    def sum_copy(r):
        return copy_to(sum_ref.at[0], sum_ref.at[r], s_send.at[2, r], s_recv.at[2, r], (t, xor(p, r)))

    def cond_first():
        msg_ref[I : I + 1, :QKV] = qv_ref[0:1, :QKV]
        msg_ref[:, 6 * ML :] = msg_ref[:, 6 * ML :] + heads_ref[...] * factor_ref[...]
        for k in range(1, NT):
            last_copy(k).start()
        lasts_buf[0] = msg_ref[...]

    def cond_second():
        for k in range(1, NT):
            last_copy(k).wait_recv()
        lasts_ref[...] = lasts_buf[...]
        grads = lasts_buf[...].reshape(NT * 8, -1)
        total = 0.0
        for k in range(6):
            g = grads[:, k * ML : (k + 1) * ML]
            high = g.astype(bf16)
            low = (g - high.astype(f32)).astype(bf16)
            total = total + dot(high, ada_ref[k], 1, 1) + dot(low, ada_ref[k], 1, 1)
        part_ref[...] = jnp.zeros_like(part_ref)
        part_ref[:, :, :RB] = total.reshape(NT, 8, RB)
        for k in range(1, NT):
            part_copy(k).start()
        sum_ref[0, t] = part_ref[0]

    def cond_third():
        for k in range(1, NT):
            part_copy(k).wait_recv()
        for r in range(1, NP):
            sum_copy(r).start()

    def cond_last():
        total = sum_ref[0]
        for r in range(1, NP):
            sum_copy(r).wait_recv()
            total = total + sum_ref[r]
        cond_ref[...] = total

    @at(0)
    def _():
        greet(t, p, NT, NP)
        send_go(0)
        for k in range(NX):
            for side in range(2):
                l_hop(k, side, 0).start()
                l_load(k, side, 1).start()
        for n in range(I):
            rows_copy(n).start()
        msg_ref[...] = base_ref[...]
        heads_ref[...] = jnp.zeros_like(heads_ref)
        qv_ref[...] = jnp.zeros_like(qv_ref)
        wt_ref[...] = w_ref[:, w_ref.shape[1] - HO :].T
        accq_ref[...] = jnp.zeros_like(accq_ref)
        acco_ref[...] = jnp.zeros_like(acco_ref)
        for n in range(I):
            rows_copy(n).wait()

    for n in range(I):
        at(max(n - 1, 0) * steps + (HL if n else 0))(functools.partial(pass_go, n))
        at(n * steps)(functools.partial(load_go, n))

    @pl.when(s == 0)
    def _():
        for k in range(NX):
            v = go_buf[k].reshape(D, T)
            gc_ref[:, k * T : (k + 1) * T] = jnp.dot(wt_ref[...], v, preferred_element_type=f32)

    @pl.when((s > 0) & (s <= HL))
    def _():
        h = s - 1
        gate = gate_ref[i * HL + h]

        def head(k):
            return pl.ds(pl.multiple_of((k * HL + h) * HP, HP), HP)

        keys_t = qkv_ref[0, head(1)]
        keys = keys_t.T
        values = qkv_ref[0, head(2)].T
        gc = gc_ref[head(0)]
        inner = jnp.sum(mixed_ref[0, head(0)] * gc, axis=0, keepdims=True)
        lane = lax.broadcasted_iota(jnp.int32, (1, 128), 1)
        row = heads_ref[pl.ds(i, 1)]
        heads_ref[pl.ds(i, 1)] = row + jnp.where(lane == h, jnp.sum(inner), 0.0)
        delta = gate * inner
        grad = (gate * gc).astype(bf16)
        lse = lse_ref[0, pl.ds(h, 1)]
        queries = qkv_ref[0, head(0)]
        dv = jnp.zeros((LEN, HP), f32)
        dk = jnp.zeros((LEN, HP), f32)
        chunk = 256
        for j in range(LEN // chunk):
            part = slice(j * chunk, (j + 1) * chunk)
            qj = queries[:, part]
            do = grad[:, part]
            sc = jnp.dot(keys, qj, preferred_element_type=f32)
            pr = jnp.exp2(sc * SCALE2 - lse[:, part])
            dp = jnp.dot(values, do, preferred_element_type=f32)
            ds = (pr * (dp - delta[:, part])).astype(bf16)
            dv = dv + jnp.dot(pr.astype(bf16), do.T, preferred_element_type=f32)
            dk = dk + jnp.dot(ds, qj.T, preferred_element_type=f32)
            dq = jnp.dot(keys_t, ds, preferred_element_type=f32)
            dqkv_ref[head(0), part] = (dq * SCALE).astype(bf16)
        dqkv_ref[head(1)] = (dk * SCALE).T.astype(bf16)
        dqkv_ref[head(2)] = dv.T.astype(bf16)

    @pl.when(s == HL + 1)
    def _():
        for r in range(NP):
            w = w_ref[r * CB : (r + 1) * CB, :QKV]
            part = jnp.dot(w, dqkv_ref[...], preferred_element_type=f32)
            if r % 2 == 0:
                own_ref[r // 2] = part
            else:
                core_out[r // 2] = part.astype(bf16)
        for b in range(0, NT, 2):
            rows = slice(b * RB, (b + 2) * RB)
            v = dot(attn_ref[0, rows], dqkv_ref[...], 1, 1)
            accq_ref[b : b + 2] = accq_ref[b : b + 2] + v.reshape(2, RB, QKV)
            v = 0.0
            for k in range(NX):
                g = go_buf[k].reshape(D, T)[rows]
                v = v + dot(g, concat_ref[0, :, k * T : (k + 1) * T], 1, 1)
            acco_ref[b : b + 2] = acco_ref[b : b + 2] + v.reshape(2, RB, HO)
        qv_ref[0:1, :QKV] = qv_ref[0:1, :QKV] + tokens(dqkv_ref[...].astype(f32))

    for n in range(I):
        at(n * steps + HL + 1)(lambda n=n: core_copy(n).start())
    for n in range(I - 1):
        at((n + 1) * steps + 1)(functools.partial(add_core, n))
        at((n + 1) * steps + HL - 1)(functools.partial(add_x, n))

        @at((n + 1) * steps + HL)
        def _(n=n):
            add_stats(n)
            core_copy(n).wait_send()

    events = [functools.partial(l_event, k, h) for h in range(1, HOPS + 1) for k in range(NX)]
    early = [steps - 1, steps, 2 * steps - 2, 2 * steps - 1, 3 * steps - 2, 3 * steps - 1] if I > 2 else []
    early = early[: len(events)]
    for n, event in zip(early, events):
        at(n)(event)

    @at(I * steps - 1)
    def _():
        rest = events[len(early) :]
        q_event(0)
        add_core(I - 1)
        todo = [functools.partial(add_x, I - 1), cond_first, functools.partial(q_event, 1),
                functools.partial(add_stats, I - 1), cond_second]
        todo += [functools.partial(q_event, h) for h in range(2, 3)] + [cond_third]
        todo += [functools.partial(q_event, h) for h in range(3, HOPS + 1)] + [cond_last]
        ratio = max(1, len(todo) // max(1, len(rest)))
        while todo or rest:
            if rest:
                rest.pop(0)()
            for _ in range(ratio if rest else len(todo)):
                if todo:
                    todo.pop(0)()
        for k in range(1, NX):
            lx_copy(k).wait_recv()
            for u in range(2):
                late_out[u] = late_out[u] + lx_in[k - 1, u].astype(f32)
        core_copy(I - 1).wait_send()
        for n in range(I):
            for k in range(1, NX):
                gm_x(n, k).wait_send()
                for f in range(NX):
                    go_x(n, k, f).wait_send()
                    go_core(n, k, f).wait_send()
                if n >= I - 2:
                    x_copy(n, k).wait_send()
            for r in range(1, NP):
                st_copy(n, r).wait_send()
            if n >= I - 2:
                for j in range(NX):
                    gin_copy(n, j).wait()
        for k in range(NX):
            for side in range(2):
                l_hop(k, side, 0).wait_send()
                if HOPS > 1:
                    l_hop(k, side, HOPS - 1).wait_send()
        for side in range(2):
            q_hop(side, HOPS - 1).wait_send()
        for k in range(1, NX):
            lx_copy(k).wait_send()
        for k in range(1, NT):
            last_copy(k).wait_send()
            part_copy(k).wait_send()
        for r in range(1, NP):
            sum_copy(r).wait_send()


def bwd_call(
    NT, NP, gate, go, gms, gm, qkv, mixed, lse, concat, attn, rows, stats, scale, w, late, base, factor, ada
):
    I, CB, T = gm.shape
    NX = NP // 2
    length = attn.shape[2]
    HL = gate.shape[0] // I
    QKV, HO = 3 * HL * HP, HL * HP
    QWIDE = (QKV + 127) // 128 * 128
    RB, FL = late.shape[3:]
    HOPS = NT // 2
    hbm = pl.BlockSpec(memory_space=pl.ANY)
    vmem = pl.BlockSpec(memory_space=pltpu.VMEM)
    dma = pltpu.SemaphoreType.DMA
    once = pl.Buffered(buffer_count=1)

    def image(*shape):
        return pl.BlockSpec(
            (1,) + shape, lambda i, s: (i,) + (0,) * len(shape), pipeline_mode=once
        )

    return pl.pallas_call(
        functools.partial(bwd_kernel, NT, NP),
        grid=(I, HL + 2),
        in_specs=[
            pl.BlockSpec(memory_space=pltpu.SMEM),
            hbm,
            hbm,
            vmem,
            image(QKV, length),
            image(HO, length),
            image(HL, length),
            image(HO, length),
            image(D, length),
            hbm,
            vmem,
            vmem,
            vmem,
            hbm,
            vmem,
            vmem,
            vmem,
        ],
        out_specs=[hbm, vmem, vmem, vmem, vmem, vmem, hbm],
        out_shape=[
            jax.ShapeDtypeStruct((I, CB, length), f32),
            jax.ShapeDtypeStruct((2, RB, FL), f32),
            jax.ShapeDtypeStruct((RB, QKV), f32),
            jax.ShapeDtypeStruct((RB, HO), f32),
            jax.ShapeDtypeStruct((NT,) + base.shape, f32),
            jax.ShapeDtypeStruct((NT, 8, 256), f32),
            jax.ShapeDtypeStruct((I, NX, NX, 2, CB, T), bf16),
        ],
        scratch_shapes=[
            pltpu.VMEM((NX, NX, 2, CB, T), bf16),
            pltpu.VMEM((I, NX - 1, CB, T), bf16),
            pltpu.VMEM((NX, CB, length), f32),
            pltpu.VMEM((NX, CB, length), bf16),
            pltpu.VMEM((2, NX, CB, length), bf16),
            pltpu.VMEM((2, NX - 1, CB, length), bf16),
            pltpu.VMEM((2, NX - 1, CB, length), bf16),
            pltpu.VMEM((CB, length), f32),
            pltpu.VMEM((NT, RB, QKV), f32),
            pltpu.VMEM((NT, RB, HO), f32),
            pltpu.VMEM((HO, D), bf16),
            pltpu.VMEM((HO, length), f32),
            pltpu.VMEM((QKV, length), bf16),
            pltpu.VMEM((I, CB, length), bf16),
            pltpu.VMEM((2, CB, length), f32),
            pltpu.VMEM((I, 8, length), f32),
            pltpu.VMEM((I, NP, 8, length), f32),
            pltpu.VMEM(base.shape, f32),
            pltpu.VMEM((8, 128), f32),
            pltpu.VMEM((8, QWIDE), f32),
            pltpu.VMEM((NX, 2, 2, RB, FL), bf16),
            pltpu.VMEM((NX, 2, 2, RB, FL), bf16),
            pltpu.VMEM((NX, 2, 2, 2, RB, FL), bf16),
            pltpu.VMEM((NX - 1, 2, RB, FL), bf16),
            pltpu.VMEM((NX - 1, 2, RB, FL), bf16),
            pltpu.VMEM((2, RB, QWIDE + HO), bf16),
            pltpu.VMEM((2, 2, RB, QWIDE + HO), bf16),
            pltpu.VMEM((NT, 8, 256), f32),
            pltpu.VMEM((NP, NT, 8, 256), f32),
            pltpu.VMEM((NT,) + base.shape, f32),
            dma((2, I, NX, NX)),
            dma((2, I, NX, NX)),
            dma((I,)),
            dma((I,)),
            dma((I, NX)),
            dma((I, NX)),
            dma((I, NP)),
            dma((I, NP)),
            dma((NX, 2, HOPS)),
            dma((NX, 2, HOPS)),
            dma((NX,)),
            dma((NX,)),
            dma((2, HOPS)),
            dma((2, HOPS)),
            dma((3, max(NT, NP))),
            dma((3, max(NT, NP))),
            dma((I, NX)),
            dma((I, NX)),
            dma((NX + I + I * NX,)),
            dma((NX, 2)),
        ],
        compiler_params=pltpu.CompilerParams(
            collective_id=1, has_side_effects=True, vmem_limit_bytes=63 * 2**20
        ),
        name="backward",
    )(gate, go, gms, gm, qkv, mixed, lse, concat, attn, rows, stats, scale, w, late, base, factor, ada)


def make_body(NT, NP):
    NX = NP // 2
    SUB = NT // NP
    RB = D // NT
    CB = D // NP
    T = LEN // NX

    def tp_xor(v, r):
        return lax.ppermute(v, "tp", [(p, p ^ r) for p in range(NP)])

    def body(
        block_input,
        condition,
        timesteps,
        head_mask,
        group_mask,
        w_ada,
        b_ada,
        w_qkv,
        b_qv,
        w_out,
        b_out,
        w_up,
        b_up,
        w_down,
        b_down,
        w_head,
        b_head,
        w_group,
        b_group,
        cotangent,
    ):
        I = condition.shape[0]
        HL = head_mask.shape[1]
        GL = group_mask.shape[1]
        FL = w_up.shape[1]
        FR = FREQ // NT
        t = lax.axis_index("tok")
        p = lax.axis_index("tp")
        xi = p // 2

        def own_order(v, axis):
            parts = [
                lax.dynamic_slice_in_dim(v, jnp.bitwise_xor(j, xi) * T, T, axis=axis)
                for j in range(NX)
            ]
            return jnp.concatenate(parts, axis=axis)

        qkv_shard = jnp.pad(
            w_qkv.reshape(RB, 3, HL, HD), ((0, 0), (0, 0), (0, 0), (0, HP - HD))
        ).reshape(RB, 3 * HL * HP)
        out_shard = jnp.pad(w_out.T.reshape(RB, HL, HD), ((0, 0), (0, 0), (0, HP - HD))).reshape(
            RB, HL * HP
        )
        QKV = 3 * HL * HP
        gap = -QKV % 128
        early_shard = jnp.concatenate(
            [qkv_shard, jnp.zeros((RB, gap), bf16), out_shard], axis=1
        )
        late_shard = jnp.stack([w_up, w_down.T])
        late_shards = jnp.stack(
            [late_shard] + [tp_xor(late_shard, 2 * k) for k in range(1, NX)]
        )
        time_feat = embed_time(timesteps).astype(bf16)
        cond_wide = condition.astype(f32)
        cond_act = jax.nn.silu(cond_wide).astype(bf16)
        pad8 = lambda v, width: jnp.pad(v, ((0, 8 - v.shape[0]), (0, width - v.shape[1])))
        message = jnp.concatenate(
            [
                jnp.pad(cond_act.reshape(I, NT, RB), ((0, 0), (0, 0), (0, 256 - RB))),
                jnp.pad(time_feat.reshape(I, NT, FR), ((0, 0), (0, 0), (0, ML - 256 - FR))),
            ],
            axis=2,
        )
        message = jnp.pad(message.transpose(1, 0, 2).astype(f32), ((0, 0), (0, 8 - I), (0, 0)))
        ada = jnp.pad(w_ada.transpose(1, 0, 2), ((0, 0), (0, 0), (0, ML - CB)))
        gates = jnp.concatenate([w_head, w_group], axis=1)
        gates = jnp.pad(gates, ((0, 0), (0, 128 - HL - GL)))
        wide = 6 * ML + 128
        mod_bias = jnp.concatenate(
            [jnp.pad(b_ada, ((0, 0), (0, ML - CB))).reshape(6 * ML), b_head, b_group]
        ).astype(f32)
        bias = jnp.concatenate(
            [
                jnp.broadcast_to(pad8(mod_bias[None], wide)[:1], (I, wide)),
                pad8(jnp.concatenate([jnp.pad(b_out, (0, ML - CB)), b_down]).astype(f32)[None], wide)[:1],
                pad8(b_up.astype(f32)[None], wide)[: 8 - I - 1],
            ],
            axis=0,
        )
        mask = pad8(jnp.concatenate([head_mask, group_mask], axis=1).astype(f32), 128)
        rows_all, early_full, mods, sig, cond_all = start_call(
            NT,
            NP,
            block_input,
            early_shard,
            message,
            ada,
            gates,
            bias,
            mask,
        )
        rows_full = [rows_all[i].reshape(D, LEN) for i in range(I)]
        early_full = early_full.reshape(D, -1)
        qkv_full, out_full = early_full[:, :QKV], early_full[:, QKV + gap :]
        head_sig, group_sig = sig[:I, :HL], sig[:I, HL : HL + GL]
        head_gate = mods[0, :I, 6 * ML : 6 * ML + HL]
        vectors = mods[:, :I, : 6 * ML].reshape(NP, I * 6, ML)[:, :, :CB]
        biases_two = mods[:, I, : 2 * ML].reshape(NP, 2, ML)[:, :, :CB]
        columns = jnp.concatenate([vectors, biases_two], axis=1).transpose(0, 2, 1).reshape(D, -1)

        def mod(i, k):
            return lax.slice_in_dim(columns, i * 6 + k, i * 6 + k + 1, axis=1)

        out_bias = columns[:, I * 6 : I * 6 + 1]
        down_bias = columns[:, I * 6 + 1 : I * 6 + 2]
        gates_x = jnp.concatenate(
            [mods[2 * k, :I, 6 * ML + HL : 6 * ML + HL + GL] for k in range(NX)], axis=1
        )
        gate_cols = jnp.repeat(gates_x, GW, axis=1).T
        up_bias = jnp.concatenate([mods[2 * k, I + 1, :FL] for k in range(NX)])[:, None]

        cot_in = own_order(cotangent, 2)
        cot_blocks = []
        for k in range(NX):
            v = cot_in[:, :, k * T : (k + 1) * T]
            v = v if k == 0 else tp_xor(v, 2 * k)
            cot_blocks.append(v)
        cot_half = jnp.stack(cot_blocks, axis=1)
        cot_full = jnp.stack([cot_half, tp_xor(cot_half, 1)], axis=2).reshape(I, D, T)

        qv = b_qv.astype(f32).reshape(2, HL, HD)
        qv_bias = jnp.stack(
            [
                jnp.pad(qv[0], ((0, 0), (0, HP - HD))),
                jnp.zeros((HL, HP), f32),
                jnp.concatenate(
                    [qv[1], jnp.ones((HL, 1), f32), jnp.zeros((HL, HP - HD - 1), f32)], axis=1
                ),
            ]
        ).reshape(3 * HL * HP, 1)

        def stats(v):
            centre = jnp.sum(v, axis=0, keepdims=True) * (1.0 / D)
            square = jnp.sum(v * v, axis=0, keepdims=True) * (1.0 / D)
            return centre, lax.rsqrt(square - centre * centre + EPS)

        image_mods = columns[:, : I * 6].reshape(D, I, 6).transpose(1, 0, 2)
        attn_all, qkv_all, mixed_all, concat_all, lse_all, stats_all, branch, late_full = fwd_call(
            NT,
            NP,
            head_gate.reshape(-1),
            rows_all.reshape(I, D, LEN),
            early_full,
            image_mods,
            qv_bias,
            late_shards,
        )
        late_full = late_full.reshape(NX, 2, D, FL)
        up_full = jnp.concatenate([late_full[k, 0] for k in range(NX)], axis=1)
        down_full = jnp.concatenate([late_full[k, 1] for k in range(NX)], axis=1)
        branch = branch.transpose(0, 2, 1, 3, 4).reshape(I, D, T)
        mids = []
        for i in range(I):
            branch_one = branch[i] + out_bias
            cot = cot_full[i].astype(f32)
            mid_rows = rows_full[i][:, :T].astype(f32) + mod(i, 2) * branch_one
            centre, inverse = stats(mid_rows)
            normed = (mid_rows - centre) * inverse
            mlp_in = (normed * (1.0 + mod(i, 4)) + mod(i, 3)).astype(bf16)
            grad_two = (mod(i, 5) * cot).astype(bf16)
            pre = dot(up_full, mlp_in, 0, 0) + up_bias
            grad_hid = dot(down_full, grad_two, 0, 0)
            gate = gate_cols[:, i : i + 1]
            inner = jnp.tanh(math.sqrt(2.0 / math.pi) * (pre + 0.044715 * pre * pre * pre))
            act = 0.5 * pre * (1.0 + inner)
            slope = 0.5 * (1.0 + inner) + 0.5 * pre * (1.0 - inner * inner) * math.sqrt(
                2.0 / math.pi
            ) * (1.0 + 3.0 * 0.044715 * pre * pre)
            hidden = (act * gate).astype(bf16)
            grad_pre = (slope * gate * grad_hid).astype(bf16)
            gate_sums = jnp.sum(jnp.sum(grad_hid * act, axis=1).reshape(NX * GL, GW), axis=1)
            up_sums = jnp.sum(grad_pre.astype(f32), axis=1)
            gpart = dot(up_full, grad_pre, 1, 0)
            got = tp_xor(gpart.astype(bf16), 1).reshape(NX, 2, CB, T)
            got = jnp.stack([got[:, 1], got[:, 0]], axis=1).reshape(D, T)
            gnorm = gpart + got.astype(f32)
            shift_sums = jnp.sum(gnorm, axis=1)
            scale_sums = jnp.sum(gnorm * normed, axis=1)
            g = gnorm * (1.0 + mod(i, 4))
            mean_g = jnp.sum(g, axis=0, keepdims=True) * (1.0 / D)
            mean_gn = jnp.sum(g * normed, axis=0, keepdims=True) * (1.0 / D)
            grad_mid = cot + inverse * (g - mean_g - normed * mean_gn)
            gate_one_sums = jnp.sum(grad_mid * branch_one, axis=1)
            grad_one = (mod(i, 2) * grad_mid).astype(bf16)
            out_sums = jnp.sum(grad_one.astype(f32), axis=1)
            bpart = dot(down_full, hidden, 1, 0).reshape(NX, 2, CB, T)
            branch_two = (
                bpart[:, 0]
                + tp_xor(bpart[:, 1].astype(bf16), 1).astype(f32)
                + down_bias.reshape(NX, 2, CB, 1)[:, 0]
            )
            half = lambda v: v.reshape(NX, 2, CB, -1)[:, 0]
            gate_two_sums = jnp.sum(half(cot) * branch_two, axis=2)
            out_half = (half(mid_rows) + half(mod(i, 5)) * branch_two).astype(bf16)
            out_blocks = [out_half[0]] + [tp_xor(out_half[k], 2 * k) for k in range(1, NX)]
            out_own = jnp.concatenate(out_blocks, axis=1)
            down_sums = jnp.sum(grad_two.astype(f32), axis=1)
            mids.append(
                dict(
                    grad_two=grad_two,
                    hidden=hidden,
                    grad_pre=grad_pre,
                    mlp_in=mlp_in,
                    grad_one=grad_one,
                    grad_mid=grad_mid,
                    out_own=out_own,
                    sums=(gate_one_sums, shift_sums, scale_sums),
                    gate_two_sums=gate_two_sums,
                    gate_sums=gate_sums,
                    up_sums=up_sums,
                    out_sums=out_sums,
                    down_sums=down_sums,
                )
            )

        block_output = own_order(jnp.stack([m["out_own"] for m in mids]), 2)

        grad_down = sum(dot(m["grad_two"], m["hidden"], 1, 1) for m in mids)
        grad_up = sum(dot(m["mlp_in"], m["grad_pre"], 1, 1) for m in mids)
        late_grads = jnp.stack(
            [
                jnp.stack([g[:, k * FL : (k + 1) * FL] for g in (grad_up, grad_down)])
                for k in range(NX)
            ]
        ).astype(bf16).reshape(NX, 2, NT, RB, FL)

        def x_message(k):
            parts = []
            for m in mids:
                for v in m["sums"]:
                    parts.append(v[2 * k * CB : (2 * k + 1) * CB])
                parts.append(m["gate_two_sums"][k])
                parts.append(m["gate_sums"][k * GL : (k + 1) * GL])
            for name, size in (("out_sums", 2 * k * CB), ("down_sums", 2 * k * CB)):
                parts.append(sum(m[name] for m in mids)[size : size + CB])
            parts.append(sum(m["up_sums"] for m in mids)[k * FL : (k + 1) * FL])
            return jnp.concatenate(parts)

        x_total = x_message(0)
        for k in range(1, NX):
            x_total = x_total + tp_xor(x_message(k), 2 * k)
        per = 4 * CB + GL
        per_image = x_total[: I * per].reshape(I, per)
        late_mods = per_image[:, : 4 * CB].reshape(I, 4, CB)
        grad_group_gate = per_image[:, 4 * CB :]
        bias_sums = x_total[I * per :]

        head_factor = head_mask.astype(f32) * head_sig * (1.0 - head_sig)
        group_logit = grad_group_gate * group_mask.astype(f32) * group_sig * (1.0 - group_sig)
        image_rows = jnp.concatenate(
            [
                jnp.pad(late_mods, ((0, 0), (2, 0), (0, ML - CB))).reshape(I, 6 * ML),
                jnp.zeros((I, HL), f32),
                group_logit,
                jnp.zeros((I, 128 - HL - GL), f32),
            ],
            axis=1,
        )
        widen = lambda v: jnp.pad(v, (0, wide - v.shape[0]))[None]
        base = jnp.concatenate(
            [
                image_rows,
                jnp.zeros((1, wide), f32),
                widen(bias_sums[: 2 * CB]),
                widen(bias_sums[2 * CB :]),
                jnp.zeros((8 - I - 3, wide), f32),
            ],
            axis=0,
        )
        grad_one = jnp.stack([m["grad_one"] for m in mids]).reshape(I, NX, 2, CB, T)
        grad_mid = jnp.stack([m["grad_mid"] for m in mids]).reshape(I, NX, 2, CB, T)
        grad_input, late, grad_qkv, grad_out, lasts, cond_sum, _ = bwd_call(
            NT,
            NP,
            head_gate.reshape(-1),
            grad_one,
            grad_mid[:, :, 0].astype(bf16),
            grad_mid[:, 0, 0],
            qkv_all,
            mixed_all,
            lse_all,
            concat_all,
            attn_all,
            rows_all,
            stats_all,
            columns[:CB, : I * 6].reshape(CB, I, 6)[:, :, 1].T[:, :, None],
            early_full,
            late_grads,
            base,
            pad8(head_factor, 128),
            ada,
        )
        grad_up, grad_down = late[0], late[1]
        mods_all = (
            lasts[:, :I, : 6 * ML].reshape(NT * I, 6, ML)[:, :, :CB].reshape(NT * I, 6 * CB)
        )
        logits_all = lasts[:, :I, 6 * ML : 6 * ML + HL + GL].reshape(NT * I, HL + GL)
        bias_rows = jnp.sum(lasts[:, I : I + 3], axis=0)
        qv_rows = bias_rows[0, :QKV].reshape(3, HL, HP)[:, :, :HD].reshape(3, HL * HD)
        cond_f = cond_all[:, :I, :RB].reshape(NT * I, RB)
        time_f = cond_all[:, :I, 256 : 256 + FR].reshape(NT * I, FR)
        grad_w_ada = lax.dot_general(
            cond_f, mods_all, (((0,), (0,)), ((), ())), precision=exact_mode
        ).reshape(RB, 6, CB)
        grad_b_ada = jnp.sum(mods_all, axis=0).reshape(6, CB)
        grad_w_gates = lax.dot_general(
            time_f, logits_all, (((0,), (0,)), ((), ())), precision=exact_mode
        )
        grad_b_gates = jnp.sum(logits_all, axis=0)
        cond_total = cond_sum[:, :I, :RB].transpose(1, 0, 2).reshape(I, D)
        grad_condition = jax.vjp(jax.nn.silu, cond_wide)[1](cond_total)[0]

        return (
            block_output,
            grad_input,
            grad_condition,
            grad_w_ada,
            grad_b_ada,
            grad_qkv.reshape(RB, 3, HL, HP)[..., :HD].reshape(RB, 3, HL * HD),
            jnp.stack([qv_rows[0], qv_rows[2]]),
            grad_out.reshape(RB, HL, HP)[..., :HD].reshape(RB, HL * HD).T,
            bias_rows[1, :CB],
            grad_up,
            bias_rows[2, :FL],
            grad_down.T,
            bias_rows[1, CB : 2 * CB],
            grad_w_gates[:, :HL],
            grad_b_gates[:HL],
            grad_w_gates[:, HL:],
            grad_b_gates[HL:],
        )

    return body


def solution(mesh):
    return jax.shard_map(
        make_body(mesh.shape["tok"], mesh.shape["tp"]),
        mesh=mesh,
        in_specs=(
            P("tok", "tp", None),
            P("tok", None),
            P("tok"),
            P("tok", "tp"),
            P("tok", "tp"),
            P("tok", None, "tp"),
            P(None, "tp"),
            P("tok", None, "tp"),
            P(None, "tp"),
            P("tp", "tok"),
            P("tp"),
            P("tok", "tp"),
            P("tp"),
            P("tp", "tok"),
            P("tp"),
            P("tok", "tp"),
            P("tp"),
            P("tok", "tp"),
            P("tp"),
            P("tok", "tp", None),
        ),
        out_specs=(
            P("tok", "tp", None),
            P("tok", "tp", None),
            P("tok", None),
            P("tok", None, "tp"),
            P(None, "tp"),
            P("tok", None, "tp"),
            P(None, "tp"),
            P("tp", "tok"),
            P("tp"),
            P("tok", "tp"),
            P("tp"),
            P("tp", "tok"),
            P("tp"),
            P("tok", "tp"),
            P("tp"),
            P("tok", "tp"),
            P("tp"),
        ),
        check_vma=False,
    )
```

```python
import functools
import math

import jax
import jax.numpy as jnp
from jax import lax
from jax.experimental import pallas as pl
from jax.experimental.pallas import tpu as pltpu
from jax.sharding import PartitionSpec as P

D = 1152
HD = 72
HP = 80
FF = 4608
FREQ = 256
GROUPS = 16
GW = FF // GROUPS
LEN = 1024
EPS = 1e-06
SCALE = HD**-0.5
SCALE2 = SCALE / math.log(2.0)

f32 = jnp.float32
bf16 = jnp.bfloat16
exact_mode = lax.Precision.HIGHEST


def dot(a, b, ca, cb):
    return lax.dot_general(a, b, (((ca,), (cb,)), ((), ())), preferred_element_type=f32)


def embed_time(timesteps):
    half_width = FREQ // 2
    indices = jnp.arange(half_width, dtype=f32)
    freq_rates = jnp.exp(-math.log(10000.0) * indices / half_width)
    angles = timesteps.astype(f32)[:, None] * freq_rates[None, :]
    return jnp.concatenate([jnp.cos(angles), jnp.sin(angles)], axis=1)


MESH = pl.DeviceIdType.MESH
ML = 384


def xor(v, k):
    out, bit = 0, 1
    while bit <= k or bit <= 8:
        b = (v // bit) % 2
        out = out + bit * (1 - b if k & bit else b)
        bit *= 2
    return out


class Ring:
    def __init__(self, NT):
        self.NT, self.tall = NT, NT // 2

    def place(self, t):
        b = t % 2
        return (1 - b) * (self.tall - 1 - t // 2) + b * (self.tall + t // 2)

    def tok(self, q):
        q = (q + 2 * self.NT) % self.NT
        b = q // self.tall
        return (1 - b) * 2 * (self.tall - 1 - q) + b * (2 * (q - self.tall) + 1)


def copy_to(src, dst, send, recv, device):
    return pltpu.make_async_remote_copy(
        src_ref=src, dst_ref=dst, send_sem=send, recv_sem=recv, device_id=device, device_id_type=MESH
    )


def greet(t, p, NT, NP):
    barrier = pltpu.get_barrier_semaphore()
    for r in range(1, NP):
        pl.semaphore_signal(barrier, inc=1, device_id=(t, xor(p, r)), device_id_type=MESH)
    for k in range(1, NT):
        pl.semaphore_signal(barrier, inc=1, device_id=((t + k) % NT, p), device_id_type=MESH)
    pl.semaphore_wait(barrier, NP - 1 + NT - 1)


class ImageMoves:
    def __init__(self, NP, x_ref, rows_ref, x_send, x_recv, c_send, c_recv, local_sem):
        self.NX = NP // 2
        self.T = x_ref.shape[2] // self.NX
        self.refs = (x_ref, rows_ref)
        self.sems = (x_send, x_recv, c_send, c_recv, local_sem)
        self.t, self.p = lax.axis_index("tok"), lax.axis_index("tp")
        self.core = (self.t, xor(self.p, 1))

    def tokens(self, who, j):
        return pl.ds(pl.multiple_of(xor(who, j) * self.T, self.T), self.T)

    def src(self, i, j):
        return self.refs[0].at[i, :, pl.ds(j * self.T, self.T)]

    def x(self, i, k, j):
        x_send, x_recv = self.sems[:2]
        at = self.tokens(xor(self.p // 2, k), j)
        dst = self.refs[1].at[i, 2 * k, :, at]
        device = (self.t, xor(self.p, 2 * k))
        return copy_to(self.src(i, j), dst, x_send.at[i, k, j], x_recv.at[i, k, j], device)

    def own(self, i, j):
        dst = self.refs[1].at[i, 0, :, self.tokens(self.p // 2, j)]
        return pltpu.make_async_copy(self.src(i, j), dst, self.sems[4].at[i, j])

    def own_core(self, i, j):
        dst = self.refs[1].at[i, 1, :, self.tokens(self.p // 2, j)]
        c_send, c_recv = self.sems[2:4]
        return copy_to(self.src(i, j), dst, c_send.at[i, 0, j], c_recv.at[i, 0, j], self.core)

    def passed(self, i, k):
        rows = self.refs[1]
        c_send, c_recv = self.sems[2:4]
        return copy_to(
            rows.at[i, 2 * k], rows.at[i, 2 * k + 1], c_send.at[i, k, 0], c_recv.at[i, k, 0], self.core
        )

    def start(self, i):
        for k in range(1, self.NX):
            for j in range(self.NX):
                self.x(i, k, j).start()
        for j in range(self.NX):
            self.own(i, j).start()
            self.own_core(i, j).start()

    def land(self, i):
        for k in range(1, self.NX):
            for j in range(self.NX):
                self.x(i, k, j).wait_recv()
            self.passed(i, k).start()

    def finish(self, i):
        for j in range(self.NX):
            self.own(i, j).wait()
            self.own_core(i, j).wait_recv()
        for k in range(1, self.NX):
            self.passed(i, k).wait_recv()

    def left(self, i):
        for j in range(self.NX):
            self.own_core(i, j).wait_send()
        for k in range(1, self.NX):
            self.passed(i, k).wait_send()
            for j in range(self.NX):
                self.x(i, k, j).wait_send()


def start_kernel(
    NT, NP, x_ref, w_ref, msg_ref, ada_ref, gates_ref, bias_ref, mask_ref,
    rows_ref, full_ref, mods_ref, sig_ref, cond_ref,
    part_ref, got_ref, x_send, x_recv, c_send, c_recv, r_send, r_recv, s_send, s_recv, local_sem,
):
    NX, SUB = NP // 2, NT // NP
    WN = w_ref.shape[1]
    half = WN // 256 * 128
    t, p = lax.axis_index("tok"), lax.axis_index("tp")
    ring = Ring(NT)
    q = ring.place(t)
    right, left = (ring.tok(q + 1), p), (ring.tok(q - 1), p)

    def where(tt):
        out = 0
        for r in range(NP):
            out = out + jnp.where(p == r, xor(tt // SUB, r), 0)
        return out * SUB + tt % SUB

    greet(t, p, NT, NP)

    small = []
    for k in range(1, NT):
        peer = (t + k) % NT
        small.append(copy_to(msg_ref.at[peer], cond_ref.at[k], s_send.at[0, k], s_recv.at[0, k], (peer, p)))
        small[-1].start()

    def hop(d, to_right):
        side = 0 if to_right else 1
        block = where(ring.tok(q - (d - 1) if to_right else q + (d - 1)))
        src = w_ref if d == 1 else full_ref.at[block]
        dst = full_ref.at[block]
        if d == NT // 2:
            cols = pl.ds(0, half) if to_right else pl.ds(half, WN - half)
            src, dst = src.at[:, cols], dst.at[:, cols]
        return copy_to(src, dst, r_send.at[side, d], r_recv.at[side, d], right if to_right else left)

    hops = {}

    def start_hop(d):
        for to_right in (True, False):
            hops[d, to_right] = hop(d, to_right)
            hops[d, to_right].start()

    def land_hop(d):
        for to_right in (True, False):
            hops[d, to_right].wait_recv()

    images = ImageMoves(NP, x_ref, rows_ref, x_send, x_recv, c_send, c_recv, local_sem)
    images.start(0)
    start_hop(1)
    keep = pltpu.make_async_copy(w_ref, full_ref.at[where(t)], local_sem.at[1, 0])
    keep.start()

    cond_ref[0] = msg_ref[t]
    for cp in small:
        cp.wait_recv()
    rb, fr = ada_ref.shape[1], gates_ref.shape[0]
    feats = cond_ref[...].reshape(NT * 8, -1).astype(bf16)
    for k in range(6):
        part = jnp.dot(feats[:, :rb], ada_ref[k], preferred_element_type=f32)
        part_ref[:, :, k * ML : (k + 1) * ML] = part.reshape(NT, 8, ML)
    part = jnp.dot(feats[:, 256 : 256 + fr], gates_ref[...], preferred_element_type=f32)
    part_ref[:, :, 6 * ML :] = part.reshape(NT, 8, 128)
    for k in range(1, NT):
        peer = (t + NT - k) % NT
        cp = copy_to(part_ref.at[k], got_ref.at[k], s_send.at[1, k], s_recv.at[1, k], (peer, p))
        cp.start()
        small.append(cp)
    land_hop(1)
    start_hop(2)
    for cp in small[NT - 1 :]:
        cp.wait_recv()
    total = part_ref[0]
    for k in range(1, NT):
        total = total + got_ref[k]
    total = total + bias_ref[...]
    sig = 1.0 / (1.0 + jnp.exp(-total[:, 6 * ML :]))
    sig_ref[...] = sig
    mods_ref[0, :, : 6 * ML] = total[:, : 6 * ML]
    mods_ref[0, :, 6 * ML :] = sig * mask_ref[...]
    mods = []
    for r in range(1, NP):
        cp = copy_to(mods_ref.at[0], mods_ref.at[r], s_send.at[2, r], s_recv.at[2, r], (t, xor(p, r)))
        cp.start()
        mods.append(cp)

    images.land(0)
    for d in range(2, NT // 2 + 1):
        land_hop(d)
        if d < NT // 2:
            start_hop(d + 1)
    images.finish(0)
    for cp in mods:
        cp.wait_recv()
    keep.wait()
    images.left(0)
    for cp in small + mods + list(hops.values()):
        cp.wait_send()


def start_call(NT, NP, x, w, msg, ada, gates, bias, mask):
    _, CB, length = x.shape
    NX = NP // 2
    RB, WN = w.shape
    wide = 6 * ML + 128
    hbm, vmem = pl.BlockSpec(memory_space=pl.ANY), pl.BlockSpec(memory_space=pltpu.VMEM)
    dma = pltpu.SemaphoreType.DMA
    return pl.pallas_call(
        functools.partial(start_kernel, NT, NP),
        in_specs=[pl.BlockSpec((1, CB, length), lambda i: (0, 0, 0))] + [vmem] * 6,
        grid=(1,),
        out_specs=[hbm, hbm, vmem, vmem, vmem],
        out_shape=[
            jax.ShapeDtypeStruct((1, NP, CB, length), bf16),
            jax.ShapeDtypeStruct((NT, RB, WN), bf16),
            jax.ShapeDtypeStruct((NP, 8, wide), f32),
            jax.ShapeDtypeStruct((8, 128), f32),
            jax.ShapeDtypeStruct((NT, 8, ML), f32),
        ],
        scratch_shapes=[
            pltpu.VMEM((NT, 8, wide), f32),
            pltpu.VMEM((NT, 8, wide), f32),
            dma((1, NX, NX)),
            dma((1, NX, NX)),
            dma((1, NX, NX)),
            dma((1, NX, NX)),
            dma((2, NT // 2 + 1)),
            dma((2, NT // 2 + 1)),
            dma((3, max(NT, NP))),
            dma((3, max(NT, NP))),
            dma((2, NX)),
        ],
        compiler_params=pltpu.CompilerParams(
            collective_id=0, has_side_effects=True, vmem_limit_bytes=32 * 2**20
        ),
        name="start",
    )(x, w, msg, ada, gates, bias, mask)


def spread(mods_ref, r, rows, CB):
    parts = [mods_ref[r, row, at : at + ML] for row, at in rows]
    parts += [jnp.zeros((8 - len(parts), ML), f32)] if len(parts) < 8 else []
    return jnp.concatenate(parts, axis=0).T[:CB]


def fwd_kernel(
    NT, NP, gate_ref, x_ref, cot_ref, first_ref, w_ref, mod_ref, bias_ref, late_ref,
    attn_ref, qkv_ref, mixed_ref, concat_ref, lse_ref, stats_ref, branch_ref, full_ref, rows_ref, cots_ref,
    wt_ref, own_ref, core_out, core_in, x_out, x_in, total_ref,
    mcol_ref, l_send, l_recv, c_send, c_recv, x_send, x_recv, b_send, b_recv, local_sem,
    rows_buf, rx_send, rx_recv, rc_send, rc_recv, r_sem, t_send, t_recv, t_sem,
):
    NX, SUB = NP // 2, NT // NP
    I, CB, T = total_ref.shape[0], total_ref.shape[2], total_ref.shape[3]
    HL = gate_ref.shape[0] // I
    QKV = 3 * HL * HP
    steps = HL + 2
    i, s = pl.program_id(0), pl.program_id(1)
    flat = i * steps + s
    t, p = lax.axis_index("tok"), lax.axis_index("tp")
    ring = Ring(NT)
    q = ring.place(t)
    right, left = (ring.tok(q + 1), p), (ring.tok(q - 1), p)
    core = (t, xor(p, 1))

    def at(n):
        return pl.when(flat == n)

    images = ImageMoves(NP, x_ref, rows_ref, rx_send, rx_recv, rc_send, rc_recv, r_sem)

    def first_keep():
        return pltpu.make_async_copy(rows_buf, rows_ref.at[0], r_sem.at[0, 0])

    def load_rows(n):
        if n:
            images.finish(n)
        if n == 1:
            first_keep().wait()
        src = rows_ref.at[n] if n else first_ref.at[0]
        cp = pltpu.make_async_copy(src, rows_buf, r_sem.at[I, 0])
        cp.start()
        cp.wait()
        if n == 0:
            first_keep().start()

    def cot_x(n, k):
        src = cot_ref.at[n, :, images.tokens(xor(p // 2, k), 0)]
        return copy_to(
            src, cots_ref.at[n, k, 0], t_send.at[0, n, k], t_recv.at[0, n, k], (t, xor(p, 2 * k))
        )

    def cot_keep(n):
        src = cot_ref.at[n, :, images.tokens(p // 2, 0)]
        return pltpu.make_async_copy(src, cots_ref.at[n, 0, 0], t_sem.at[n])

    def cot_core(n, k):
        src = cots_ref.at[n, k, 0] if k else cot_ref.at[n, :, images.tokens(p // 2, 0)]
        return copy_to(src, cots_ref.at[n, k, 1], t_send.at[1, n, k], t_recv.at[1, n, k], core)

    def start_cot():
        for n in range(I):
            for k in range(1, NX):
                cot_x(n, k).start()

    def land_cot():
        for n in range(I):
            for k in range(1, NX):
                cot_x(n, k).wait_recv()
                cot_core(n, k).start()

    def where(tt):
        out = 0
        for r in range(NP):
            out = out + jnp.where(p == r, xor(tt // SUB, r), 0)
        return out * SUB + tt % SUB

    def hop(k, d, side):
        block = where(ring.tok(q - (d - 1) if side == 0 else q + (d - 1)))
        dst = full_ref.at[k, :, block]
        src = late_ref.at[k] if d == 1 else dst
        if d == NT // 2:
            src, dst = src.at[side], dst.at[side]
        return copy_to(src, dst, l_send.at[k, side, d], l_recv.at[k, side, d], left if side else right)

    def keep(k):
        return pltpu.make_async_copy(late_ref.at[k], full_ref.at[k, :, where(t)], local_sem.at[k])

    def start_hop(k, d):
        for side in range(2):
            hop(k, d, side).start()

    def land_hop(k, d):
        for side in range(2):
            hop(k, d, side).wait_recv()
        if d < NT // 2:
            start_hop(k, d + 1)

    def core_copy(i):
        return copy_to(core_out.at[i], core_in.at[i], c_send.at[i], c_recv.at[i], core)

    def x_copy(i, k):
        return copy_to(
            x_out.at[i, k], x_in.at[i, k], x_send.at[i, k], x_recv.at[i, k], (t, xor(p, 2 * k))
        )

    def back_copy(i):
        return copy_to(total_ref.at[i], branch_ref.at[i, 1], b_send.at[i], b_recv.at[i], core)

    def back_keep(i):
        return pltpu.make_async_copy(total_ref.at[i], branch_ref.at[i, 0], local_sem.at[NX + i])

    def add_core(i):
        core_copy(i).wait_recv()
        for f in range(NX):
            for k in range(NX):
                cols = slice(k * T, (k + 1) * T)
                v = own_ref[f, :, cols] + core_in[i, f, :, cols].astype(f32)
                if k == 0:
                    total_ref[i, f] = v
                else:
                    x_out[i, k, f] = v.astype(bf16)
        for k in range(1, NX):
            x_copy(i, k).start()

    def add_x(i):
        for k in range(1, NX):
            x_copy(i, k).wait_recv()
        for f in range(NX):
            v = total_ref[i, f]
            for k in range(1, NX):
                v = v + x_in[i, k, f ^ k].astype(f32)
            total_ref[i, f] = v
        back_copy(i).start()
        back_keep(i).start()

    @at(0)
    def _():
        barrier = pltpu.get_barrier_semaphore()
        peers = [right, left, core] + [(t, xor(p, 2 * k)) for k in range(1, NX)]
        for peer in peers:
            pl.semaphore_signal(barrier, inc=1, device_id=peer, device_id_type=MESH)
        pl.semaphore_wait(barrier, len(peers))
        if I > 1:
            images.start(1)
        for k in range(NX):
            start_hop(k, 1)
        for n in range(I):
            cot_keep(n).start()
            cot_core(n, 0).start()
        for k in range(NX):
            keep(k).start()
        wt_ref[...] = w_ref[:, :QKV].T

    for n in range(I):
        if n:

            @at((n - 1) * steps + HL)
            def _(n=n):
                images.land(n)
                if n + 1 < I:
                    images.start(n + 1)
                else:
                    start_cot()

        at(n * steps)(functools.partial(load_rows, n))

    @pl.when(s == 0)
    def _():
        for r in range(NP):
            rows = [(pl.ds(i, 1), 0), (pl.ds(i, 1), ML)]
            mcol_ref[r * CB : (r + 1) * CB] = spread(mod_ref, r, rows, CB)
        width = 256
        for j in range(LEN // width):
            cols = slice(j * width, (j + 1) * width)
            v = rows_buf[:, :, cols].reshape(D, width).astype(f32)
            centre = jnp.sum(v, axis=0, keepdims=True) * (1.0 / D)
            square = jnp.sum(v * v, axis=0, keepdims=True) * (1.0 / D)
            inverse = lax.rsqrt(square - centre * centre + EPS)
            stats_ref[0, 0:1, cols] = centre
            stats_ref[0, 1:2, cols] = inverse
            n = (v - centre) * inverse
            a = (n * (1.0 + mcol_ref[:, 1:2]) + mcol_ref[:, 0:1]).astype(bf16)
            attn_ref[0, :, cols] = a
            out = jnp.dot(wt_ref[...], a, preferred_element_type=f32) + bias_ref[...]
            qkv_ref[0, :, cols] = out.astype(bf16)

    @pl.when((s > 0) & (s <= HL))
    def _():
        h = s - 1
        gate = gate_ref[i * HL + h]

        def head(k):
            return pl.ds(pl.multiple_of((k * HL + h) * HP, HP), HP)

        keys = qkv_ref[0, head(1)].T
        sc = jnp.dot(keys, qkv_ref[0, head(0)], preferred_element_type=f32)
        top = jnp.max(sc, axis=0, keepdims=True)
        pr = jnp.exp2((sc - top) * SCALE2).astype(bf16)
        out = jnp.dot(qkv_ref[0, head(2)], pr, preferred_element_type=f32)
        total = out[HD : HD + 1]
        mixed = out * (1.0 / total)
        mixed_ref[0, head(0)] = mixed
        concat_ref[0, head(0)] = (mixed * gate).astype(bf16)
        lse_ref[0, pl.ds(h, 1)] = top * SCALE2 + jnp.log2(total)

    @pl.when(s == HL + 1)
    def _():
        for r in range(NP):
            w = w_ref[r * CB : (r + 1) * CB, w_ref.shape[1] - HL * HP :]
            part = jnp.dot(w, concat_ref[0], preferred_element_type=f32)
            if r % 2 == 0:
                own_ref[r // 2] = part
            else:
                core_out[i, r // 2] = part.astype(bf16)
        core_copy(i).start()

    for n in range(I - 1):
        at((n + 1) * steps + 1)(functools.partial(add_core, n))
        at((n + 1) * steps + HL)(functools.partial(add_x, n))

    events = [(k, d) for d in range(1, NT // 2 + 1) for k in range(NX)]
    early = [steps + HL, 2 * steps - 1][: len(events)] if I > 1 else []
    for n, (k, d) in zip(early, events):
        at(n)(functools.partial(land_hop, k, d))

    @at(I * steps - 1)
    def _():
        if I == 1:
            start_cot()
        add_core(I - 1)
        land_cot()
        rest = events[len(early) :]
        for n, (k, d) in enumerate(rest):
            land_hop(k, d)
            if n == 0:
                add_x(I - 1)
        for n in range(I):
            back_copy(n).wait_recv()
        if I == 1:
            first_keep().wait()
        for n in range(I):
            if n:
                images.left(n)
            cot_keep(n).wait()
            for k in range(NX):
                cot_core(n, k).wait_recv()
                cot_core(n, k).wait_send()
                if k:
                    cot_x(n, k).wait_send()
        for n in range(I):
            core_copy(n).wait_send()
            back_copy(n).wait_send()
            back_keep(n).wait()
            for k in range(1, NX):
                x_copy(n, k).wait_send()
        for k in range(NX):
            keep(k).wait()
            for d in range(1, NT // 2 + 1):
                for side in range(2):
                    hop(k, d, side).wait_send()


def fwd_call(NT, NP, gate, x, cot, first, w, mods, bias, late):
    I, _, length = x.shape
    NX = NP // 2
    CB, T = D // NP, length // NX
    HL = gate.shape[0] // I
    QKV = 3 * HL * HP
    RB, FL = late.shape[2:]
    hbm = pl.BlockSpec(memory_space=pl.ANY)
    vmem = pl.BlockSpec(memory_space=pltpu.VMEM)
    dma = pltpu.SemaphoreType.DMA

    def image(*shape):
        return pl.BlockSpec((1,) + shape, lambda i, s: (i,) + (0,) * len(shape))

    return pl.pallas_call(
        functools.partial(fwd_kernel, NT, NP),
        grid=(I, HL + 2),
        in_specs=[
            pl.BlockSpec(memory_space=pltpu.SMEM),
            vmem,
            vmem,
            hbm,
            vmem,
            vmem,
            vmem,
            vmem,
        ],
        out_specs=[
            image(D, length),
            image(QKV, length),
            image(HL * HP, length),
            image(HL * HP, length),
            image(HL, length),
            image(8, length),
            hbm,
            hbm,
            hbm,
            hbm,
        ],
        out_shape=[
            jax.ShapeDtypeStruct((I, D, length), bf16),
            jax.ShapeDtypeStruct((I, QKV, length), bf16),
            jax.ShapeDtypeStruct((I, HL * HP, length), f32),
            jax.ShapeDtypeStruct((I, HL * HP, length), bf16),
            jax.ShapeDtypeStruct((I, HL, length), f32),
            jax.ShapeDtypeStruct((I, 8, length), f32),
            jax.ShapeDtypeStruct((I, 2, NX, CB, T), f32),
            jax.ShapeDtypeStruct((NX, 2, NT, RB, FL), bf16),
            jax.ShapeDtypeStruct((I, NP, CB, length), bf16),
            jax.ShapeDtypeStruct((I, NX, 2, CB, T), bf16),
        ],
        scratch_shapes=[
            pltpu.VMEM((QKV, D), bf16),
            pltpu.VMEM((NX, CB, length), f32),
            pltpu.VMEM((I, NX, CB, length), bf16),
            pltpu.VMEM((I, NX, CB, length), bf16),
            pltpu.VMEM((I, NX, NX, CB, T), bf16),
            pltpu.VMEM((I, NX, NX, CB, T), bf16),
            pltpu.VMEM((I, NX, CB, T), f32),
            pltpu.VMEM((D, 8), f32),
            dma((NX, 2, NT // 2 + 1)),
            dma((NX, 2, NT // 2 + 1)),
            dma((I,)),
            dma((I,)),
            dma((I, NX)),
            dma((I, NX)),
            dma((I,)),
            dma((I,)),
            dma((NX + I,)),
            pltpu.VMEM((NP, CB, length), bf16),
            dma((I, NX, NX)),
            dma((I, NX, NX)),
            dma((I, NX, NX)),
            dma((I, NX, NX)),
            dma((I + 1, NX)),
            dma((2, I, NX)),
            dma((2, I, NX)),
            dma((I,)),
        ],
        compiler_params=pltpu.CompilerParams(
            collective_id=2, has_side_effects=True, vmem_limit_bytes=60 * 2**20
        ),
        name="forward",
    )(gate, x, cot, first, w, mods, bias, late)


def lane_sum(v):
    total = v[:, :128]
    for j in range(1, v.shape[1] // 128):
        total = total + v[:, j * 128 : (j + 1) * 128]
    return jnp.sum(total.T, axis=0, keepdims=True)


def mlp_kernel(
    NT, NP, branch_ref, rows_ref, cot_ref, mods_ref, gate_ref, w_ref,
    lhs_ref, rhs_ref, go_ref, gms_ref, gm_ref, sums_ref, fsums_ref, out_ref, go0_ref,
    mid_ref, gn_ref, b2_ref, st_ref, gn_out, gn_in, b2_out, b2_in, o_buf,
    mcol_ref, g_send, g_recv, b_send, b_recv, x_send, x_recv, local_sem, go_buf, f_send, f_recv,
):
    NX = NP // 2
    _, _, D_, T = lhs_ref.shape
    CB = D // NP
    I = pl.num_programs(0)
    FL = w_ref.shape[3]
    i = pl.program_id(0)
    slot = i % 2
    t, p = lax.axis_index("tok"), lax.axis_index("tp")
    xi = p // 2
    core = (t, xor(p, 1))

    def gn_copy(n):
        return copy_to(gn_out, gn_in.at[n % 2], g_send.at[n], g_recv.at[n], core)

    def b2_copy(n):
        return copy_to(b2_out, b2_in.at[n % 2], b_send.at[n], b_recv.at[n], core)

    def place(n):
        return out_ref.at[n, :, pl.ds(pl.multiple_of(xi * T, T), T)]

    def out_copy(n, k):
        return copy_to(
            o_buf.at[n % 2, k], place(n), x_send.at[n, k], x_recv.at[n, k], (t, xor(p, 2 * k))
        )

    def out_keep(n):
        return pltpu.make_async_copy(o_buf.at[n % 2, 0], place(n), local_sem.at[n])

    def out_left(n):
        out_keep(n).wait()
        for k in range(1, NX):
            out_copy(n, k).wait_send()

    def go_x(k, f):
        return copy_to(
            go_buf.at[f], go0_ref.at[k, f ^ k, 0], f_send.at[0, k, f], f_recv.at[0, k, f],
            (t, xor(p, 2 * k)),
        )

    def go_core(k, f):
        return copy_to(
            go0_ref.at[k, f, 0], go0_ref.at[k, f, 1], f_send.at[1, k, f], f_recv.at[1, k, f], core
        )

    @pl.when(i == 0)
    def _():
        barrier = pltpu.get_barrier_semaphore()
        peers = [core] + [(t, xor(p, 2 * k)) for k in range(1, NX)]
        for peer in peers:
            pl.semaphore_signal(barrier, inc=1, device_id=peer, device_id_type=MESH)
        pl.semaphore_wait(barrier, len(peers))

    count = out_ref.shape[0]
    for r in range(NP):
        rows = [(pl.ds(i, 1), k * ML) for k in range(6)]
        rows += [(slice(count, count + 1), 0), (slice(count, count + 1), ML)]
        mcol_ref[r * CB : (r + 1) * CB] = spread(mods_ref, r, rows, CB)

    def col(k):
        return mcol_ref[:, k : k + 1]

    width = min(256, T)
    chunks = [slice(j * width, (j + 1) * width) for j in range(T // width)]

    def branch_one(cols):
        parts = [branch_ref[0, r % 2, r // 2, :, cols] for r in range(NP)]
        return jnp.concatenate(parts, axis=0) + col(6)

    for cols in chunks:
        x = jnp.concatenate([rows_ref[0, r, :, cols] for r in range(NP)], axis=0).astype(f32)
        mid = x + col(2) * branch_one(cols)
        mid_ref[:, cols] = mid
        centre = jnp.sum(mid, axis=0, keepdims=True) * (1.0 / D)
        square = jnp.sum(mid * mid, axis=0, keepdims=True) * (1.0 / D)
        inverse = lax.rsqrt(square - centre * centre + EPS)
        st_ref[0:1, cols] = centre
        st_ref[1:2, cols] = inverse
        n = (mid - centre) * inverse
        lhs_ref[0, 0, :, cols] = (n * (1.0 + col(4)) + col(3)).astype(bf16)
        lhs_ref[0, 1, :, cols] = (col(5) * cot_ref[0, :, cols].astype(f32)).astype(bf16)

    root = math.sqrt(2.0 / math.pi)
    tile = 384
    for k in range(NX):
        for at in range(0, FL, tile):
            rows = slice(at, min(at + tile, FL))
            size = rows.stop - rows.start
            vec = [gate_ref[k, pl.ds(i, 1), rows], mods_ref[2 * k, count + 1 : count + 2, rows]]
            vec = jnp.concatenate(vec + [jnp.zeros((6, size), f32)], axis=0).T
            pre = dot(w_ref[k, 0, :, rows], lhs_ref[0, 0], 0, 0) + vec[:, 1:2]
            grad_hid = dot(w_ref[k, 1, :, rows], lhs_ref[0, 1], 0, 0)
            gate = vec[:, 0:1]
            square = pre * pre
            inner = jnp.tanh(pre * (root + (root * 0.044715) * square))
            half = 0.5 * (1.0 + inner)
            act = pre * half
            slope = half + (0.5 * pre) * (1.0 - inner * inner) * (root + (3.0 * root * 0.044715) * square)
            rhs_ref[0, 1, k, rows] = (act * gate).astype(bf16)
            grad_pre = (slope * gate * grad_hid).astype(bf16)
            rhs_ref[0, 0, k, rows] = grad_pre
            to = slice(k * FL + rows.start, k * FL + rows.stop)
            fsums_ref[0, 0:1, to] = lane_sum(grad_pre.astype(f32))
            fsums_ref[0, 1:2, to] = lane_sum(grad_hid * act)

    def product(u, r):
        total = 0.0
        for k in range(NX):
            w = w_ref[k, u, r * CB : (r + 1) * CB]
            total = total + jnp.dot(w, rhs_ref[0, u, k], preferred_element_type=f32)
        return total

    for r in range(NP):
        v = product(0, r)
        gn_ref[r * CB : (r + 1) * CB] = v
        gn_out[r * CB : (r + 1) * CB] = v.astype(bf16)
    gn_copy(i).start()
    for r in range(NP):
        v = product(1, r)
        if r % 2:
            b2_out[r // 2] = v.astype(bf16)
        else:
            b2_ref[r // 2] = v
    b2_copy(i).start()

    gn_copy(i).wait_recv()
    gn_copy(i).wait_send()
    for r in range(NP):
        mine, theirs = slice(r * CB, (r + 1) * CB), slice((r ^ 1) * CB, ((r ^ 1) + 1) * CB)
        gn_ref[mine] = gn_ref[mine] + gn_in[slot, theirs].astype(f32)
    totals = [0.0] * 5

    def fold(v):
        total = v[:, :128]
        for j in range(1, v.shape[1] // 128):
            total = total + v[:, j * 128 : (j + 1) * 128]
        return total

    for cols in chunks:
        gnorm = gn_ref[:, cols]
        inverse = st_ref[1:2, cols]
        n = (mid_ref[:, cols] - st_ref[0:1, cols]) * inverse
        g = gnorm * (1.0 + col(4))
        mean_g = jnp.sum(g, axis=0, keepdims=True) * (1.0 / D)
        mean_gn = jnp.sum(g * n, axis=0, keepdims=True) * (1.0 / D)
        grad_mid = cot_ref[0, :, cols].astype(f32) + inverse * (g - mean_g - n * mean_gn)
        grad_one = (col(2) * grad_mid).astype(bf16)
        go_ref[0, :, cols] = grad_one
        gm_ref[0, :, cols] = grad_mid[:CB]
        for k in range(NX):
            gms_ref[0, k, :, cols] = grad_mid[2 * k * CB : (2 * k + 1) * CB].astype(bf16)
        terms = (
            grad_mid * branch_one(cols),
            gnorm,
            gnorm * n,
            grad_one.astype(f32),
            lhs_ref[0, 1, :, cols].astype(f32),
        )
        totals = [a + fold(b) for a, b in zip(totals, terms)]
    @pl.when(i == 0)
    def _():
        for f in range(NX):
            go_buf[f] = go_ref[0, 2 * f * CB : (2 * f + 1) * CB]
        for k in range(1, NX):
            for f in range(NX):
                go_x(k, f).start()

    for row, v in enumerate(totals):
        sums_ref[0, row : row + 1, :] = jnp.sum(v.T, axis=0, keepdims=True)

    @pl.when(i >= 2)
    def _():
        out_left(i - 2)

    b2_copy(i).wait_recv()
    b2_copy(i).wait_send()
    for f in range(NX):
        rows = slice(2 * f * CB, (2 * f + 1) * CB)
        v = b2_ref[f] + b2_in[slot, f].astype(f32) + mcol_ref[rows, 7:8]
        sums_ref[0, 5 : 6, f * CB : (f + 1) * CB] = lane_sum(cot_ref[0, rows].astype(f32) * v)
        o_buf[slot, f] = (mid_ref[rows] + mcol_ref[rows, 5:6] * v).astype(bf16)
    out_keep(i).start()
    for k in range(1, NX):
        out_copy(i, k).start()

    @pl.when(i == I - 1)
    def _():
        for k in range(1, NX):
            for f in range(NX):
                go_x(k, f ^ k).wait_recv()
                go_core(k, f).start()
        for n in range(x_send.shape[0]):
            for k in range(1, NX):
                out_copy(n, k).wait_recv()
            if n >= x_send.shape[0] - 2:
                out_left(n)
        for k in range(1, NX):
            for f in range(NX):
                go_core(k, f).wait_recv()
                go_core(k, f).wait_send()
                go_x(k, f).wait_send()


def mlp_call(NT, NP, branch, rows, cot, mods, gates, w):
    I, NX = branch.shape[0], NP // 2
    CB, T = branch.shape[3:]
    FL = w.shape[3]
    hbm = pl.BlockSpec(memory_space=pl.ANY)
    vmem = pl.BlockSpec(memory_space=pltpu.VMEM)
    dma = pltpu.SemaphoreType.DMA

    def image(*shape):
        return pl.BlockSpec((1,) + shape, lambda i: (i,) + (0,) * len(shape))

    return pl.pallas_call(
        functools.partial(mlp_kernel, NT, NP),
        grid=(I,),
        in_specs=[
            pl.BlockSpec(
                (1, 2, NX, CB, T), lambda i: (i, 0, 0, 0, 0), pipeline_mode=pl.Buffered(buffer_count=1)
            ),
            image(NP, CB, T),
            image(D, T),
            vmem,
            vmem,
            vmem,
        ],
        out_specs=[
            image(2, D, T),
            image(2, NX, FL, T),
            image(D, T),
            image(NX, CB, T),
            image(CB, T),
            image(8, D),
            image(8, NX * FL),
            hbm,
            hbm,
        ],
        out_shape=[
            jax.ShapeDtypeStruct((I, 2, D, T), bf16),
            jax.ShapeDtypeStruct((I, 2, NX, FL, T), bf16),
            jax.ShapeDtypeStruct((I, D, T), bf16),
            jax.ShapeDtypeStruct((I, NX, CB, T), bf16),
            jax.ShapeDtypeStruct((I, CB, T), f32),
            jax.ShapeDtypeStruct((I, 8, D), f32),
            jax.ShapeDtypeStruct((I, 8, NX * FL), f32),
            jax.ShapeDtypeStruct((I, CB, NX * T), bf16),
            jax.ShapeDtypeStruct((NX, NX, 2, CB, T), bf16),
        ],
        scratch_shapes=[
            pltpu.VMEM((D, T), f32),
            pltpu.VMEM((D, T), f32),
            pltpu.VMEM((NX, CB, T), f32),
            pltpu.VMEM((8, T), f32),
            pltpu.VMEM((D, T), bf16),
            pltpu.VMEM((2, D, T), bf16),
            pltpu.VMEM((NX, CB, T), bf16),
            pltpu.VMEM((2, NX, CB, T), bf16),
            pltpu.VMEM((2, NX, CB, T), bf16),
            pltpu.VMEM((D, 8), f32),
            dma((I,)),
            dma((I,)),
            dma((I,)),
            dma((I,)),
            dma((I, NX)),
            dma((I, NX)),
            dma((I,)),
            pltpu.VMEM((NX, CB, T), bf16),
            dma((2, NX, NX)),
            dma((2, NX, NX)),
        ],
        compiler_params=pltpu.CompilerParams(
            collective_id=3, has_side_effects=True, vmem_limit_bytes=60 * 2**20
        ),
        name="feed_forward",
    )(branch, rows, cot, mods, gates, w)


def grads_kernel(lhs_ref, rhs_ref, out_ref):
    I, _, rows, _ = lhs_ref.shape
    NT, RB = out_ref.shape[2:4]
    for b in range(0, NT, 2):
        total = 0.0
        for i in range(I):
            a = lhs_ref[i, 0, b * RB : (b + 2) * RB]
            total = total + dot(a, rhs_ref[i, 0, 0], 1, 1)
        out_ref[0, 0, b : b + 2] = total.astype(bf16).reshape(2, RB, -1)


def grads_call(NT, lhs, rhs):
    I, _, NX, FL, T = rhs.shape
    RB = D // NT
    return pl.pallas_call(
        grads_kernel,
        grid=(2, NX),
        in_specs=[
            pl.BlockSpec((I, 1, D, T), lambda u, k: (0, u, 0, 0)),
            pl.BlockSpec((I, 1, 1, FL, T), lambda u, k: (0, u, k, 0, 0)),
        ],
        out_specs=pl.BlockSpec((1, 1, NT, RB, FL), lambda u, k: (k, u, 0, 0, 0)),
        out_shape=jax.ShapeDtypeStruct((NX, 2, NT, RB, FL), bf16),
        compiler_params=pltpu.CompilerParams(vmem_limit_bytes=48 * 2**20),
        name="late_grads",
    )(lhs, rhs)


def bwd_kernel(
    NT, NP, gate_ref, go_ref, go0_ref, gms_ref, gm_ref, qkv_ref, mixed_ref, lse_ref, concat_ref, attn_ref,
    rows_ref, stats_ref, scale_ref, w_ref, late_ref, base_ref, factor_ref, ada_ref,
    gin_ref, late_out, gqkv_ref, gout_ref, lasts_ref, cond_ref, gox_ref,
    go_buf, gmx_ref, own_ref, core_out, core_in, x_out, x_in, gn_ref, accq_ref, acco_ref, wt_ref,
    gc_ref, dqkv_ref, rows_buf, gin_buf, st_out, st_in, msg_ref, heads_ref, qv_ref,
    l_own, l_out, l_in, lx_out, lx_in, q_out, q_in, part_ref, sum_ref, lasts_buf,
    g_send, g_recv, c_send, c_recv, x_send, x_recv, t_send, t_recv, l_send, l_recv, lx_send, lx_recv,
    q_send, q_recv, s_send, s_recv, m_send, m_recv, local_sem, own_sem,
):
    NX, SUB = NP // 2, NT // NP
    I, CB, T = gm_ref.shape
    HL = gate_ref.shape[0] // I
    QKV, HO = 3 * HL * HP, HL * HP
    RB = D // NT
    HOPS = NT // 2
    steps = HL + 2
    i, s = pl.program_id(0), pl.program_id(1)
    flat = i * steps + s
    t, p = lax.axis_index("tok"), lax.axis_index("tp")
    xi = p // 2
    ring = Ring(NT)
    q = ring.place(t)
    right, left = (ring.tok(q + 1), p), (ring.tok(q - 1), p)
    core = (t, xor(p, 1))

    def at(n):
        return pl.when(flat == n)

    def partner(k):
        return (t, xor(p, 2 * k))

    def where(tt):
        out = 0
        for r in range(NP):
            out = out + jnp.where(p == r, xor(tt // SUB, r), 0)
        return out * SUB + tt % SUB

    def go_x(n, k, f):
        return copy_to(
            go_ref.at[n, f, 0], gox_ref.at[n, k, f ^ k, 0], g_send.at[0, n, k, f],
            g_recv.at[0, n, k, f], partner(k),
        )

    def go_core(n, k, f):
        return copy_to(
            gox_ref.at[n, k, f, 0], gox_ref.at[n, k, f, 1], g_send.at[1, n, k, f],
            g_recv.at[1, n, k, f], core,
        )

    def gm_x(n, k):
        return copy_to(gms_ref.at[n, k], gmx_ref.at[n, k - 1], m_send.at[n, k], m_recv.at[n, k], partner(k))

    def send_go(n):
        for k in range(1, NX):
            for f in range(NX):
                go_x(n, k, f).start()

    def pass_go(n):
        for k in range(1, NX):
            for f in range(NX):
                go_x(n, k, f ^ k).wait_recv()
                go_core(n, k, f).start()
        if n + 1 < I:
            send_go(n + 1)
        for m in [n - 1] if n + 1 < I else [n - 1, n]:
            if m >= 0:
                for k in range(1, NX):
                    gm_x(m, k).start()

    def load_go(n):
        def load(k):
            src = go_ref.at[n] if k == 0 else gox_ref.at[n, k] if n else go0_ref.at[k]
            return pltpu.make_async_copy(src, go_buf.at[k], local_sem.at[k])

        load(0).start()
        for k in range(1, NX):
            for f in range(NX if n else 0):
                go_core(n, k, f).wait_recv()
            load(k).start()
        for k in range(NX):
            load(k).wait()

    def rows_copy(n):
        return pltpu.make_async_copy(rows_ref.at[n, 0], rows_buf.at[n], local_sem.at[NX + n])

    def core_copy(n):
        return copy_to(core_out, core_in.at[n % 2], c_send.at[n], c_recv.at[n], core)

    def x_copy(n, k):
        return copy_to(
            x_out.at[n % 2, k - 1], x_in.at[n % 2, k - 1], x_send.at[n, k], x_recv.at[n, k], partner(k)
        )

    def st_copy(n, r):
        return copy_to(
            st_out.at[n], st_in.at[n, r], t_send.at[n, r], t_recv.at[n, r], (t, xor(p, r))
        )

    def gin_copy(n, j):
        to = pl.ds(pl.multiple_of(xor(xi, j) * T, T), T)
        return pltpu.make_async_copy(
            gin_buf.at[n % 2, :, pl.ds(j * T, T)], gin_ref.at[n, :, to], local_sem.at[NX + I + n * NX + j]
        )

    def add_core(n):
        core_copy(n).wait_recv()
        if n >= 2:
            for k in range(1, NX):
                x_copy(n - 2, k).wait_send()
        for f in range(NX):
            v = own_ref[f] + core_in[n % 2, f].astype(f32)
            if f == 0:
                gn_ref[...] = v
            else:
                x_out[n % 2, f - 1] = v.astype(bf16)
        for k in range(1, NX):
            x_copy(n, k).start()

    def tokens(v):
        total = v[:, :128]
        for j in range(1, LEN // 128):
            total = total + v[:, j * 128 : (j + 1) * 128]
        return jnp.sum(total.T, axis=0, keepdims=True)

    def own_scale(n):
        return 1.0 + scale_ref[0, :, ML : 2 * ML].T[:CB, n : n + 1]

    def normed(n):
        return (rows_buf[n].astype(f32) - stats_ref[n, 0:1]) * stats_ref[n, 1:2]

    def add_x(n):
        for k in range(1, NX):
            x_copy(n, k).wait_recv()
        for j in range(NX):
            v = gn_ref[:, j * T : (j + 1) * T]
            for k in range(1, NX):
                v = v + x_in[n % 2, k - 1, :, (j ^ k) * T : ((j ^ k) + 1) * T].astype(f32)
            gn_ref[:, j * T : (j + 1) * T] = v
        v = gn_ref[...]
        vn = v * normed(n)
        scale = own_scale(n)
        st_out[n, 0:1] = jnp.sum(v * scale, axis=0, keepdims=True)
        st_out[n, 1:2] = jnp.sum(vn * scale, axis=0, keepdims=True)
        for r in range(1, NP):
            st_copy(n, r).start()
        msg_ref[n : n + 1, :CB] = tokens(v)
        msg_ref[n : n + 1, ML : ML + CB] = tokens(vn)

    def add_stats(n):
        for r in range(1, NP):
            st_copy(n, r).wait_recv()
        if n >= 2:
            for j in range(NX):
                gin_copy(n - 2, j).wait()
        for k in range(1, NX):
            gm_x(n, k).wait_recv()
        for j in range(NX):
            cols = slice(j * T, (j + 1) * T)
            a, b = st_out[n, 0:1, cols], st_out[n, 1:2, cols]
            for r in range(1, NP):
                m = j ^ (r // 2)
                a = a + st_in[n, r, 0:1, m * T : (m + 1) * T]
                b = b + st_in[n, r, 1:2, m * T : (m + 1) * T]
            centre, inverse = stats_ref[n, 0:1, cols], stats_ref[n, 1:2, cols]
            nrm = (rows_buf[n, :, cols].astype(f32) - centre) * inverse
            g = gn_ref[:, cols] * own_scale(n)
            mid = gm_ref[n] if j == 0 else gmx_ref[n, j - 1].astype(f32)
            gin_buf[n % 2, :, cols] = mid + inverse * (g - a * (1.0 / D) - nrm * (b * (1.0 / D)))
        for j in range(NX):
            gin_copy(n, j).start()

    def l_block(side, h):
        d = HOPS - h
        return where(ring.tok(q + d if side == 0 else q - d))

    def l_load(k, side, h):
        return pltpu.make_async_copy(
            late_ref.at[k, :, l_block(side, h)], l_own.at[k, side], own_sem.at[k, side]
        )

    def l_hop(k, side, h):
        to = left if side else right
        if h == 0:
            return copy_to(
                late_ref.at[k, side, l_block(side, 0)], l_in.at[k, side, 0, side],
                l_send.at[k, side, h], l_recv.at[k, side, h], to,
            )
        return copy_to(
            l_out.at[k, side], l_in.at[k, side, h % 2], l_send.at[k, side, h], l_recv.at[k, side, h], to
        )

    def l_event(k, h):
        for side in range(2):
            l_hop(k, side, h - 1).wait_recv()
        for side in range(2):
            if h < HOPS or side == 0:
                l_load(k, side, h).wait()
            if 1 < h < HOPS:
                l_hop(k, side, h - 1).wait_send()
        if h < HOPS:
            for side in range(2):
                for u in range(2):
                    v = l_own[k, side, u]
                    if h > 1 or u == side:
                        v = (v.astype(f32) + l_in[k, side, (h - 1) % 2, u].astype(f32)).astype(bf16)
                    l_out[k, side, u] = v
            for side in range(2):
                l_hop(k, side, h).start()
                if h + 1 < HOPS or side == 0:
                    l_load(k, side, h + 1).start()
        else:
            for u in range(2):
                v = l_own[k, 0, u].astype(f32)
                for side in range(2):
                    if HOPS > 1 or u == side:
                        v = v + l_in[k, side, (h - 1) % 2, u].astype(f32)
                if k == 0:
                    late_out[u] = v
                else:
                    lx_out[k - 1, u] = v.astype(bf16)
            if k:
                lx_copy(k).start()

    def lx_copy(k):
        return copy_to(lx_out.at[k - 1], lx_in.at[k - 1], lx_send.at[k], lx_recv.at[k], partner(k))

    half = (QKV // 2 + 127) // 128 * 128

    def q_block(side, h):
        return l_block(side, h)

    def q_hop(side, h):
        to = left if side else right
        return copy_to(
            q_out.at[side], q_in.at[side, h % 2], q_send.at[side, h], q_recv.at[side, h], to
        )

    def q_event(h):
        if h:
            for side in range(2):
                q_hop(side, h - 1).wait_recv()
        if h < HOPS:
            for side in range(2):
                if h:
                    q_hop(side, h - 1).wait_send()
                block = q_block(side, h)
                a, b = accq_ref[block], acco_ref[block]
                if h:
                    a = a + q_in[side, (h - 1) % 2, :, :QKV].astype(f32)
                    b = b + q_in[side, (h - 1) % 2, :, QWIDE:].astype(f32)
                else:
                    lane = lax.broadcasted_iota(jnp.int32, a.shape, 1)
                    a = jnp.where((lane < half) if side == 0 else (lane >= half), a, 0.0)
                    b = b if side == 0 else jnp.zeros_like(b)
                q_out[side, :, :QKV] = a.astype(bf16)
                q_out[side, :, QWIDE:] = b.astype(bf16)
            for side in range(2):
                q_hop(side, h).start()
        else:
            a, b = accq_ref[q_block(0, h)], acco_ref[q_block(0, h)]
            for side in range(2):
                a = a + q_in[side, (h - 1) % 2, :, :QKV].astype(f32)
                b = b + q_in[side, (h - 1) % 2, :, QWIDE:].astype(f32)
            gqkv_ref[...] = a
            gout_ref[...] = b

    QWIDE = (QKV + 127) // 128 * 128

    def last_copy(k):
        return copy_to(msg_ref, lasts_buf.at[k], s_send.at[0, k], s_recv.at[0, k], ((t + k) % NT, p))

    def part_copy(k):
        return copy_to(
            part_ref.at[k], sum_ref.at[0, t], s_send.at[1, k], s_recv.at[1, k], ((t + NT - k) % NT, p)
        )

    def sum_copy(r):
        return copy_to(sum_ref.at[0], sum_ref.at[r], s_send.at[2, r], s_recv.at[2, r], (t, xor(p, r)))

    def cond_first():
        msg_ref[I : I + 1, :QKV] = qv_ref[0:1, :QKV]
        msg_ref[:, 6 * ML :] = msg_ref[:, 6 * ML :] + heads_ref[...] * factor_ref[...]
        for k in range(1, NT):
            last_copy(k).start()
        lasts_buf[0] = msg_ref[...]

    def cond_second():
        for k in range(1, NT):
            last_copy(k).wait_recv()
        lasts_ref[...] = lasts_buf[...]
        grads = lasts_buf[...].reshape(NT * 8, -1)
        total = 0.0
        for k in range(6):
            g = grads[:, k * ML : (k + 1) * ML]
            high = g.astype(bf16)
            low = (g - high.astype(f32)).astype(bf16)
            total = total + dot(high, ada_ref[k], 1, 1) + dot(low, ada_ref[k], 1, 1)
        part_ref[...] = jnp.zeros_like(part_ref)
        part_ref[:, :, :RB] = total.reshape(NT, 8, RB)
        for k in range(1, NT):
            part_copy(k).start()
        sum_ref[0, t] = part_ref[0]

    def cond_third():
        for k in range(1, NT):
            part_copy(k).wait_recv()
        for r in range(1, NP):
            sum_copy(r).start()

    def cond_last():
        total = sum_ref[0]
        for r in range(1, NP):
            sum_copy(r).wait_recv()
            total = total + sum_ref[r]
        cond_ref[...] = total

    @at(0)
    def _():
        greet(t, p, NT, NP)
        if I > 1:
            send_go(1)
        for k in range(NX):
            for side in range(2):
                l_hop(k, side, 0).start()
                l_load(k, side, 1).start()
        for n in range(I):
            rows_copy(n).start()
        msg_ref[...] = base_ref[...]
        heads_ref[...] = jnp.zeros_like(heads_ref)
        qv_ref[...] = jnp.zeros_like(qv_ref)
        wt_ref[...] = w_ref[:, w_ref.shape[1] - HO :].T
        accq_ref[...] = jnp.zeros_like(accq_ref)
        acco_ref[...] = jnp.zeros_like(acco_ref)
        for n in range(I):
            rows_copy(n).wait()

    for n in range(I):
        if n:
            at((n - 1) * steps + HL)(functools.partial(pass_go, n))
        at(n * steps)(functools.partial(load_go, n))

    @pl.when(s == 0)
    def _():
        for k in range(NX):
            v = go_buf[k].reshape(D, T)
            gc_ref[:, k * T : (k + 1) * T] = jnp.dot(wt_ref[...], v, preferred_element_type=f32)

    @pl.when((s > 0) & (s <= HL))
    def _():
        h = s - 1
        gate = gate_ref[i * HL + h]

        def head(k):
            return pl.ds(pl.multiple_of((k * HL + h) * HP, HP), HP)

        keys_t = qkv_ref[0, head(1)]
        keys = keys_t.T
        values = qkv_ref[0, head(2)].T
        gc = gc_ref[head(0)]
        inner = jnp.sum(mixed_ref[0, head(0)] * gc, axis=0, keepdims=True)
        lane = lax.broadcasted_iota(jnp.int32, (1, 128), 1)
        row = heads_ref[pl.ds(i, 1)]
        heads_ref[pl.ds(i, 1)] = row + jnp.where(lane == h, jnp.sum(inner), 0.0)
        delta = gate * inner
        grad = (gate * gc).astype(bf16)
        lse = lse_ref[0, pl.ds(h, 1)]
        queries = qkv_ref[0, head(0)]
        dv = jnp.zeros((LEN, HP), f32)
        dk = jnp.zeros((LEN, HP), f32)
        chunk = 256
        for j in range(LEN // chunk):
            part = slice(j * chunk, (j + 1) * chunk)
            qj = queries[:, part]
            do = grad[:, part]
            sc = jnp.dot(keys, qj, preferred_element_type=f32)
            pr = jnp.exp2(sc * SCALE2 - lse[:, part])
            dp = jnp.dot(values, do, preferred_element_type=f32)
            ds = (pr * (dp - delta[:, part])).astype(bf16)
            dv = dv + jnp.dot(pr.astype(bf16), do.T, preferred_element_type=f32)
            dk = dk + jnp.dot(ds, qj.T, preferred_element_type=f32)
            dq = jnp.dot(keys_t, ds, preferred_element_type=f32)
            dqkv_ref[head(0), part] = (dq * SCALE).astype(bf16)
        dqkv_ref[head(1)] = (dk * SCALE).T.astype(bf16)
        dqkv_ref[head(2)] = dv.T.astype(bf16)

    @pl.when(s == HL + 1)
    def _():
        for r in range(NP):
            w = w_ref[r * CB : (r + 1) * CB, :QKV]
            part = jnp.dot(w, dqkv_ref[...], preferred_element_type=f32)
            if r % 2 == 0:
                own_ref[r // 2] = part
            else:
                core_out[r // 2] = part.astype(bf16)
        for b in range(0, NT, 2):
            rows = slice(b * RB, (b + 2) * RB)
            v = dot(attn_ref[0, rows], dqkv_ref[...], 1, 1)
            accq_ref[b : b + 2] = accq_ref[b : b + 2] + v.reshape(2, RB, QKV)
            v = 0.0
            for k in range(NX):
                g = go_buf[k].reshape(D, T)[rows]
                v = v + dot(g, concat_ref[0, :, k * T : (k + 1) * T], 1, 1)
            acco_ref[b : b + 2] = acco_ref[b : b + 2] + v.reshape(2, RB, HO)
        qv_ref[0:1, :QKV] = qv_ref[0:1, :QKV] + tokens(dqkv_ref[...].astype(f32))

    for n in range(I):
        at(n * steps + HL + 1)(lambda n=n: core_copy(n).start())
    for n in range(I - 1):
        at((n + 1) * steps + 1)(functools.partial(add_core, n))
        at((n + 1) * steps + HL - 1)(functools.partial(add_x, n))

        @at((n + 1) * steps + HL)
        def _(n=n):
            add_stats(n)
            core_copy(n).wait_send()

    events = [functools.partial(l_event, k, h) for h in range(1, HOPS + 1) for k in range(NX)]
    early = [2, 3, steps + HL - 1, steps + HL, 3 * steps - 2, 3 * steps - 1] if I > 2 else []
    early = early[: len(events)]
    for n, event in zip(early, events):
        at(n)(event)

    @at(I * steps - 1)
    def _():
        rest = events[len(early) :]
        q_event(0)
        add_core(I - 1)
        todo = [functools.partial(add_x, I - 1), cond_first, functools.partial(q_event, 1),
                functools.partial(add_stats, I - 1), cond_second]
        todo += [functools.partial(q_event, h) for h in range(2, 3)] + [cond_third]
        todo += [functools.partial(q_event, h) for h in range(3, HOPS + 1)] + [cond_last]
        ratio = max(1, len(todo) // max(1, len(rest)))
        while todo or rest:
            if rest:
                rest.pop(0)()
            for _ in range(ratio if rest else len(todo)):
                if todo:
                    todo.pop(0)()
        for k in range(1, NX):
            lx_copy(k).wait_recv()
            for u in range(2):
                late_out[u] = late_out[u] + lx_in[k - 1, u].astype(f32)
        core_copy(I - 1).wait_send()
        for n in range(I):
            for k in range(1, NX):
                gm_x(n, k).wait_send()
                for f in range(NX if n else 0):
                    go_x(n, k, f).wait_send()
                    go_core(n, k, f).wait_send()
                if n >= I - 2:
                    x_copy(n, k).wait_send()
            for r in range(1, NP):
                st_copy(n, r).wait_send()
            if n >= I - 2:
                for j in range(NX):
                    gin_copy(n, j).wait()
        for k in range(NX):
            for side in range(2):
                l_hop(k, side, 0).wait_send()
                if HOPS > 1:
                    l_hop(k, side, HOPS - 1).wait_send()
        for side in range(2):
            q_hop(side, HOPS - 1).wait_send()
        for k in range(1, NX):
            lx_copy(k).wait_send()
        for k in range(1, NT):
            last_copy(k).wait_send()
            part_copy(k).wait_send()
        for r in range(1, NP):
            sum_copy(r).wait_send()


def bwd_call(
    NT, NP, gate, go, go0, gms, gm, qkv, mixed, lse, concat, attn, rows, stats, scale, w, late, base, factor, ada
):
    I, CB, T = gm.shape
    NX = NP // 2
    length = attn.shape[2]
    HL = gate.shape[0] // I
    QKV, HO = 3 * HL * HP, HL * HP
    QWIDE = (QKV + 127) // 128 * 128
    RB, FL = late.shape[3:]
    HOPS = NT // 2
    hbm = pl.BlockSpec(memory_space=pl.ANY)
    vmem = pl.BlockSpec(memory_space=pltpu.VMEM)
    dma = pltpu.SemaphoreType.DMA
    once = pl.Buffered(buffer_count=1)

    def image(*shape):
        return pl.BlockSpec(
            (1,) + shape, lambda i, s: (i,) + (0,) * len(shape), pipeline_mode=once
        )

    return pl.pallas_call(
        functools.partial(bwd_kernel, NT, NP),
        grid=(I, HL + 2),
        in_specs=[
            pl.BlockSpec(memory_space=pltpu.SMEM),
            hbm,
            hbm,
            hbm,
            vmem,
            image(QKV, length),
            image(HO, length),
            image(HL, length),
            image(HO, length),
            image(D, length),
            hbm,
            vmem,
            vmem,
            vmem,
            hbm,
            vmem,
            vmem,
            vmem,
        ],
        out_specs=[hbm, vmem, vmem, vmem, vmem, vmem, hbm],
        out_shape=[
            jax.ShapeDtypeStruct((I, CB, length), f32),
            jax.ShapeDtypeStruct((2, RB, FL), f32),
            jax.ShapeDtypeStruct((RB, QKV), f32),
            jax.ShapeDtypeStruct((RB, HO), f32),
            jax.ShapeDtypeStruct((NT,) + base.shape, f32),
            jax.ShapeDtypeStruct((NT, 8, 256), f32),
            jax.ShapeDtypeStruct((I, NX, NX, 2, CB, T), bf16),
        ],
        scratch_shapes=[
            pltpu.VMEM((NX, NX, 2, CB, T), bf16),
            pltpu.VMEM((I, NX - 1, CB, T), bf16),
            pltpu.VMEM((NX, CB, length), f32),
            pltpu.VMEM((NX, CB, length), bf16),
            pltpu.VMEM((2, NX, CB, length), bf16),
            pltpu.VMEM((2, NX - 1, CB, length), bf16),
            pltpu.VMEM((2, NX - 1, CB, length), bf16),
            pltpu.VMEM((CB, length), f32),
            pltpu.VMEM((NT, RB, QKV), f32),
            pltpu.VMEM((NT, RB, HO), f32),
            pltpu.VMEM((HO, D), bf16),
            pltpu.VMEM((HO, length), f32),
            pltpu.VMEM((QKV, length), bf16),
            pltpu.VMEM((I, CB, length), bf16),
            pltpu.VMEM((2, CB, length), f32),
            pltpu.VMEM((I, 8, length), f32),
            pltpu.VMEM((I, NP, 8, length), f32),
            pltpu.VMEM(base.shape, f32),
            pltpu.VMEM((8, 128), f32),
            pltpu.VMEM((8, QWIDE), f32),
            pltpu.VMEM((NX, 2, 2, RB, FL), bf16),
            pltpu.VMEM((NX, 2, 2, RB, FL), bf16),
            pltpu.VMEM((NX, 2, 2, 2, RB, FL), bf16),
            pltpu.VMEM((NX - 1, 2, RB, FL), bf16),
            pltpu.VMEM((NX - 1, 2, RB, FL), bf16),
            pltpu.VMEM((2, RB, QWIDE + HO), bf16),
            pltpu.VMEM((2, 2, RB, QWIDE + HO), bf16),
            pltpu.VMEM((NT, 8, 256), f32),
            pltpu.VMEM((NP, NT, 8, 256), f32),
            pltpu.VMEM((NT,) + base.shape, f32),
            dma((2, I, NX, NX)),
            dma((2, I, NX, NX)),
            dma((I,)),
            dma((I,)),
            dma((I, NX)),
            dma((I, NX)),
            dma((I, NP)),
            dma((I, NP)),
            dma((NX, 2, HOPS)),
            dma((NX, 2, HOPS)),
            dma((NX,)),
            dma((NX,)),
            dma((2, HOPS)),
            dma((2, HOPS)),
            dma((3, max(NT, NP))),
            dma((3, max(NT, NP))),
            dma((I, NX)),
            dma((I, NX)),
            dma((NX + I + I * NX,)),
            dma((NX, 2)),
        ],
        compiler_params=pltpu.CompilerParams(
            collective_id=1, has_side_effects=True, vmem_limit_bytes=63 * 2**20
        ),
        name="backward",
    )(gate, go, go0, gms, gm, qkv, mixed, lse, concat, attn, rows, stats, scale, w, late, base, factor, ada)


def make_body(NT, NP):
    NX = NP // 2
    SUB = NT // NP
    RB = D // NT
    CB = D // NP
    T = LEN // NX

    def tp_xor(v, r):
        return lax.ppermute(v, "tp", [(p, p ^ r) for p in range(NP)])

    def body(
        block_input,
        condition,
        timesteps,
        head_mask,
        group_mask,
        w_ada,
        b_ada,
        w_qkv,
        b_qv,
        w_out,
        b_out,
        w_up,
        b_up,
        w_down,
        b_down,
        w_head,
        b_head,
        w_group,
        b_group,
        cotangent,
    ):
        I = condition.shape[0]
        HL = head_mask.shape[1]
        GL = group_mask.shape[1]
        FL = w_up.shape[1]
        FR = FREQ // NT
        t = lax.axis_index("tok")
        p = lax.axis_index("tp")
        xi = p // 2

        qkv_shard = jnp.pad(
            w_qkv.reshape(RB, 3, HL, HD), ((0, 0), (0, 0), (0, 0), (0, HP - HD))
        ).reshape(RB, 3 * HL * HP)
        out_shard = jnp.pad(w_out.T.reshape(RB, HL, HD), ((0, 0), (0, 0), (0, HP - HD))).reshape(
            RB, HL * HP
        )
        QKV = 3 * HL * HP
        gap = -QKV % 128
        early_shard = jnp.concatenate(
            [qkv_shard, jnp.zeros((RB, gap), bf16), out_shard], axis=1
        )
        late_shard = jnp.stack([w_up, w_down.T])
        late_shards = jnp.stack(
            [late_shard] + [tp_xor(late_shard, 2 * k) for k in range(1, NX)]
        )
        time_feat = embed_time(timesteps).astype(bf16)
        cond_wide = condition.astype(f32)
        cond_act = jax.nn.silu(cond_wide).astype(bf16)
        pad8 = lambda v, width: jnp.pad(v, ((0, 8 - v.shape[0]), (0, width - v.shape[1])))
        message = jnp.concatenate(
            [
                jnp.pad(cond_act.reshape(I, NT, RB), ((0, 0), (0, 0), (0, 256 - RB))),
                jnp.pad(time_feat.reshape(I, NT, FR), ((0, 0), (0, 0), (0, ML - 256 - FR))),
            ],
            axis=2,
        )
        message = jnp.pad(message.transpose(1, 0, 2).astype(f32), ((0, 0), (0, 8 - I), (0, 0)))
        ada = jnp.pad(w_ada.transpose(1, 0, 2), ((0, 0), (0, 0), (0, ML - CB)))
        gates = jnp.concatenate([w_head, w_group], axis=1)
        gates = jnp.pad(gates, ((0, 0), (0, 128 - HL - GL)))
        wide = 6 * ML + 128
        mod_bias = jnp.concatenate(
            [jnp.pad(b_ada, ((0, 0), (0, ML - CB))).reshape(6 * ML), b_head, b_group]
        ).astype(f32)
        bias = jnp.concatenate(
            [
                jnp.broadcast_to(pad8(mod_bias[None], wide)[:1], (I, wide)),
                pad8(jnp.concatenate([jnp.pad(b_out, (0, ML - CB)), b_down]).astype(f32)[None], wide)[:1],
                pad8(b_up.astype(f32)[None], wide)[: 8 - I - 1],
            ],
            axis=0,
        )
        mask = pad8(jnp.concatenate([head_mask, group_mask], axis=1).astype(f32), 128)
        first, early_full, mods, sig, cond_all = start_call(
            NT,
            NP,
            block_input,
            early_shard,
            message,
            ada,
            gates,
            bias,
            mask,
        )
        early_full = early_full.reshape(D, -1)
        head_sig, group_sig = sig[:I, :HL], sig[:I, HL : HL + GL]
        head_gate = mods[0, :I, 6 * ML : 6 * ML + HL]
        group_rows = jnp.stack(
            [
                jnp.repeat(mods[2 * k, :, 6 * ML + HL : 6 * ML + HL + GL], GW, axis=1)
                for k in range(NX)
            ]
        )

        qv = b_qv.astype(f32).reshape(2, HL, HD)
        qv_bias = jnp.stack(
            [
                jnp.pad(qv[0], ((0, 0), (0, HP - HD))),
                jnp.zeros((HL, HP), f32),
                jnp.concatenate(
                    [qv[1], jnp.ones((HL, 1), f32), jnp.zeros((HL, HP - HD - 1), f32)], axis=1
                ),
            ]
        ).reshape(3 * HL * HP, 1)

        attn_all, qkv_all, mixed_all, concat_all, lse_all, stats_all, branch, late_full, rows_all, cots = (
            fwd_call(
                NT,
                NP,
                head_gate.reshape(-1),
                block_input,
                cotangent,
                first,
                early_full,
                mods,
                qv_bias,
                late_shards,
            )
        )
        late_full = late_full.reshape(NX, 2, D, FL)

        lhs, rhs, grad_one, grad_mid_out, grad_mid_own, sums, fsums, block_output, go_first = mlp_call(
            NT,
            NP,
            branch,
            rows_all,
            cots.reshape(I, D, T),
            mods,
            group_rows,
            late_full,
        )
        late_grads = grads_call(NT, lhs, rhs)

        gate_sums = jnp.sum(fsums[:, 1].reshape(I, NX * GL, GW), axis=2)
        up_sums = jnp.sum(fsums[:, 0], axis=0)
        all_sums = jnp.sum(sums[:, 3:5], axis=0)

        def x_message(k):
            mine = slice(2 * k * CB, (2 * k + 1) * CB)
            parts = [
                jnp.concatenate(
                    [
                        sums[:, :3, mine].reshape(I, 3 * CB),
                        sums[:, 5, k * CB : (k + 1) * CB],
                        gate_sums[:, k * GL : (k + 1) * GL],
                    ],
                    axis=1,
                ).reshape(-1),
                all_sums[:, mine].reshape(-1),
                up_sums[k * FL : (k + 1) * FL],
            ]
            return jnp.concatenate(parts)

        x_total = x_message(0)
        for k in range(1, NX):
            x_total = x_total + tp_xor(x_message(k), 2 * k)
        per = 4 * CB + GL
        per_image = x_total[: I * per].reshape(I, per)
        late_mods = per_image[:, : 4 * CB].reshape(I, 4, CB)
        grad_group_gate = per_image[:, 4 * CB :]
        bias_sums = x_total[I * per :]

        head_factor = head_mask.astype(f32) * head_sig * (1.0 - head_sig)
        group_logit = grad_group_gate * group_mask.astype(f32) * group_sig * (1.0 - group_sig)
        image_rows = jnp.concatenate(
            [
                jnp.pad(late_mods, ((0, 0), (2, 0), (0, ML - CB))).reshape(I, 6 * ML),
                jnp.zeros((I, HL), f32),
                group_logit,
                jnp.zeros((I, 128 - HL - GL), f32),
            ],
            axis=1,
        )
        widen = lambda v: jnp.pad(v, (0, wide - v.shape[0]))[None]
        base = jnp.concatenate(
            [
                image_rows,
                jnp.zeros((1, wide), f32),
                widen(bias_sums[: 2 * CB]),
                widen(bias_sums[2 * CB :]),
                jnp.zeros((8 - I - 3, wide), f32),
            ],
            axis=0,
        )
        grad_input, late, grad_qkv, grad_out, lasts, cond_sum, _ = bwd_call(
            NT,
            NP,
            head_gate.reshape(-1),
            grad_one.reshape(I, NX, 2, CB, T),
            go_first,
            grad_mid_out,
            grad_mid_own,
            qkv_all,
            mixed_all,
            lse_all,
            concat_all,
            attn_all,
            rows_all,
            stats_all,
            mods,
            early_full,
            late_grads,
            base,
            pad8(head_factor, 128),
            ada,
        )
        grad_up, grad_down = late[0], late[1]
        mods_all = (
            lasts[:, :I, : 6 * ML].reshape(NT * I, 6, ML)[:, :, :CB].reshape(NT * I, 6 * CB)
        )
        logits_all = lasts[:, :I, 6 * ML : 6 * ML + HL + GL].reshape(NT * I, HL + GL)
        bias_rows = jnp.sum(lasts[:, I : I + 3], axis=0)
        qv_rows = bias_rows[0, :QKV].reshape(3, HL, HP)[:, :, :HD].reshape(3, HL * HD)
        cond_f = cond_all[:, :I, :RB].reshape(NT * I, RB)
        time_f = cond_all[:, :I, 256 : 256 + FR].reshape(NT * I, FR)
        grad_w_ada = lax.dot_general(
            cond_f, mods_all, (((0,), (0,)), ((), ())), precision=exact_mode
        ).reshape(RB, 6, CB)
        grad_b_ada = jnp.sum(mods_all, axis=0).reshape(6, CB)
        grad_w_gates = lax.dot_general(
            time_f, logits_all, (((0,), (0,)), ((), ())), precision=exact_mode
        )
        grad_b_gates = jnp.sum(logits_all, axis=0)
        cond_total = cond_sum[:, :I, :RB].transpose(1, 0, 2).reshape(I, D)
        grad_condition = jax.vjp(jax.nn.silu, cond_wide)[1](cond_total)[0]

        return (
            block_output,
            grad_input,
            grad_condition,
            grad_w_ada,
            grad_b_ada,
            grad_qkv.reshape(RB, 3, HL, HP)[..., :HD].reshape(RB, 3, HL * HD),
            jnp.stack([qv_rows[0], qv_rows[2]]),
            grad_out.reshape(RB, HL, HP)[..., :HD].reshape(RB, HL * HD).T,
            bias_rows[1, :CB],
            grad_up,
            bias_rows[2, :FL],
            grad_down.T,
            bias_rows[1, CB : 2 * CB],
            grad_w_gates[:, :HL],
            grad_b_gates[:HL],
            grad_w_gates[:, HL:],
            grad_b_gates[HL:],
        )

    return body


def solution(mesh):
    return jax.shard_map(
        make_body(mesh.shape["tok"], mesh.shape["tp"]),
        mesh=mesh,
        in_specs=(
            P("tok", "tp", None),
            P("tok", None),
            P("tok"),
            P("tok", "tp"),
            P("tok", "tp"),
            P("tok", None, "tp"),
            P(None, "tp"),
            P("tok", None, "tp"),
            P(None, "tp"),
            P("tp", "tok"),
            P("tp"),
            P("tok", "tp"),
            P("tp"),
            P("tp", "tok"),
            P("tp"),
            P("tok", "tp"),
            P("tp"),
            P("tok", "tp"),
            P("tp"),
            P("tok", "tp", None),
        ),
        out_specs=(
            P("tok", "tp", None),
            P("tok", "tp", None),
            P("tok", None),
            P("tok", None, "tp"),
            P(None, "tp"),
            P("tok", None, "tp"),
            P(None, "tp"),
            P("tp", "tok"),
            P("tp"),
            P("tok", "tp"),
            P("tp"),
            P("tp", "tok"),
            P("tp"),
            P("tok", "tp"),
            P("tp"),
            P("tok", "tp"),
            P("tp"),
        ),
        check_vma=False,
    )
```

```python
import functools
import math

import jax
import jax.numpy as jnp
from jax import lax
from jax.experimental import pallas as pl
from jax.experimental.pallas import tpu as pltpu
from jax.sharding import PartitionSpec as P

D = 1152
HD = 72
HP = 80
FF = 4608
FREQ = 256
GROUPS = 16
GW = FF // GROUPS
LEN = 1024
EPS = 1e-06
SCALE = HD**-0.5
SCALE2 = SCALE / math.log(2.0)

f32 = jnp.float32
bf16 = jnp.bfloat16
exact_mode = lax.Precision.HIGHEST


def dot(a, b, ca, cb):
    return lax.dot_general(a, b, (((ca,), (cb,)), ((), ())), preferred_element_type=f32)


def embed_time(timesteps):
    half_width = FREQ // 2
    indices = jnp.arange(half_width, dtype=f32)
    freq_rates = jnp.exp(-math.log(10000.0) * indices / half_width)
    angles = timesteps.astype(f32)[:, None] * freq_rates[None, :]
    return jnp.concatenate([jnp.cos(angles), jnp.sin(angles)], axis=1)


MESH = pl.DeviceIdType.MESH
ML = 384


def xor(v, k):
    out, bit = 0, 1
    while bit <= k or bit <= 8:
        b = (v // bit) % 2
        out = out + bit * (1 - b if k & bit else b)
        bit *= 2
    return out


class Ring:
    def __init__(self, NT):
        self.NT, self.tall = NT, NT // 2

    def place(self, t):
        b = t % 2
        return (1 - b) * (self.tall - 1 - t // 2) + b * (self.tall + t // 2)

    def tok(self, q):
        q = (q + 2 * self.NT) % self.NT
        b = q // self.tall
        return (1 - b) * 2 * (self.tall - 1 - q) + b * (2 * (q - self.tall) + 1)


def copy_to(src, dst, send, recv, device):
    return pltpu.make_async_remote_copy(
        src_ref=src, dst_ref=dst, send_sem=send, recv_sem=recv, device_id=device, device_id_type=MESH
    )


def greet(t, p, NT, NP):
    barrier = pltpu.get_barrier_semaphore()
    for r in range(1, NP):
        pl.semaphore_signal(barrier, inc=1, device_id=(t, xor(p, r)), device_id_type=MESH)
    for k in range(1, NT):
        pl.semaphore_signal(barrier, inc=1, device_id=((t + k) % NT, p), device_id_type=MESH)
    pl.semaphore_wait(barrier, NP - 1 + NT - 1)


class ImageMoves:
    def __init__(self, NP, x_ref, rows_ref, x_send, x_recv, c_send, c_recv, local_sem):
        self.NX = NP // 2
        self.T = x_ref.shape[2] // self.NX
        self.refs = (x_ref, rows_ref)
        self.sems = (x_send, x_recv, c_send, c_recv, local_sem)
        self.t, self.p = lax.axis_index("tok"), lax.axis_index("tp")
        self.core = (self.t, xor(self.p, 1))

    def tokens(self, who, j):
        return pl.ds(pl.multiple_of(xor(who, j) * self.T, self.T), self.T)

    def src(self, i, j):
        return self.refs[0].at[i, :, pl.ds(j * self.T, self.T)]

    def x(self, i, k, j):
        x_send, x_recv = self.sems[:2]
        at = self.tokens(xor(self.p // 2, k), j)
        dst = self.refs[1].at[i, 2 * k, :, at]
        device = (self.t, xor(self.p, 2 * k))
        return copy_to(self.src(i, j), dst, x_send.at[i, k, j], x_recv.at[i, k, j], device)

    def own(self, i, j):
        dst = self.refs[1].at[i, 0, :, self.tokens(self.p // 2, j)]
        return pltpu.make_async_copy(self.src(i, j), dst, self.sems[4].at[i, j])

    def own_core(self, i, j):
        dst = self.refs[1].at[i, 1, :, self.tokens(self.p // 2, j)]
        c_send, c_recv = self.sems[2:4]
        return copy_to(self.src(i, j), dst, c_send.at[i, 0, j], c_recv.at[i, 0, j], self.core)

    def passed(self, i, k):
        rows = self.refs[1]
        c_send, c_recv = self.sems[2:4]
        return copy_to(
            rows.at[i, 2 * k], rows.at[i, 2 * k + 1], c_send.at[i, k, 0], c_recv.at[i, k, 0], self.core
        )

    def start(self, i):
        for k in range(1, self.NX):
            for j in range(self.NX):
                self.x(i, k, j).start()
        for j in range(self.NX):
            self.own(i, j).start()
            self.own_core(i, j).start()

    def land(self, i):
        for k in range(1, self.NX):
            for j in range(self.NX):
                self.x(i, k, j).wait_recv()
            self.passed(i, k).start()

    def finish(self, i):
        for j in range(self.NX):
            self.own(i, j).wait()
            self.own_core(i, j).wait_recv()
        for k in range(1, self.NX):
            self.passed(i, k).wait_recv()

    def left(self, i):
        for j in range(self.NX):
            self.own_core(i, j).wait_send()
        for k in range(1, self.NX):
            self.passed(i, k).wait_send()
            for j in range(self.NX):
                self.x(i, k, j).wait_send()


def start_kernel(
    NT, NP, x_ref, w_ref, msg_ref, ada_ref, gates_ref, bias_ref, mask_ref,
    rows_ref, full_ref, mods_ref, sig_ref, cond_ref,
    part_ref, got_ref, x_send, x_recv, c_send, c_recv, r_send, r_recv, s_send, s_recv, local_sem,
):
    NX, SUB = NP // 2, NT // NP
    WN = w_ref.shape[1]
    half = WN // 256 * 128
    t, p = lax.axis_index("tok"), lax.axis_index("tp")
    ring = Ring(NT)
    q = ring.place(t)
    right, left = (ring.tok(q + 1), p), (ring.tok(q - 1), p)

    def where(tt):
        out = 0
        for r in range(NP):
            out = out + jnp.where(p == r, xor(tt // SUB, r), 0)
        return out * SUB + tt % SUB

    greet(t, p, NT, NP)

    small = []
    for k in range(1, NT):
        peer = (t + k) % NT
        small.append(copy_to(msg_ref.at[peer], cond_ref.at[k], s_send.at[0, k], s_recv.at[0, k], (peer, p)))
        small[-1].start()

    def hop(d, to_right):
        side = 0 if to_right else 1
        block = where(ring.tok(q - (d - 1) if to_right else q + (d - 1)))
        src = w_ref if d == 1 else full_ref.at[block]
        dst = full_ref.at[block]
        if d == NT // 2:
            cols = pl.ds(0, half) if to_right else pl.ds(half, WN - half)
            src, dst = src.at[:, cols], dst.at[:, cols]
        return copy_to(src, dst, r_send.at[side, d], r_recv.at[side, d], right if to_right else left)

    hops = {}

    def start_hop(d):
        for to_right in (True, False):
            hops[d, to_right] = hop(d, to_right)
            hops[d, to_right].start()

    def land_hop(d):
        for to_right in (True, False):
            hops[d, to_right].wait_recv()

    images = ImageMoves(NP, x_ref, rows_ref, x_send, x_recv, c_send, c_recv, local_sem)
    images.start(0)
    start_hop(1)
    keep = pltpu.make_async_copy(w_ref, full_ref.at[where(t)], local_sem.at[1, 0])
    keep.start()

    cond_ref[0] = msg_ref[t]
    for cp in small:
        cp.wait_recv()
    rb, fr = ada_ref.shape[1], gates_ref.shape[0]
    feats = cond_ref[...].reshape(NT * 8, -1).astype(bf16)
    for k in range(6):
        part = jnp.dot(feats[:, :rb], ada_ref[k], preferred_element_type=f32)
        part_ref[:, :, k * ML : (k + 1) * ML] = part.reshape(NT, 8, ML)
    part = jnp.dot(feats[:, 256 : 256 + fr], gates_ref[...], preferred_element_type=f32)
    part_ref[:, :, 6 * ML :] = part.reshape(NT, 8, 128)
    for k in range(1, NT):
        peer = (t + NT - k) % NT
        cp = copy_to(part_ref.at[k], got_ref.at[k], s_send.at[1, k], s_recv.at[1, k], (peer, p))
        cp.start()
        small.append(cp)
    land_hop(1)
    start_hop(2)
    for cp in small[NT - 1 :]:
        cp.wait_recv()
    total = part_ref[0]
    for k in range(1, NT):
        total = total + got_ref[k]
    total = total + bias_ref[...]
    sig = 1.0 / (1.0 + jnp.exp(-total[:, 6 * ML :]))
    sig_ref[...] = sig
    mods_ref[0, :, : 6 * ML] = total[:, : 6 * ML]
    mods_ref[0, :, 6 * ML :] = sig * mask_ref[...]
    mods = []
    for r in range(1, NP):
        cp = copy_to(mods_ref.at[0], mods_ref.at[r], s_send.at[2, r], s_recv.at[2, r], (t, xor(p, r)))
        cp.start()
        mods.append(cp)

    images.land(0)
    for d in range(2, NT // 2 + 1):
        land_hop(d)
        if d < NT // 2:
            start_hop(d + 1)
    images.finish(0)
    for cp in mods:
        cp.wait_recv()
    keep.wait()
    images.left(0)
    for cp in small + mods + list(hops.values()):
        cp.wait_send()


def start_call(NT, NP, x, w, msg, ada, gates, bias, mask):
    _, CB, length = x.shape
    NX = NP // 2
    RB, WN = w.shape
    wide = 6 * ML + 128
    hbm, vmem = pl.BlockSpec(memory_space=pl.ANY), pl.BlockSpec(memory_space=pltpu.VMEM)
    dma = pltpu.SemaphoreType.DMA
    return pl.pallas_call(
        functools.partial(start_kernel, NT, NP),
        in_specs=[pl.BlockSpec((1, CB, length), lambda i: (0, 0, 0))] + [vmem] * 6,
        grid=(1,),
        out_specs=[hbm, hbm, vmem, vmem, vmem],
        out_shape=[
            jax.ShapeDtypeStruct((1, NP, CB, length), bf16),
            jax.ShapeDtypeStruct((NT, RB, WN), bf16),
            jax.ShapeDtypeStruct((NP, 8, wide), f32),
            jax.ShapeDtypeStruct((8, 128), f32),
            jax.ShapeDtypeStruct((NT, 8, ML), f32),
        ],
        scratch_shapes=[
            pltpu.VMEM((NT, 8, wide), f32),
            pltpu.VMEM((NT, 8, wide), f32),
            dma((1, NX, NX)),
            dma((1, NX, NX)),
            dma((1, NX, NX)),
            dma((1, NX, NX)),
            dma((2, NT // 2 + 1)),
            dma((2, NT // 2 + 1)),
            dma((3, max(NT, NP))),
            dma((3, max(NT, NP))),
            dma((2, NX)),
        ],
        compiler_params=pltpu.CompilerParams(
            collective_id=0, has_side_effects=True, vmem_limit_bytes=32 * 2**20
        ),
        name="start",
    )(x, w, msg, ada, gates, bias, mask)


def spread(mods_ref, r, rows, CB):
    parts = [mods_ref[r, row, at : at + ML] for row, at in rows]
    parts += [jnp.zeros((8 - len(parts), ML), f32)] if len(parts) < 8 else []
    return jnp.concatenate(parts, axis=0).T[:CB]


def fwd_kernel(
    NT, NP, gate_ref, x_ref, cot_ref, first_ref, w_ref, mod_ref, bias_ref, late_ref,
    attn_ref, qkv_ref, mixed_ref, concat_ref, lse_ref, stats_ref, branch_ref, full_ref, rows_ref, cots_ref,
    wt_ref, own_ref, core_out, core_in, x_out, x_in, total_ref,
    mcol_ref, l_send, l_recv, c_send, c_recv, x_send, x_recv, b_send, b_recv, local_sem,
    rows_buf, rx_send, rx_recv, rc_send, rc_recv, r_sem, t_send, t_recv, t_sem,
):
    NX, SUB = NP // 2, NT // NP
    I, CB, T = total_ref.shape[0], total_ref.shape[2], total_ref.shape[3]
    HL = gate_ref.shape[0] // I
    QKV = 3 * HL * HP
    steps = HL + 2
    i, s = pl.program_id(0), pl.program_id(1)
    flat = i * steps + s
    t, p = lax.axis_index("tok"), lax.axis_index("tp")
    ring = Ring(NT)
    q = ring.place(t)
    right, left = (ring.tok(q + 1), p), (ring.tok(q - 1), p)
    core = (t, xor(p, 1))

    def at(n):
        return pl.when(flat == n)

    images = ImageMoves(NP, x_ref, rows_ref, rx_send, rx_recv, rc_send, rc_recv, r_sem)

    def first_keep():
        return pltpu.make_async_copy(rows_buf, rows_ref.at[0], r_sem.at[0, 0])

    def load_rows(n):
        if n:
            images.finish(n)
        if n == 1:
            first_keep().wait()
        src = rows_ref.at[n] if n else first_ref.at[0]
        cp = pltpu.make_async_copy(src, rows_buf, r_sem.at[I, 0])
        cp.start()
        cp.wait()
        if n == 0:
            first_keep().start()

    def cot_x(n, k):
        src = cot_ref.at[n, :, images.tokens(xor(p // 2, k), 0)]
        return copy_to(
            src, cots_ref.at[n, k, 0], t_send.at[0, n, k], t_recv.at[0, n, k], (t, xor(p, 2 * k))
        )

    def cot_keep(n):
        src = cot_ref.at[n, :, images.tokens(p // 2, 0)]
        return pltpu.make_async_copy(src, cots_ref.at[n, 0, 0], t_sem.at[n])

    def cot_core(n, k):
        src = cots_ref.at[n, k, 0] if k else cot_ref.at[n, :, images.tokens(p // 2, 0)]
        return copy_to(src, cots_ref.at[n, k, 1], t_send.at[1, n, k], t_recv.at[1, n, k], core)

    def start_cot():
        for n in range(I):
            for k in range(1, NX):
                cot_x(n, k).start()

    def land_cot():
        for n in range(I):
            for k in range(1, NX):
                cot_x(n, k).wait_recv()
                cot_core(n, k).start()

    def where(tt):
        out = 0
        for r in range(NP):
            out = out + jnp.where(p == r, xor(tt // SUB, r), 0)
        return out * SUB + tt % SUB

    def hop(k, d, side):
        block = where(ring.tok(q - (d - 1) if side == 0 else q + (d - 1)))
        dst = full_ref.at[k, :, block]
        src = late_ref.at[k] if d == 1 else dst
        if d == NT // 2:
            src, dst = src.at[side], dst.at[side]
        return copy_to(src, dst, l_send.at[k, side, d], l_recv.at[k, side, d], left if side else right)

    def keep(k):
        return pltpu.make_async_copy(late_ref.at[k], full_ref.at[k, :, where(t)], local_sem.at[k])

    def start_hop(k, d):
        for side in range(2):
            hop(k, d, side).start()

    def land_hop(k, d):
        for side in range(2):
            hop(k, d, side).wait_recv()
        if d < NT // 2:
            start_hop(k, d + 1)

    def core_copy(i):
        return copy_to(core_out.at[i], core_in.at[i], c_send.at[i], c_recv.at[i], core)

    def x_copy(i, k):
        return copy_to(
            x_out.at[i, k], x_in.at[i, k], x_send.at[i, k], x_recv.at[i, k], (t, xor(p, 2 * k))
        )

    def back_copy(i):
        return copy_to(total_ref.at[i], branch_ref.at[i, 1], b_send.at[i], b_recv.at[i], core)

    def back_keep(i):
        return pltpu.make_async_copy(total_ref.at[i], branch_ref.at[i, 0], local_sem.at[NX + i])

    def add_core(i):
        core_copy(i).wait_recv()
        for f in range(NX):
            for k in range(NX):
                cols = slice(k * T, (k + 1) * T)
                v = own_ref[f, :, cols] + core_in[i, f, :, cols].astype(f32)
                if k == 0:
                    total_ref[i, f] = v
                else:
                    x_out[i, k, f] = v.astype(bf16)
        for k in range(1, NX):
            x_copy(i, k).start()

    def add_x(i):
        for k in range(1, NX):
            x_copy(i, k).wait_recv()
        for f in range(NX):
            v = total_ref[i, f]
            for k in range(1, NX):
                v = v + x_in[i, k, f ^ k].astype(f32)
            total_ref[i, f] = v
        back_copy(i).start()
        back_keep(i).start()

    @at(0)
    def _():
        barrier = pltpu.get_barrier_semaphore()
        peers = [right, left, core] + [(t, xor(p, 2 * k)) for k in range(1, NX)]
        for peer in peers:
            pl.semaphore_signal(barrier, inc=1, device_id=peer, device_id_type=MESH)
        pl.semaphore_wait(barrier, len(peers))
        if I > 1:
            images.start(1)
        for k in range(NX):
            start_hop(k, 1)
        for n in range(I):
            cot_keep(n).start()
            cot_core(n, 0).start()
        for k in range(NX):
            keep(k).start()
        wt_ref[...] = w_ref[:, :QKV].T

    for n in range(I):
        if n:

            @at((n - 1) * steps + HL)
            def _(n=n):
                images.land(n)
                if n + 1 < I:
                    images.start(n + 1)
                else:
                    start_cot()

        at(n * steps)(functools.partial(load_rows, n))

    @pl.when(s == 0)
    def _():
        for r in range(NP):
            rows = [(pl.ds(i, 1), 0), (pl.ds(i, 1), ML)]
            mcol_ref[r * CB : (r + 1) * CB] = spread(mod_ref, r, rows, CB)
        width = 256
        for j in range(LEN // width):
            cols = slice(j * width, (j + 1) * width)
            v = rows_buf[:, :, cols].reshape(D, width).astype(f32)
            centre = jnp.sum(v, axis=0, keepdims=True) * (1.0 / D)
            square = jnp.sum(v * v, axis=0, keepdims=True) * (1.0 / D)
            inverse = lax.rsqrt(square - centre * centre + EPS)
            stats_ref[0, 0:1, cols] = centre
            stats_ref[0, 1:2, cols] = inverse
            n = (v - centre) * inverse
            a = (n * (1.0 + mcol_ref[:, 1:2]) + mcol_ref[:, 0:1]).astype(bf16)
            attn_ref[0, :, cols] = a
            out = jnp.dot(wt_ref[...], a, preferred_element_type=f32) + bias_ref[...]
            qkv_ref[0, :, cols] = out.astype(bf16)

    @pl.when((s > 0) & (s <= HL))
    def _():
        h = s - 1
        gate = gate_ref[i * HL + h]

        def head(k):
            return pl.ds(pl.multiple_of((k * HL + h) * HP, HP), HP)

        keys = qkv_ref[0, head(1)].T
        sc = jnp.dot(keys, qkv_ref[0, head(0)], preferred_element_type=f32)
        top = jnp.max(sc, axis=0, keepdims=True)
        pr = jnp.exp2((sc - top) * SCALE2).astype(bf16)
        out = jnp.dot(qkv_ref[0, head(2)], pr, preferred_element_type=f32)
        total = out[HD : HD + 1]
        mixed = out * (1.0 / total)
        mixed_ref[0, head(0)] = mixed
        concat_ref[0, head(0)] = (mixed * gate).astype(bf16)
        lse_ref[0, pl.ds(h, 1)] = top * SCALE2 + jnp.log2(total)

    @pl.when(s == HL + 1)
    def _():
        for r in range(NP):
            w = w_ref[r * CB : (r + 1) * CB, w_ref.shape[1] - HL * HP :]
            part = jnp.dot(w, concat_ref[0], preferred_element_type=f32)
            if r % 2 == 0:
                own_ref[r // 2] = part
            else:
                core_out[i, r // 2] = part.astype(bf16)
        core_copy(i).start()

    for n in range(I - 1):
        at((n + 1) * steps + 1)(functools.partial(add_core, n))
        at((n + 1) * steps + HL)(functools.partial(add_x, n))

    events = [(k, d) for d in range(1, NT // 2 + 1) for k in range(NX)]
    early = [6, 7, 13, 14] if I > 2 else []
    for n, (k, d) in zip(early, events):
        at(n)(functools.partial(land_hop, k, d))

    @at(I * steps - 1)
    def _():
        if I == 1:
            start_cot()
        add_core(I - 1)
        land_cot()
        rest = events[len(early) :]
        for n, (k, d) in enumerate(rest):
            land_hop(k, d)
            if n == 0:
                add_x(I - 1)
        for n in range(I):
            back_copy(n).wait_recv()
        if I == 1:
            first_keep().wait()
        for n in range(I):
            if n:
                images.left(n)
            cot_keep(n).wait()
            for k in range(NX):
                cot_core(n, k).wait_recv()
                cot_core(n, k).wait_send()
                if k:
                    cot_x(n, k).wait_send()
        for n in range(I):
            core_copy(n).wait_send()
            back_copy(n).wait_send()
            back_keep(n).wait()
            for k in range(1, NX):
                x_copy(n, k).wait_send()
        for k in range(NX):
            keep(k).wait()
            for d in range(1, NT // 2 + 1):
                for side in range(2):
                    hop(k, d, side).wait_send()


def fwd_call(NT, NP, gate, x, cot, first, w, mods, bias, late):
    I, _, length = x.shape
    NX = NP // 2
    CB, T = D // NP, length // NX
    HL = gate.shape[0] // I
    QKV = 3 * HL * HP
    RB, FL = late.shape[2:]
    hbm = pl.BlockSpec(memory_space=pl.ANY)
    vmem = pl.BlockSpec(memory_space=pltpu.VMEM)
    dma = pltpu.SemaphoreType.DMA

    def image(*shape):
        return pl.BlockSpec((1,) + shape, lambda i, s: (i,) + (0,) * len(shape))

    return pl.pallas_call(
        functools.partial(fwd_kernel, NT, NP),
        grid=(I, HL + 2),
        in_specs=[
            pl.BlockSpec(memory_space=pltpu.SMEM),
            vmem,
            vmem,
            hbm,
            vmem,
            vmem,
            vmem,
            vmem,
        ],
        out_specs=[
            image(D, length),
            image(QKV, length),
            image(HL * HP, length),
            image(HL * HP, length),
            image(HL, length),
            image(8, length),
            hbm,
            hbm,
            hbm,
            hbm,
        ],
        out_shape=[
            jax.ShapeDtypeStruct((I, D, length), bf16),
            jax.ShapeDtypeStruct((I, QKV, length), bf16),
            jax.ShapeDtypeStruct((I, HL * HP, length), f32),
            jax.ShapeDtypeStruct((I, HL * HP, length), bf16),
            jax.ShapeDtypeStruct((I, HL, length), f32),
            jax.ShapeDtypeStruct((I, 8, length), f32),
            jax.ShapeDtypeStruct((I, 2, NX, CB, T), f32),
            jax.ShapeDtypeStruct((NX, 2, NT, RB, FL), bf16),
            jax.ShapeDtypeStruct((I, NP, CB, length), bf16),
            jax.ShapeDtypeStruct((I, NX, 2, CB, T), bf16),
        ],
        scratch_shapes=[
            pltpu.VMEM((QKV, D), bf16),
            pltpu.VMEM((NX, CB, length), f32),
            pltpu.VMEM((I, NX, CB, length), bf16),
            pltpu.VMEM((I, NX, CB, length), bf16),
            pltpu.VMEM((I, NX, NX, CB, T), bf16),
            pltpu.VMEM((I, NX, NX, CB, T), bf16),
            pltpu.VMEM((I, NX, CB, T), f32),
            pltpu.VMEM((D, 8), f32),
            dma((NX, 2, NT // 2 + 1)),
            dma((NX, 2, NT // 2 + 1)),
            dma((I,)),
            dma((I,)),
            dma((I, NX)),
            dma((I, NX)),
            dma((I,)),
            dma((I,)),
            dma((NX + I,)),
            pltpu.VMEM((NP, CB, length), bf16),
            dma((I, NX, NX)),
            dma((I, NX, NX)),
            dma((I, NX, NX)),
            dma((I, NX, NX)),
            dma((I + 1, NX)),
            dma((2, I, NX)),
            dma((2, I, NX)),
            dma((I,)),
        ],
        compiler_params=pltpu.CompilerParams(
            collective_id=2, has_side_effects=True, vmem_limit_bytes=60 * 2**20
        ),
        name="forward",
    )(gate, x, cot, first, w, mods, bias, late)


def lane_sum(v):
    total = v[:, :128]
    for j in range(1, v.shape[1] // 128):
        total = total + v[:, j * 128 : (j + 1) * 128]
    return jnp.sum(total.T, axis=0, keepdims=True)


def mlp_kernel(
    NT, NP, branch_ref, rows_ref, cot_ref, mods_ref, gate_ref, w_ref,
    lhs_ref, rhs_ref, go_ref, gms_ref, gm_ref, sums_ref, fsums_ref, out_ref, go0_ref,
    mid_ref, gn_ref, b2_ref, st_ref, gn_out, gn_in, b2_out, b2_in, o_buf,
    mcol_ref, g_send, g_recv, b_send, b_recv, x_send, x_recv, local_sem, go_buf, f_send, f_recv,
):
    NX = NP // 2
    _, _, D_, T = lhs_ref.shape
    CB = D // NP
    I = pl.num_programs(0)
    FL = w_ref.shape[3]
    i = pl.program_id(0)
    slot = i % 2
    t, p = lax.axis_index("tok"), lax.axis_index("tp")
    xi = p // 2
    core = (t, xor(p, 1))

    def gn_copy(n):
        return copy_to(gn_out, gn_in.at[n % 2], g_send.at[n], g_recv.at[n], core)

    def b2_copy(n):
        return copy_to(b2_out, b2_in.at[n % 2], b_send.at[n], b_recv.at[n], core)

    def place(n):
        return out_ref.at[n, :, pl.ds(pl.multiple_of(xi * T, T), T)]

    def out_copy(n, k):
        return copy_to(
            o_buf.at[n % 2, k], place(n), x_send.at[n, k], x_recv.at[n, k], (t, xor(p, 2 * k))
        )

    def out_keep(n):
        return pltpu.make_async_copy(o_buf.at[n % 2, 0], place(n), local_sem.at[n])

    def out_left(n):
        out_keep(n).wait()
        for k in range(1, NX):
            out_copy(n, k).wait_send()

    def go_x(k, f):
        return copy_to(
            go_buf.at[f], go0_ref.at[k, f ^ k, 0], f_send.at[0, k, f], f_recv.at[0, k, f],
            (t, xor(p, 2 * k)),
        )

    def go_core(k, f):
        return copy_to(
            go0_ref.at[k, f, 0], go0_ref.at[k, f, 1], f_send.at[1, k, f], f_recv.at[1, k, f], core
        )

    @pl.when(i == 0)
    def _():
        barrier = pltpu.get_barrier_semaphore()
        peers = [core] + [(t, xor(p, 2 * k)) for k in range(1, NX)]
        for peer in peers:
            pl.semaphore_signal(barrier, inc=1, device_id=peer, device_id_type=MESH)
        pl.semaphore_wait(barrier, len(peers))

    count = out_ref.shape[0]
    for r in range(NP):
        rows = [(pl.ds(i, 1), k * ML) for k in range(6)]
        rows += [(slice(count, count + 1), 0), (slice(count, count + 1), ML)]
        mcol_ref[r * CB : (r + 1) * CB] = spread(mods_ref, r, rows, CB)

    def col(k):
        return mcol_ref[:, k : k + 1]

    width = min(256, T)
    chunks = [slice(j * width, (j + 1) * width) for j in range(T // width)]

    def branch_one(cols):
        parts = [branch_ref[0, r % 2, r // 2, :, cols] for r in range(NP)]
        return jnp.concatenate(parts, axis=0) + col(6)

    for cols in chunks:
        x = jnp.concatenate([rows_ref[0, r, :, cols] for r in range(NP)], axis=0).astype(f32)
        mid = x + col(2) * branch_one(cols)
        mid_ref[:, cols] = mid
        centre = jnp.sum(mid, axis=0, keepdims=True) * (1.0 / D)
        square = jnp.sum(mid * mid, axis=0, keepdims=True) * (1.0 / D)
        inverse = lax.rsqrt(square - centre * centre + EPS)
        st_ref[0:1, cols] = centre
        st_ref[1:2, cols] = inverse
        n = (mid - centre) * inverse
        lhs_ref[0, 0, :, cols] = (n * (1.0 + col(4)) + col(3)).astype(bf16)
        lhs_ref[0, 1, :, cols] = (col(5) * cot_ref[0, :, cols].astype(f32)).astype(bf16)

    root = math.sqrt(2.0 / math.pi)
    tile = 384
    for k in range(NX):
        for at in range(0, FL, tile):
            rows = slice(at, min(at + tile, FL))
            size = rows.stop - rows.start
            vec = [gate_ref[k, pl.ds(i, 1), rows], mods_ref[2 * k, count + 1 : count + 2, rows]]
            vec = jnp.concatenate(vec + [jnp.zeros((6, size), f32)], axis=0).T
            pre = dot(w_ref[k, 0, :, rows], lhs_ref[0, 0], 0, 0) + vec[:, 1:2]
            grad_hid = dot(w_ref[k, 1, :, rows], lhs_ref[0, 1], 0, 0)
            gate = vec[:, 0:1]
            square = pre * pre
            inner = jnp.tanh(pre * (root + (root * 0.044715) * square))
            half = 0.5 * (1.0 + inner)
            act = pre * half
            slope = half + (0.5 * pre) * (1.0 - inner * inner) * (root + (3.0 * root * 0.044715) * square)
            rhs_ref[0, 1, k, rows] = (act * gate).astype(bf16)
            grad_pre = (slope * gate * grad_hid).astype(bf16)
            rhs_ref[0, 0, k, rows] = grad_pre
            to = slice(k * FL + rows.start, k * FL + rows.stop)
            fsums_ref[0, 0:1, to] = lane_sum(grad_pre.astype(f32))
            fsums_ref[0, 1:2, to] = lane_sum(grad_hid * act)

    def product(u, r):
        total = 0.0
        for k in range(NX):
            w = w_ref[k, u, r * CB : (r + 1) * CB]
            total = total + jnp.dot(w, rhs_ref[0, u, k], preferred_element_type=f32)
        return total

    for r in range(NP):
        v = product(0, r)
        gn_ref[r * CB : (r + 1) * CB] = v
        gn_out[r * CB : (r + 1) * CB] = v.astype(bf16)
    gn_copy(i).start()
    for r in range(NP):
        v = product(1, r)
        if r % 2:
            b2_out[r // 2] = v.astype(bf16)
        else:
            b2_ref[r // 2] = v
    b2_copy(i).start()

    gn_copy(i).wait_recv()
    gn_copy(i).wait_send()
    for r in range(NP):
        mine, theirs = slice(r * CB, (r + 1) * CB), slice((r ^ 1) * CB, ((r ^ 1) + 1) * CB)
        gn_ref[mine] = gn_ref[mine] + gn_in[slot, theirs].astype(f32)
    totals = [0.0] * 5

    def fold(v):
        total = v[:, :128]
        for j in range(1, v.shape[1] // 128):
            total = total + v[:, j * 128 : (j + 1) * 128]
        return total

    for cols in chunks:
        gnorm = gn_ref[:, cols]
        inverse = st_ref[1:2, cols]
        n = (mid_ref[:, cols] - st_ref[0:1, cols]) * inverse
        g = gnorm * (1.0 + col(4))
        mean_g = jnp.sum(g, axis=0, keepdims=True) * (1.0 / D)
        mean_gn = jnp.sum(g * n, axis=0, keepdims=True) * (1.0 / D)
        grad_mid = cot_ref[0, :, cols].astype(f32) + inverse * (g - mean_g - n * mean_gn)
        grad_one = (col(2) * grad_mid).astype(bf16)
        go_ref[0, :, cols] = grad_one
        gm_ref[0, :, cols] = grad_mid[:CB]
        for k in range(NX):
            gms_ref[0, k, :, cols] = grad_mid[2 * k * CB : (2 * k + 1) * CB].astype(bf16)
        terms = (
            grad_mid * branch_one(cols),
            gnorm,
            gnorm * n,
            grad_one.astype(f32),
            lhs_ref[0, 1, :, cols].astype(f32),
        )
        totals = [a + fold(b) for a, b in zip(totals, terms)]
    @pl.when(i == 0)
    def _():
        for f in range(NX):
            go_buf[f] = go_ref[0, 2 * f * CB : (2 * f + 1) * CB]
        for k in range(1, NX):
            for f in range(NX):
                go_x(k, f).start()

    for row, v in enumerate(totals):
        sums_ref[0, row : row + 1, :] = jnp.sum(v.T, axis=0, keepdims=True)

    @pl.when(i >= 2)
    def _():
        out_left(i - 2)

    b2_copy(i).wait_recv()
    b2_copy(i).wait_send()
    for f in range(NX):
        rows = slice(2 * f * CB, (2 * f + 1) * CB)
        v = b2_ref[f] + b2_in[slot, f].astype(f32) + mcol_ref[rows, 7:8]
        sums_ref[0, 5 : 6, f * CB : (f + 1) * CB] = lane_sum(cot_ref[0, rows].astype(f32) * v)
        o_buf[slot, f] = (mid_ref[rows] + mcol_ref[rows, 5:6] * v).astype(bf16)
    out_keep(i).start()
    for k in range(1, NX):
        out_copy(i, k).start()

    @pl.when(i == I - 1)
    def _():
        for k in range(1, NX):
            for f in range(NX):
                go_x(k, f ^ k).wait_recv()
                go_core(k, f).start()
        for n in range(x_send.shape[0]):
            for k in range(1, NX):
                out_copy(n, k).wait_recv()
            if n >= x_send.shape[0] - 2:
                out_left(n)
        for k in range(1, NX):
            for f in range(NX):
                go_core(k, f).wait_recv()
                go_core(k, f).wait_send()
                go_x(k, f).wait_send()


def mlp_call(NT, NP, branch, rows, cot, mods, gates, w):
    I, NX = branch.shape[0], NP // 2
    CB, T = branch.shape[3:]
    FL = w.shape[3]
    hbm = pl.BlockSpec(memory_space=pl.ANY)
    vmem = pl.BlockSpec(memory_space=pltpu.VMEM)
    dma = pltpu.SemaphoreType.DMA

    def image(*shape):
        return pl.BlockSpec((1,) + shape, lambda i: (i,) + (0,) * len(shape))

    return pl.pallas_call(
        functools.partial(mlp_kernel, NT, NP),
        grid=(I,),
        in_specs=[
            pl.BlockSpec(
                (1, 2, NX, CB, T), lambda i: (i, 0, 0, 0, 0), pipeline_mode=pl.Buffered(buffer_count=1)
            ),
            image(NP, CB, T),
            image(D, T),
            vmem,
            vmem,
            vmem,
        ],
        out_specs=[
            image(2, D, T),
            image(2, NX, FL, T),
            image(D, T),
            image(NX, CB, T),
            image(CB, T),
            image(8, D),
            image(8, NX * FL),
            hbm,
            hbm,
        ],
        out_shape=[
            jax.ShapeDtypeStruct((I, 2, D, T), bf16),
            jax.ShapeDtypeStruct((I, 2, NX, FL, T), bf16),
            jax.ShapeDtypeStruct((I, D, T), bf16),
            jax.ShapeDtypeStruct((I, NX, CB, T), bf16),
            jax.ShapeDtypeStruct((I, CB, T), f32),
            jax.ShapeDtypeStruct((I, 8, D), f32),
            jax.ShapeDtypeStruct((I, 8, NX * FL), f32),
            jax.ShapeDtypeStruct((I, CB, NX * T), bf16),
            jax.ShapeDtypeStruct((NX, NX, 2, CB, T), bf16),
        ],
        scratch_shapes=[
            pltpu.VMEM((D, T), f32),
            pltpu.VMEM((D, T), f32),
            pltpu.VMEM((NX, CB, T), f32),
            pltpu.VMEM((8, T), f32),
            pltpu.VMEM((D, T), bf16),
            pltpu.VMEM((2, D, T), bf16),
            pltpu.VMEM((NX, CB, T), bf16),
            pltpu.VMEM((2, NX, CB, T), bf16),
            pltpu.VMEM((2, NX, CB, T), bf16),
            pltpu.VMEM((D, 8), f32),
            dma((I,)),
            dma((I,)),
            dma((I,)),
            dma((I,)),
            dma((I, NX)),
            dma((I, NX)),
            dma((I,)),
            pltpu.VMEM((NX, CB, T), bf16),
            dma((2, NX, NX)),
            dma((2, NX, NX)),
        ],
        compiler_params=pltpu.CompilerParams(
            collective_id=3, has_side_effects=True, vmem_limit_bytes=60 * 2**20
        ),
        name="feed_forward",
    )(branch, rows, cot, mods, gates, w)


def grads_kernel(lhs_ref, rhs_ref, out_ref):
    I, _, rows, _ = lhs_ref.shape
    NT, RB = out_ref.shape[2:4]
    for b in range(0, NT, 2):
        total = 0.0
        for i in range(I):
            a = lhs_ref[i, 0, b * RB : (b + 2) * RB]
            total = total + dot(a, rhs_ref[i, 0, 0], 1, 1)
        out_ref[0, 0, b : b + 2] = total.astype(bf16).reshape(2, RB, -1)


def grads_call(NT, lhs, rhs):
    I, _, NX, FL, T = rhs.shape
    RB = D // NT
    return pl.pallas_call(
        grads_kernel,
        grid=(2, NX),
        in_specs=[
            pl.BlockSpec((I, 1, D, T), lambda u, k: (0, u, 0, 0)),
            pl.BlockSpec((I, 1, 1, FL, T), lambda u, k: (0, u, k, 0, 0)),
        ],
        out_specs=pl.BlockSpec((1, 1, NT, RB, FL), lambda u, k: (k, u, 0, 0, 0)),
        out_shape=jax.ShapeDtypeStruct((NX, 2, NT, RB, FL), bf16),
        compiler_params=pltpu.CompilerParams(vmem_limit_bytes=48 * 2**20),
        name="late_grads",
    )(lhs, rhs)


def bwd_kernel(
    NT, NP, gate_ref, go_ref, go0_ref, gms_ref, gm_ref, qkv_ref, mixed_ref, lse_ref, concat_ref, attn_ref,
    rows_ref, stats_ref, scale_ref, w_ref, late_ref, base_ref, factor_ref, ada_ref,
    gin_ref, late_out, gqkv_ref, gout_ref, lasts_ref, cond_ref, gox_ref,
    go_buf, gmx_ref, own_ref, core_out, core_in, x_out, x_in, gn_ref, accq_ref, acco_ref, wt_ref,
    gc_ref, dqkv_ref, rows_buf, gin_buf, st_out, st_in, msg_ref, heads_ref, qv_ref,
    l_own, l_out, l_in, lx_out, lx_in, q_out, q_in, part_ref, sum_ref, lasts_buf,
    g_send, g_recv, c_send, c_recv, x_send, x_recv, t_send, t_recv, l_send, l_recv, lx_send, lx_recv,
    q_send, q_recv, s_send, s_recv, m_send, m_recv, m2_send, m2_recv, local_sem, own_sem,
):
    NX, SUB = NP // 2, NT // NP
    I, CB, T = gm_ref.shape
    HL = gate_ref.shape[0] // I
    QKV, HO = 3 * HL * HP, HL * HP
    RB = D // NT
    HOPS = NT // 2
    steps = HL + 2
    i, s = pl.program_id(0), pl.program_id(1)
    flat = i * steps + s
    t, p = lax.axis_index("tok"), lax.axis_index("tp")
    xi = p // 2
    ring = Ring(NT)
    q = ring.place(t)
    right, left = (ring.tok(q + 1), p), (ring.tok(q - 1), p)
    core = (t, xor(p, 1))

    def at(n):
        return pl.when(flat == n)

    def partner(k):
        return (t, xor(p, 2 * k))

    def where(tt):
        out = 0
        for r in range(NP):
            out = out + jnp.where(p == r, xor(tt // SUB, r), 0)
        return out * SUB + tt % SUB

    def go_x(n, k, f):
        return copy_to(
            go_ref.at[n, f, 0], gox_ref.at[n, k, f ^ k, 0], g_send.at[0, n, k, f],
            g_recv.at[0, n, k, f], partner(k),
        )

    def go_core(n, k, f):
        return copy_to(
            gox_ref.at[n, k, f, 0], gox_ref.at[n, k, f, 1], g_send.at[1, n, k, f],
            g_recv.at[1, n, k, f], core,
        )

    def gm_x(n, k):
        return copy_to(gms_ref.at[n, k], gmx_ref.at[n, k - 1], m_send.at[n, k], m_recv.at[n, k], partner(k))

    def send_go(n):
        for k in range(1, NX):
            for f in range(NX):
                go_x(n, k, f).start()

    def pass_go(n):
        for k in range(1, NX):
            for f in range(NX):
                go_x(n, k, f ^ k).wait_recv()
                go_core(n, k, f).start()
        if n + 1 < I:
            send_go(n + 1)
        for m in [n - 1] if n + 1 < I else [n - 1, n]:
            if m >= 0:
                for k in range(1, NX):
                    gm_x(m, k).start()

    def load_go(n):
        def load(k):
            src = go_ref.at[n] if k == 0 else gox_ref.at[n, k] if n else go0_ref.at[k]
            return pltpu.make_async_copy(src, go_buf.at[k], local_sem.at[k])

        load(0).start()
        for k in range(1, NX):
            for f in range(NX if n else 0):
                go_core(n, k, f).wait_recv()
            load(k).start()
        for k in range(NX):
            load(k).wait()

    def rows_copy(n):
        return pltpu.make_async_copy(rows_ref.at[n, 0], rows_buf.at[n], local_sem.at[NX + n])

    def core_copy(n):
        return copy_to(core_out, core_in.at[n % 2], c_send.at[n], c_recv.at[n], core)

    def x_copy(n, k):
        return copy_to(
            x_out.at[n % 2, k - 1], x_in.at[n % 2, k - 1], x_send.at[n, k], x_recv.at[n, k], partner(k)
        )

    def st_copy(n, r):
        return copy_to(
            st_out.at[n], st_in.at[n, r], t_send.at[n, r], t_recv.at[n, r], (t, xor(p, r))
        )

    def gin_copy(n, j):
        to = pl.ds(pl.multiple_of(xor(xi, j) * T, T), T)
        return pltpu.make_async_copy(
            gin_buf.at[n % 2, :, pl.ds(j * T, T)], gin_ref.at[n, :, to], local_sem.at[NX + I + n * NX + j]
        )

    def add_core(n):
        core_copy(n).wait_recv()
        if n >= 2:
            for k in range(1, NX):
                x_copy(n - 2, k).wait_send()
        for f in range(NX):
            v = own_ref[f] + core_in[n % 2, f].astype(f32)
            if f == 0:
                gn_ref[...] = v
            else:
                x_out[n % 2, f - 1] = v.astype(bf16)
        for k in range(1, NX):
            x_copy(n, k).start()

    def tokens(v):
        total = v[:, :128]
        for j in range(1, LEN // 128):
            total = total + v[:, j * 128 : (j + 1) * 128]
        return jnp.sum(total.T, axis=0, keepdims=True)

    def own_scale(n):
        return 1.0 + scale_ref[0, :, ML : 2 * ML].T[:CB, n : n + 1]

    def normed(n):
        return (rows_buf[n].astype(f32) - stats_ref[n, 0:1]) * stats_ref[n, 1:2]

    def add_x(n):
        for k in range(1, NX):
            x_copy(n, k).wait_recv()
        for j in range(NX):
            v = gn_ref[:, j * T : (j + 1) * T]
            for k in range(1, NX):
                v = v + x_in[n % 2, k - 1, :, (j ^ k) * T : ((j ^ k) + 1) * T].astype(f32)
            gn_ref[:, j * T : (j + 1) * T] = v
        v = gn_ref[...]
        vn = v * normed(n)
        scale = own_scale(n)
        st_out[n, 0:1] = jnp.sum(v * scale, axis=0, keepdims=True)
        st_out[n, 1:2] = jnp.sum(vn * scale, axis=0, keepdims=True)
        for r in range(1, NP):
            st_copy(n, r).start()
        msg_ref[n : n + 1, :CB] = tokens(v)
        msg_ref[n : n + 1, ML : ML + CB] = tokens(vn)

    def add_stats(n):
        for r in range(1, NP):
            st_copy(n, r).wait_recv()
        if n >= 2:
            for j in range(NX):
                gin_copy(n - 2, j).wait()
        for k in range(1, NX):
            gm_x(n, k).wait_recv()
        for j in range(NX):
            cols = slice(j * T, (j + 1) * T)
            a, b = st_out[n, 0:1, cols], st_out[n, 1:2, cols]
            for r in range(1, NP):
                m = j ^ (r // 2)
                a = a + st_in[n, r, 0:1, m * T : (m + 1) * T]
                b = b + st_in[n, r, 1:2, m * T : (m + 1) * T]
            centre, inverse = stats_ref[n, 0:1, cols], stats_ref[n, 1:2, cols]
            nrm = (rows_buf[n, :, cols].astype(f32) - centre) * inverse
            g = gn_ref[:, cols] * own_scale(n)
            mid = gm_ref[n] if j == 0 else gmx_ref[n, j - 1].astype(f32)
            gin_buf[n % 2, :, cols] = mid + inverse * (g - a * (1.0 / D) - nrm * (b * (1.0 / D)))
        for j in range(NX):
            gin_copy(n, j).start()

    def l_block(side, h):
        d = HOPS - h
        return where(ring.tok(q + d if side == 0 else q - d))

    def l_load(k, side, h):
        return pltpu.make_async_copy(
            late_ref.at[k, :, l_block(side, h)], l_own.at[k, side], own_sem.at[k, side]
        )

    def l_hop(k, side, h):
        to = left if side else right
        if h == 0:
            return copy_to(
                late_ref.at[k, side, l_block(side, 0)], l_in.at[k, side, 0, side],
                l_send.at[k, side, h], l_recv.at[k, side, h], to,
            )
        return copy_to(
            l_out.at[k, side], l_in.at[k, side, h % 2], l_send.at[k, side, h], l_recv.at[k, side, h], to
        )

    def l_event(k, h):
        for side in range(2):
            l_hop(k, side, h - 1).wait_recv()
        for side in range(2):
            if h < HOPS or side == 0:
                l_load(k, side, h).wait()
            if 1 < h < HOPS:
                l_hop(k, side, h - 1).wait_send()
        if h < HOPS:
            for side in range(2):
                for u in range(2):
                    v = l_own[k, side, u]
                    if h > 1 or u == side:
                        v = (v.astype(f32) + l_in[k, side, (h - 1) % 2, u].astype(f32)).astype(bf16)
                    l_out[k, side, u] = v
            for side in range(2):
                l_hop(k, side, h).start()
                if h + 1 < HOPS or side == 0:
                    l_load(k, side, h + 1).start()
        else:
            for u in range(2):
                v = l_own[k, 0, u].astype(f32)
                for side in range(2):
                    if HOPS > 1 or u == side:
                        v = v + l_in[k, side, (h - 1) % 2, u].astype(f32)
                if k == 0:
                    late_out[u] = v
                else:
                    lx_out[k - 1, u] = v.astype(bf16)
            if k:
                lx_copy(k).start()

    def lx_copy(k):
        return copy_to(lx_out.at[k - 1], lx_in.at[k - 1], lx_send.at[k], lx_recv.at[k], partner(k))

    half = (QKV // 2 + 127) // 128 * 128

    def q_block(side, h):
        return l_block(side, h)

    def q_hop(side, h):
        to = left if side else right
        return copy_to(
            q_out.at[side], q_in.at[side, h % 2], q_send.at[side, h], q_recv.at[side, h], to
        )

    def q_event(h):
        if h:
            for side in range(2):
                q_hop(side, h - 1).wait_recv()
        if h < HOPS:
            for side in range(2):
                if h:
                    q_hop(side, h - 1).wait_send()
                block = q_block(side, h)
                a, b = accq_ref[block], acco_ref[block]
                if h:
                    a = a + q_in[side, (h - 1) % 2, :, :QKV].astype(f32)
                    b = b + q_in[side, (h - 1) % 2, :, QWIDE:].astype(f32)
                else:
                    lane = lax.broadcasted_iota(jnp.int32, a.shape, 1)
                    a = jnp.where((lane < half) if side == 0 else (lane >= half), a, 0.0)
                    b = b if side == 0 else jnp.zeros_like(b)
                q_out[side, :, :QKV] = a.astype(bf16)
                q_out[side, :, QWIDE:] = b.astype(bf16)
            for side in range(2):
                q_hop(side, h).start()
        else:
            a, b = accq_ref[q_block(0, h)], acco_ref[q_block(0, h)]
            for side in range(2):
                a = a + q_in[side, (h - 1) % 2, :, :QKV].astype(f32)
                b = b + q_in[side, (h - 1) % 2, :, QWIDE:].astype(f32)
            gqkv_ref[...] = a
            gout_ref[...] = b

    QWIDE = (QKV + 127) // 128 * 128

    pieces = ((1024, 6 * ML - 1024), (0, 1024), (6 * ML, 128))

    def last_copy(k, n):
        lanes = pl.ds(*pieces[n])
        return copy_to(
            msg_ref.at[:, lanes], lasts_buf.at[k, :, lanes], m2_send.at[n, k], m2_recv.at[n, k],
            ((t + k) % NT, p),
        )

    def part_copy(k):
        return copy_to(
            part_ref.at[k], sum_ref.at[0, t], s_send.at[1, k], s_recv.at[1, k], ((t + NT - k) % NT, p)
        )

    def sum_copy(r):
        return copy_to(sum_ref.at[0], sum_ref.at[r], s_send.at[2, r], s_recv.at[2, r], (t, xor(p, r)))

    def cond_first():
        msg_ref[I : I + 1, :QKV] = qv_ref[0:1, :QKV]
        msg_ref[:, 6 * ML :] = msg_ref[:, 6 * ML :] + heads_ref[...] * factor_ref[...]
        for k in range(1, NT):
            last_copy(k, 1).start()
            last_copy(k, 2).start()
        lasts_buf[0] = msg_ref[...]

    def cond_second():
        for k in range(1, NT):
            for n in range(3):
                last_copy(k, n).wait_recv()
        lasts_ref[...] = lasts_buf[...]
        grads = lasts_buf[...].reshape(NT * 8, -1)
        total = 0.0
        for k in range(6):
            g = grads[:, k * ML : (k + 1) * ML]
            high = g.astype(bf16)
            low = (g - high.astype(f32)).astype(bf16)
            total = total + dot(high, ada_ref[k], 1, 1) + dot(low, ada_ref[k], 1, 1)
        part_ref[...] = jnp.zeros_like(part_ref)
        part_ref[:, :, :RB] = total.reshape(NT, 8, RB)
        for k in range(1, NT):
            part_copy(k).start()
        sum_ref[0, t] = part_ref[0]

    def cond_third():
        for k in range(1, NT):
            part_copy(k).wait_recv()
        for r in range(1, NP):
            sum_copy(r).start()

    def cond_last():
        total = sum_ref[0]
        for r in range(1, NP):
            sum_copy(r).wait_recv()
            total = total + sum_ref[r]
        cond_ref[...] = total

    def finish_core():
        if I > 1:
            add_x(I - 2)
            add_stats(I - 2)
        add_core(I - 1)

    @at(0)
    def _():
        greet(t, p, NT, NP)
        if I > 1:
            send_go(1)
        for k in range(NX):
            for side in range(2):
                l_hop(k, side, 0).start()
                l_load(k, side, 1).start()
        for n in range(I):
            rows_copy(n).start()
        msg_ref[...] = base_ref[...]
        for k in range(1, NT):
            last_copy(k, 0).start()
        heads_ref[...] = jnp.zeros_like(heads_ref)
        qv_ref[...] = jnp.zeros_like(qv_ref)
        wt_ref[...] = w_ref[:, w_ref.shape[1] - HO :].T
        accq_ref[...] = jnp.zeros_like(accq_ref)
        acco_ref[...] = jnp.zeros_like(acco_ref)
        for n in range(I):
            rows_copy(n).wait()

    for n in range(I):
        if n:
            at((n - 1) * steps + HL)(functools.partial(pass_go, n))
        at(n * steps)(functools.partial(load_go, n))

    @pl.when(s == 0)
    def _():
        for k in range(NX):
            v = go_buf[k].reshape(D, T)
            gc_ref[:, k * T : (k + 1) * T] = jnp.dot(wt_ref[...], v, preferred_element_type=f32)

    @pl.when((s > 0) & (s <= HL))
    def _():
        h = s - 1
        gate = gate_ref[i * HL + h]

        def head(k):
            return pl.ds(pl.multiple_of((k * HL + h) * HP, HP), HP)

        keys_t = qkv_ref[0, head(1)]
        keys = keys_t.T
        values = qkv_ref[0, head(2)].T
        gc = gc_ref[head(0)]
        inner = jnp.sum(mixed_ref[0, head(0)] * gc, axis=0, keepdims=True)
        lane = lax.broadcasted_iota(jnp.int32, (1, 128), 1)
        row = heads_ref[pl.ds(i, 1)]
        heads_ref[pl.ds(i, 1)] = row + jnp.where(lane == h, jnp.sum(inner), 0.0)
        delta = gate * inner
        grad = (gate * gc).astype(bf16)
        lse = lse_ref[0, pl.ds(h, 1)]
        queries = qkv_ref[0, head(0)]
        dv = jnp.zeros((LEN, HP), f32)
        dk = jnp.zeros((LEN, HP), f32)
        chunk = 256
        for j in range(LEN // chunk):
            part = slice(j * chunk, (j + 1) * chunk)
            qj = queries[:, part]
            do = grad[:, part]
            sc = jnp.dot(keys, qj, preferred_element_type=f32)
            pr = jnp.exp2(sc * SCALE2 - lse[:, part])
            dp = jnp.dot(values, do, preferred_element_type=f32)
            ds = (pr * (dp - delta[:, part])).astype(bf16)
            dv = dv + jnp.dot(pr.astype(bf16), do.T, preferred_element_type=f32)
            dk = dk + jnp.dot(ds, qj.T, preferred_element_type=f32)
            dq = jnp.dot(keys_t, ds, preferred_element_type=f32)
            dqkv_ref[head(0), part] = (dq * SCALE).astype(bf16)
        dqkv_ref[head(1)] = (dk * SCALE).T.astype(bf16)
        dqkv_ref[head(2)] = dv.T.astype(bf16)

    @pl.when(s == HL + 1)
    def _():
        for n in range(1, I):
            at(n * steps + HL + 1)(lambda n=n: core_copy(n - 1).wait_send())
        for r in range(NP):
            w = w_ref[r * CB : (r + 1) * CB, :QKV]
            part = jnp.dot(w, dqkv_ref[...], preferred_element_type=f32)
            if r % 2 == 0:
                own_ref[r // 2] = part
            else:
                core_out[r // 2] = part.astype(bf16)
        for n in range(I):
            at(n * steps + HL + 1)(lambda n=n: core_copy(n).start())
        for b in range(0, NT, 2):
            rows = slice(b * RB, (b + 2) * RB)
            v = dot(attn_ref[0, rows], dqkv_ref[...], 1, 1)
            accq_ref[b : b + 2] = accq_ref[b : b + 2] + v.reshape(2, RB, QKV)
        at(I * steps - 1)(functools.partial(finish_core))
        for b in range(0, NT, 2):
            rows = slice(b * RB, (b + 2) * RB)
            v = 0.0
            for k in range(NX):
                g = go_buf[k].reshape(D, T)[rows]
                v = v + dot(g, concat_ref[0, :, k * T : (k + 1) * T], 1, 1)
            acco_ref[b : b + 2] = acco_ref[b : b + 2] + v.reshape(2, RB, HO)
        qv_ref[0:1, :QKV] = qv_ref[0:1, :QKV] + tokens(dqkv_ref[...].astype(f32))

    for n in range(I - 1):
        at((n + 1) * steps + 1)(functools.partial(add_core, n))
        if n + 2 < I:
            at((n + 1) * steps + HL + 1)(functools.partial(add_x, n))
        if n + 2 < I:
            at((n + 2) * steps)(functools.partial(add_stats, n))

    events = [
        functools.partial(l_event, k, h) for h in range(1, HOPS + 1) for k in reversed(range(NX))
    ]
    early = [2, 3, 8, 9, 13, 14] if I > 2 else []
    early = early[: len(events)]
    for n, event in zip(early, events):
        at(n)(event)

    @at(I * steps - 1)
    def _():
        rest = events[len(early) :]
        q_event(0)
        todo = [functools.partial(add_x, I - 1), cond_first, functools.partial(q_event, 1)]
        todo += [functools.partial(add_stats, I - 1), cond_second]
        todo += rest[:-1] + [functools.partial(q_event, 2), cond_third] + rest[-1:]
        todo += [functools.partial(q_event, h) for h in range(3, HOPS)] + [cond_last]
        todo += [functools.partial(q_event, HOPS)]
        for step in todo:
            step()
        for k in range(1, NX):
            lx_copy(k).wait_recv()
            for u in range(2):
                late_out[u] = late_out[u] + lx_in[k - 1, u].astype(f32)
        core_copy(I - 1).wait_send()
        for n in range(I):
            for k in range(1, NX):
                gm_x(n, k).wait_send()
                for f in range(NX if n else 0):
                    go_x(n, k, f).wait_send()
                    go_core(n, k, f).wait_send()
                if n >= I - 2:
                    x_copy(n, k).wait_send()
            for r in range(1, NP):
                st_copy(n, r).wait_send()
            if n >= I - 2:
                for j in range(NX):
                    gin_copy(n, j).wait()
        for k in range(NX):
            for side in range(2):
                l_hop(k, side, 0).wait_send()
                if HOPS > 1:
                    l_hop(k, side, HOPS - 1).wait_send()
        for side in range(2):
            q_hop(side, HOPS - 1).wait_send()
        for k in range(1, NX):
            lx_copy(k).wait_send()
        for k in range(1, NT):
            for n in range(3):
                last_copy(k, n).wait_send()
            part_copy(k).wait_send()
        for r in range(1, NP):
            sum_copy(r).wait_send()


def bwd_call(
    NT, NP, gate, go, go0, gms, gm, qkv, mixed, lse, concat, attn, rows, stats, scale, w, late, base, factor, ada
):
    I, CB, T = gm.shape
    NX = NP // 2
    length = attn.shape[2]
    HL = gate.shape[0] // I
    QKV, HO = 3 * HL * HP, HL * HP
    QWIDE = (QKV + 127) // 128 * 128
    RB, FL = late.shape[3:]
    HOPS = NT // 2
    hbm = pl.BlockSpec(memory_space=pl.ANY)
    vmem = pl.BlockSpec(memory_space=pltpu.VMEM)
    dma = pltpu.SemaphoreType.DMA
    once = pl.Buffered(buffer_count=1)

    def image(*shape):
        return pl.BlockSpec(
            (1,) + shape, lambda i, s: (i,) + (0,) * len(shape), pipeline_mode=once
        )

    return pl.pallas_call(
        functools.partial(bwd_kernel, NT, NP),
        grid=(I, HL + 2),
        in_specs=[
            pl.BlockSpec(memory_space=pltpu.SMEM),
            hbm,
            hbm,
            hbm,
            vmem,
            image(QKV, length),
            image(HO, length),
            image(HL, length),
            image(HO, length),
            image(D, length),
            hbm,
            vmem,
            vmem,
            vmem,
            hbm,
            vmem,
            vmem,
            vmem,
        ],
        out_specs=[hbm, vmem, vmem, vmem, vmem, vmem, hbm],
        out_shape=[
            jax.ShapeDtypeStruct((I, CB, length), f32),
            jax.ShapeDtypeStruct((2, RB, FL), f32),
            jax.ShapeDtypeStruct((RB, QKV), f32),
            jax.ShapeDtypeStruct((RB, HO), f32),
            jax.ShapeDtypeStruct((NT,) + base.shape, f32),
            jax.ShapeDtypeStruct((NT, 8, 256), f32),
            jax.ShapeDtypeStruct((I, NX, NX, 2, CB, T), bf16),
        ],
        scratch_shapes=[
            pltpu.VMEM((NX, NX, 2, CB, T), bf16),
            pltpu.VMEM((I, NX - 1, CB, T), bf16),
            pltpu.VMEM((NX, CB, length), f32),
            pltpu.VMEM((NX, CB, length), bf16),
            pltpu.VMEM((2, NX, CB, length), bf16),
            pltpu.VMEM((2, NX - 1, CB, length), bf16),
            pltpu.VMEM((2, NX - 1, CB, length), bf16),
            pltpu.VMEM((CB, length), f32),
            pltpu.VMEM((NT, RB, QKV), f32),
            pltpu.VMEM((NT, RB, HO), f32),
            pltpu.VMEM((HO, D), bf16),
            pltpu.VMEM((HO, length), f32),
            pltpu.VMEM((QKV, length), bf16),
            pltpu.VMEM((I, CB, length), bf16),
            pltpu.VMEM((2, CB, length), f32),
            pltpu.VMEM((I, 8, length), f32),
            pltpu.VMEM((I, NP, 8, length), f32),
            pltpu.VMEM(base.shape, f32),
            pltpu.VMEM((8, 128), f32),
            pltpu.VMEM((8, QWIDE), f32),
            pltpu.VMEM((NX, 2, 2, RB, FL), bf16),
            pltpu.VMEM((NX, 2, 2, RB, FL), bf16),
            pltpu.VMEM((NX, 2, 2, 2, RB, FL), bf16),
            pltpu.VMEM((NX - 1, 2, RB, FL), bf16),
            pltpu.VMEM((NX - 1, 2, RB, FL), bf16),
            pltpu.VMEM((2, RB, QWIDE + HO), bf16),
            pltpu.VMEM((2, 2, RB, QWIDE + HO), bf16),
            pltpu.VMEM((NT, 8, 256), f32),
            pltpu.VMEM((NP, NT, 8, 256), f32),
            pltpu.VMEM((NT,) + base.shape, f32),
            dma((2, I, NX, NX)),
            dma((2, I, NX, NX)),
            dma((I,)),
            dma((I,)),
            dma((I, NX)),
            dma((I, NX)),
            dma((I, NP)),
            dma((I, NP)),
            dma((NX, 2, HOPS)),
            dma((NX, 2, HOPS)),
            dma((NX,)),
            dma((NX,)),
            dma((2, HOPS)),
            dma((2, HOPS)),
            dma((3, max(NT, NP))),
            dma((3, max(NT, NP))),
            dma((I, NX)),
            dma((I, NX)),
            dma((3, NT)),
            dma((3, NT)),
            dma((NX + I + I * NX,)),
            dma((NX, 2)),
        ],
        compiler_params=pltpu.CompilerParams(
            collective_id=1, has_side_effects=True, vmem_limit_bytes=63 * 2**20
        ),
        name="backward",
    )(gate, go, go0, gms, gm, qkv, mixed, lse, concat, attn, rows, stats, scale, w, late, base, factor, ada)


def make_body(NT, NP):
    NX = NP // 2
    SUB = NT // NP
    RB = D // NT
    CB = D // NP
    T = LEN // NX

    def tp_xor(v, r):
        return lax.ppermute(v, "tp", [(p, p ^ r) for p in range(NP)])

    def body(
        block_input,
        condition,
        timesteps,
        head_mask,
        group_mask,
        w_ada,
        b_ada,
        w_qkv,
        b_qv,
        w_out,
        b_out,
        w_up,
        b_up,
        w_down,
        b_down,
        w_head,
        b_head,
        w_group,
        b_group,
        cotangent,
    ):
        I = condition.shape[0]
        HL = head_mask.shape[1]
        GL = group_mask.shape[1]
        FL = w_up.shape[1]
        FR = FREQ // NT
        t = lax.axis_index("tok")
        p = lax.axis_index("tp")
        xi = p // 2

        qkv_shard = jnp.pad(
            w_qkv.reshape(RB, 3, HL, HD), ((0, 0), (0, 0), (0, 0), (0, HP - HD))
        ).reshape(RB, 3 * HL * HP)
        out_shard = jnp.pad(w_out.T.reshape(RB, HL, HD), ((0, 0), (0, 0), (0, HP - HD))).reshape(
            RB, HL * HP
        )
        QKV = 3 * HL * HP
        gap = -QKV % 128
        early_shard = jnp.concatenate(
            [qkv_shard, jnp.zeros((RB, gap), bf16), out_shard], axis=1
        )
        late_shard = jnp.stack([w_up, w_down.T])
        late_shards = jnp.stack(
            [late_shard] + [tp_xor(late_shard, 2 * k) for k in range(1, NX)]
        )
        time_feat = embed_time(timesteps).astype(bf16)
        cond_wide = condition.astype(f32)
        cond_act = jax.nn.silu(cond_wide).astype(bf16)
        pad8 = lambda v, width: jnp.pad(v, ((0, 8 - v.shape[0]), (0, width - v.shape[1])))
        message = jnp.concatenate(
            [
                jnp.pad(cond_act.reshape(I, NT, RB), ((0, 0), (0, 0), (0, 256 - RB))),
                jnp.pad(time_feat.reshape(I, NT, FR), ((0, 0), (0, 0), (0, ML - 256 - FR))),
            ],
            axis=2,
        )
        message = jnp.pad(message.transpose(1, 0, 2).astype(f32), ((0, 0), (0, 8 - I), (0, 0)))
        ada = jnp.pad(w_ada.transpose(1, 0, 2), ((0, 0), (0, 0), (0, ML - CB)))
        gates = jnp.concatenate([w_head, w_group], axis=1)
        gates = jnp.pad(gates, ((0, 0), (0, 128 - HL - GL)))
        wide = 6 * ML + 128
        mod_bias = jnp.concatenate(
            [jnp.pad(b_ada, ((0, 0), (0, ML - CB))).reshape(6 * ML), b_head, b_group]
        ).astype(f32)
        bias = jnp.concatenate(
            [
                jnp.broadcast_to(pad8(mod_bias[None], wide)[:1], (I, wide)),
                pad8(jnp.concatenate([jnp.pad(b_out, (0, ML - CB)), b_down]).astype(f32)[None], wide)[:1],
                pad8(b_up.astype(f32)[None], wide)[: 8 - I - 1],
            ],
            axis=0,
        )
        mask = pad8(jnp.concatenate([head_mask, group_mask], axis=1).astype(f32), 128)
        first, early_full, mods, sig, cond_all = start_call(
            NT,
            NP,
            block_input,
            early_shard,
            message,
            ada,
            gates,
            bias,
            mask,
        )
        early_full = early_full.reshape(D, -1)
        head_sig, group_sig = sig[:I, :HL], sig[:I, HL : HL + GL]
        head_gate = mods[0, :I, 6 * ML : 6 * ML + HL]
        group_rows = jnp.stack(
            [
                jnp.repeat(mods[2 * k, :, 6 * ML + HL : 6 * ML + HL + GL], GW, axis=1)
                for k in range(NX)
            ]
        )

        qv = b_qv.astype(f32).reshape(2, HL, HD)
        qv_bias = jnp.stack(
            [
                jnp.pad(qv[0], ((0, 0), (0, HP - HD))),
                jnp.zeros((HL, HP), f32),
                jnp.concatenate(
                    [qv[1], jnp.ones((HL, 1), f32), jnp.zeros((HL, HP - HD - 1), f32)], axis=1
                ),
            ]
        ).reshape(3 * HL * HP, 1)

        attn_all, qkv_all, mixed_all, concat_all, lse_all, stats_all, branch, late_full, rows_all, cots = (
            fwd_call(
                NT,
                NP,
                head_gate.reshape(-1),
                block_input,
                cotangent,
                first,
                early_full,
                mods,
                qv_bias,
                late_shards,
            )
        )
        late_full = late_full.reshape(NX, 2, D, FL)

        lhs, rhs, grad_one, grad_mid_out, grad_mid_own, sums, fsums, block_output, go_first = mlp_call(
            NT,
            NP,
            branch,
            rows_all,
            cots.reshape(I, D, T),
            mods,
            group_rows,
            late_full,
        )
        late_grads = grads_call(NT, lhs, rhs)

        gate_sums = jnp.sum(fsums[:, 1].reshape(I, NX * GL, GW), axis=2)
        up_sums = jnp.sum(fsums[:, 0], axis=0)
        all_sums = jnp.sum(sums[:, 3:5], axis=0)

        def x_message(k):
            mine = slice(2 * k * CB, (2 * k + 1) * CB)
            parts = [
                jnp.concatenate(
                    [
                        sums[:, :3, mine].reshape(I, 3 * CB),
                        sums[:, 5, k * CB : (k + 1) * CB],
                        gate_sums[:, k * GL : (k + 1) * GL],
                    ],
                    axis=1,
                ).reshape(-1),
                all_sums[:, mine].reshape(-1),
                up_sums[k * FL : (k + 1) * FL],
            ]
            return jnp.concatenate(parts)

        x_total = x_message(0)
        for k in range(1, NX):
            x_total = x_total + tp_xor(x_message(k), 2 * k)
        per = 4 * CB + GL
        per_image = x_total[: I * per].reshape(I, per)
        late_mods = per_image[:, : 4 * CB].reshape(I, 4, CB)
        grad_group_gate = per_image[:, 4 * CB :]
        bias_sums = x_total[I * per :]

        head_factor = head_mask.astype(f32) * head_sig * (1.0 - head_sig)
        group_logit = grad_group_gate * group_mask.astype(f32) * group_sig * (1.0 - group_sig)
        image_rows = jnp.concatenate(
            [
                jnp.pad(late_mods, ((0, 0), (2, 0), (0, ML - CB))).reshape(I, 6 * ML),
                jnp.zeros((I, HL), f32),
                group_logit,
                jnp.zeros((I, 128 - HL - GL), f32),
            ],
            axis=1,
        )
        widen = lambda v: jnp.pad(v, (0, wide - v.shape[0]))[None]
        base = jnp.concatenate(
            [
                image_rows,
                jnp.zeros((1, wide), f32),
                widen(bias_sums[: 2 * CB]),
                widen(bias_sums[2 * CB :]),
                jnp.zeros((8 - I - 3, wide), f32),
            ],
            axis=0,
        )
        grad_input, late, grad_qkv, grad_out, lasts, cond_sum, _ = bwd_call(
            NT,
            NP,
            head_gate.reshape(-1),
            grad_one.reshape(I, NX, 2, CB, T),
            go_first,
            grad_mid_out,
            grad_mid_own,
            qkv_all,
            mixed_all,
            lse_all,
            concat_all,
            attn_all,
            rows_all,
            stats_all,
            mods,
            early_full,
            late_grads,
            base,
            pad8(head_factor, 128),
            ada,
        )
        grad_up, grad_down = late[0], late[1]
        mods_all = (
            lasts[:, :I, : 6 * ML].reshape(NT * I, 6, ML)[:, :, :CB].reshape(NT * I, 6 * CB)
        )
        logits_all = lasts[:, :I, 6 * ML : 6 * ML + HL + GL].reshape(NT * I, HL + GL)
        bias_rows = jnp.sum(lasts[:, I : I + 3], axis=0)
        qv_rows = bias_rows[0, :QKV].reshape(3, HL, HP)[:, :, :HD].reshape(3, HL * HD)
        cond_f = cond_all[:, :I, :RB].reshape(NT * I, RB)
        time_f = cond_all[:, :I, 256 : 256 + FR].reshape(NT * I, FR)
        grad_w_ada = lax.dot_general(
            cond_f, mods_all, (((0,), (0,)), ((), ())), precision=exact_mode
        ).reshape(RB, 6, CB)
        grad_b_ada = jnp.sum(mods_all, axis=0).reshape(6, CB)
        grad_w_gates = lax.dot_general(
            time_f, logits_all, (((0,), (0,)), ((), ())), precision=exact_mode
        )
        grad_b_gates = jnp.sum(logits_all, axis=0)
        cond_total = cond_sum[:, :I, :RB].transpose(1, 0, 2).reshape(I, D)
        grad_condition = jax.vjp(jax.nn.silu, cond_wide)[1](cond_total)[0]

        return (
            block_output,
            grad_input,
            grad_condition,
            grad_w_ada,
            grad_b_ada,
            grad_qkv.reshape(RB, 3, HL, HP)[..., :HD].reshape(RB, 3, HL * HD),
            jnp.stack([qv_rows[0], qv_rows[2]]),
            grad_out.reshape(RB, HL, HP)[..., :HD].reshape(RB, HL * HD).T,
            bias_rows[1, :CB],
            grad_up,
            bias_rows[2, :FL],
            grad_down.T,
            bias_rows[1, CB : 2 * CB],
            grad_w_gates[:, :HL],
            grad_b_gates[:HL],
            grad_w_gates[:, HL:],
            grad_b_gates[HL:],
        )

    return body


def solution(mesh):
    return jax.shard_map(
        make_body(mesh.shape["tok"], mesh.shape["tp"]),
        mesh=mesh,
        in_specs=(
            P("tok", "tp", None),
            P("tok", None),
            P("tok"),
            P("tok", "tp"),
            P("tok", "tp"),
            P("tok", None, "tp"),
            P(None, "tp"),
            P("tok", None, "tp"),
            P(None, "tp"),
            P("tp", "tok"),
            P("tp"),
            P("tok", "tp"),
            P("tp"),
            P("tp", "tok"),
            P("tp"),
            P("tok", "tp"),
            P("tp"),
            P("tok", "tp"),
            P("tp"),
            P("tok", "tp", None),
        ),
        out_specs=(
            P("tok", "tp", None),
            P("tok", "tp", None),
            P("tok", None),
            P("tok", None, "tp"),
            P(None, "tp"),
            P("tok", None, "tp"),
            P(None, "tp"),
            P("tp", "tok"),
            P("tp"),
            P("tok", "tp"),
            P("tp"),
            P("tp", "tok"),
            P("tp"),
            P("tok", "tp"),
            P("tp"),
            P("tok", "tp"),
            P("tp"),
        ),
        check_vma=False,
    )
```

```python
import functools
import math

import jax
import jax.numpy as jnp
from jax import lax
from jax.experimental import pallas as pl
from jax.experimental.pallas import tpu as pltpu
from jax.sharding import PartitionSpec as P

D = 1152
HD = 72
HP = 80
FF = 4608
FREQ = 256
GROUPS = 16
GW = FF // GROUPS
LEN = 1024
EPS = 1e-06
SCALE = HD**-0.5
SCALE2 = SCALE / math.log(2.0)

f32 = jnp.float32
bf16 = jnp.bfloat16
exact_mode = lax.Precision.HIGHEST


def dot(a, b, ca, cb):
    return lax.dot_general(a, b, (((ca,), (cb,)), ((), ())), preferred_element_type=f32)


def embed_time(timesteps):
    half_width = FREQ // 2
    indices = jnp.arange(half_width, dtype=f32)
    freq_rates = jnp.exp(-math.log(10000.0) * indices / half_width)
    angles = timesteps.astype(f32)[:, None] * freq_rates[None, :]
    return jnp.concatenate([jnp.cos(angles), jnp.sin(angles)], axis=1)


MESH = pl.DeviceIdType.MESH
ML = 384


def xor(v, k):
    out, bit = 0, 1
    while bit <= k or bit <= 8:
        b = (v // bit) % 2
        out = out + bit * (1 - b if k & bit else b)
        bit *= 2
    return out


class Ring:
    def __init__(self, NT):
        self.NT, self.tall = NT, NT // 2

    def place(self, t):
        b = t % 2
        return (1 - b) * (self.tall - 1 - t // 2) + b * (self.tall + t // 2)

    def tok(self, q):
        q = (q + 2 * self.NT) % self.NT
        b = q // self.tall
        return (1 - b) * 2 * (self.tall - 1 - q) + b * (2 * (q - self.tall) + 1)


def copy_to(src, dst, send, recv, device):
    return pltpu.make_async_remote_copy(
        src_ref=src, dst_ref=dst, send_sem=send, recv_sem=recv, device_id=device, device_id_type=MESH
    )


def greet(t, p, NT, NP):
    barrier = pltpu.get_barrier_semaphore()
    for r in range(1, NP):
        pl.semaphore_signal(barrier, inc=1, device_id=(t, xor(p, r)), device_id_type=MESH)
    for k in range(1, NT):
        pl.semaphore_signal(barrier, inc=1, device_id=((t + k) % NT, p), device_id_type=MESH)
    pl.semaphore_wait(barrier, NP - 1 + NT - 1)


class ImageMoves:
    def __init__(self, NP, x_ref, rows_ref, x_send, x_recv, c_send, c_recv, local_sem):
        self.NX = NP // 2
        self.T = x_ref.shape[2] // self.NX
        self.refs = (x_ref, rows_ref)
        self.sems = (x_send, x_recv, c_send, c_recv, local_sem)
        self.t, self.p = lax.axis_index("tok"), lax.axis_index("tp")
        self.core = (self.t, xor(self.p, 1))

    def tokens(self, who, j):
        return pl.ds(pl.multiple_of(xor(who, j) * self.T, self.T), self.T)

    def src(self, i, j):
        return self.refs[0].at[i, :, pl.ds(j * self.T, self.T)]

    def x(self, i, k, j):
        x_send, x_recv = self.sems[:2]
        at = self.tokens(xor(self.p // 2, k), j)
        dst = self.refs[1].at[i, 2 * k, :, at]
        device = (self.t, xor(self.p, 2 * k))
        return copy_to(self.src(i, j), dst, x_send.at[i, k, j], x_recv.at[i, k, j], device)

    def own(self, i, j):
        dst = self.refs[1].at[i, 0, :, self.tokens(self.p // 2, j)]
        return pltpu.make_async_copy(self.src(i, j), dst, self.sems[4].at[i, j])

    def own_core(self, i, j):
        dst = self.refs[1].at[i, 1, :, self.tokens(self.p // 2, j)]
        c_send, c_recv = self.sems[2:4]
        return copy_to(self.src(i, j), dst, c_send.at[i, 0, j], c_recv.at[i, 0, j], self.core)

    def passed(self, i, k):
        rows = self.refs[1]
        c_send, c_recv = self.sems[2:4]
        return copy_to(
            rows.at[i, 2 * k], rows.at[i, 2 * k + 1], c_send.at[i, k, 0], c_recv.at[i, k, 0], self.core
        )

    def start(self, i):
        for k in range(1, self.NX):
            for j in range(self.NX):
                self.x(i, k, j).start()
        for j in range(self.NX):
            self.own(i, j).start()
            self.own_core(i, j).start()

    def land(self, i):
        for k in range(1, self.NX):
            for j in range(self.NX):
                self.x(i, k, j).wait_recv()
            self.passed(i, k).start()

    def finish(self, i):
        for j in range(self.NX):
            self.own(i, j).wait()
            self.own_core(i, j).wait_recv()
        for k in range(1, self.NX):
            self.passed(i, k).wait_recv()

    def left(self, i):
        for j in range(self.NX):
            self.own_core(i, j).wait_send()
        for k in range(1, self.NX):
            self.passed(i, k).wait_send()
            for j in range(self.NX):
                self.x(i, k, j).wait_send()


def start_kernel(
    NT, NP, x_ref, w_ref, msg_ref, ada_ref, gates_ref, bias_ref, mask_ref,
    rows_ref, full_ref, mods_ref, sig_ref, cond_ref,
    part_ref, got_ref, x_send, x_recv, c_send, c_recv, r_send, r_recv, s_send, s_recv, local_sem,
):
    NX, SUB = NP // 2, NT // NP
    WN = w_ref.shape[1]
    half = WN // 256 * 128
    t, p = lax.axis_index("tok"), lax.axis_index("tp")
    ring = Ring(NT)
    q = ring.place(t)
    right, left = (ring.tok(q + 1), p), (ring.tok(q - 1), p)

    def where(tt):
        out = 0
        for r in range(NP):
            out = out + jnp.where(p == r, xor(tt // SUB, r), 0)
        return out * SUB + tt % SUB

    greet(t, p, NT, NP)

    small = []
    for k in range(1, NT):
        peer = (t + k) % NT
        small.append(copy_to(msg_ref.at[peer], cond_ref.at[k], s_send.at[0, k], s_recv.at[0, k], (peer, p)))
        small[-1].start()

    def hop(d, to_right):
        side = 0 if to_right else 1
        block = where(ring.tok(q - (d - 1) if to_right else q + (d - 1)))
        src = w_ref if d == 1 else full_ref.at[block]
        dst = full_ref.at[block]
        if d == NT // 2:
            cols = pl.ds(0, half) if to_right else pl.ds(half, WN - half)
            src, dst = src.at[:, cols], dst.at[:, cols]
        return copy_to(src, dst, r_send.at[side, d], r_recv.at[side, d], right if to_right else left)

    hops = {}

    def start_hop(d):
        for to_right in (True, False):
            hops[d, to_right] = hop(d, to_right)
            hops[d, to_right].start()

    def land_hop(d):
        for to_right in (True, False):
            hops[d, to_right].wait_recv()

    images = ImageMoves(NP, x_ref, rows_ref, x_send, x_recv, c_send, c_recv, local_sem)
    images.start(0)
    start_hop(1)
    keep = pltpu.make_async_copy(w_ref, full_ref.at[where(t)], local_sem.at[1, 0])
    keep.start()

    cond_ref[0] = msg_ref[t]
    for cp in small:
        cp.wait_recv()
    rb, fr = ada_ref.shape[1], gates_ref.shape[0]
    feats = cond_ref[...].reshape(NT * 8, -1).astype(bf16)
    for k in range(6):
        part = jnp.dot(feats[:, :rb], ada_ref[k], preferred_element_type=f32)
        part_ref[:, :, k * ML : (k + 1) * ML] = part.reshape(NT, 8, ML)
    part = jnp.dot(feats[:, 256 : 256 + fr], gates_ref[...], preferred_element_type=f32)
    part_ref[:, :, 6 * ML :] = part.reshape(NT, 8, 128)
    for k in range(1, NT):
        peer = (t + NT - k) % NT
        cp = copy_to(part_ref.at[k], got_ref.at[k], s_send.at[1, k], s_recv.at[1, k], (peer, p))
        cp.start()
        small.append(cp)
    land_hop(1)
    start_hop(2)
    for cp in small[NT - 1 :]:
        cp.wait_recv()
    total = part_ref[0]
    for k in range(1, NT):
        total = total + got_ref[k]
    total = total + bias_ref[...]
    sig = 1.0 / (1.0 + jnp.exp(-total[:, 6 * ML :]))
    sig_ref[...] = sig
    mods_ref[0, :, : 6 * ML] = total[:, : 6 * ML]
    mods_ref[0, :, 6 * ML :] = sig * mask_ref[...]
    mods = []
    for r in range(1, NP):
        cp = copy_to(mods_ref.at[0], mods_ref.at[r], s_send.at[2, r], s_recv.at[2, r], (t, xor(p, r)))
        cp.start()
        mods.append(cp)

    images.land(0)
    for d in range(2, NT // 2 + 1):
        land_hop(d)
        if d < NT // 2:
            start_hop(d + 1)
    images.finish(0)
    for cp in mods:
        cp.wait_recv()
    keep.wait()
    images.left(0)
    for cp in small + mods + list(hops.values()):
        cp.wait_send()


def start_call(NT, NP, x, w, msg, ada, gates, bias, mask):
    _, CB, length = x.shape
    NX = NP // 2
    RB, WN = w.shape
    wide = 6 * ML + 128
    hbm, vmem = pl.BlockSpec(memory_space=pl.ANY), pl.BlockSpec(memory_space=pltpu.VMEM)
    dma = pltpu.SemaphoreType.DMA
    return pl.pallas_call(
        functools.partial(start_kernel, NT, NP),
        in_specs=[pl.BlockSpec((1, CB, length), lambda i: (0, 0, 0))] + [vmem] * 6,
        grid=(1,),
        out_specs=[hbm, hbm, vmem, vmem, vmem],
        out_shape=[
            jax.ShapeDtypeStruct((1, NP, CB, length), bf16),
            jax.ShapeDtypeStruct((NT, RB, WN), bf16),
            jax.ShapeDtypeStruct((NP, 8, wide), f32),
            jax.ShapeDtypeStruct((8, 128), f32),
            jax.ShapeDtypeStruct((NT, 8, ML), f32),
        ],
        scratch_shapes=[
            pltpu.VMEM((NT, 8, wide), f32),
            pltpu.VMEM((NT, 8, wide), f32),
            dma((1, NX, NX)),
            dma((1, NX, NX)),
            dma((1, NX, NX)),
            dma((1, NX, NX)),
            dma((2, NT // 2 + 1)),
            dma((2, NT // 2 + 1)),
            dma((3, max(NT, NP))),
            dma((3, max(NT, NP))),
            dma((2, NX)),
        ],
        compiler_params=pltpu.CompilerParams(
            collective_id=0, has_side_effects=True, vmem_limit_bytes=32 * 2**20
        ),
        name="start",
    )(x, w, msg, ada, gates, bias, mask)


def spread(mods_ref, r, rows, CB):
    parts = [mods_ref[r, row, at : at + ML] for row, at in rows]
    parts += [jnp.zeros((8 - len(parts), ML), f32)] if len(parts) < 8 else []
    return jnp.concatenate(parts, axis=0).T[:CB]


def fwd_kernel(
    NT, NP, gate_ref, x_ref, cot_ref, first_ref, w_ref, mod_ref, bias_ref, late_ref,
    attn_ref, qkv_ref, mixed_ref, concat_ref, lse_ref, stats_ref, branch_ref, full_ref, rows_ref, cots_ref,
    wt_ref, own_ref, core_out, core_in, x_out, x_in, total_ref,
    mcol_ref, l_send, l_recv, c_send, c_recv, x_send, x_recv, b_send, b_recv, local_sem,
    rows_buf, rx_send, rx_recv, rc_send, rc_recv, r_sem, t_send, t_recv, t_sem,
):
    NX, SUB = NP // 2, NT // NP
    I, CB, T = total_ref.shape[0], total_ref.shape[2], total_ref.shape[3]
    HL = gate_ref.shape[0] // I
    QKV = 3 * HL * HP
    steps = HL + 2
    i, s = pl.program_id(0), pl.program_id(1)
    flat = i * steps + s
    t, p = lax.axis_index("tok"), lax.axis_index("tp")
    ring = Ring(NT)
    q = ring.place(t)
    right, left = (ring.tok(q + 1), p), (ring.tok(q - 1), p)
    core = (t, xor(p, 1))

    def at(n):
        return pl.when(flat == n)

    images = ImageMoves(NP, x_ref, rows_ref, rx_send, rx_recv, rc_send, rc_recv, r_sem)

    def first_keep():
        return pltpu.make_async_copy(rows_buf, rows_ref.at[0], r_sem.at[0, 0])

    def load_rows(n):
        if n:
            images.finish(n)
        if n == 1:
            first_keep().wait()
        src = rows_ref.at[n] if n else first_ref.at[0]
        cp = pltpu.make_async_copy(src, rows_buf, r_sem.at[I, 0])
        cp.start()
        cp.wait()
        if n == 0:
            first_keep().start()

    def cot_x(n, k):
        src = cot_ref.at[n, :, images.tokens(xor(p // 2, k), 0)]
        return copy_to(
            src, cots_ref.at[n, k, 0], t_send.at[0, n, k], t_recv.at[0, n, k], (t, xor(p, 2 * k))
        )

    def cot_keep(n):
        src = cot_ref.at[n, :, images.tokens(p // 2, 0)]
        return pltpu.make_async_copy(src, cots_ref.at[n, 0, 0], t_sem.at[n])

    def cot_core(n, k):
        src = cots_ref.at[n, k, 0] if k else cot_ref.at[n, :, images.tokens(p // 2, 0)]
        return copy_to(src, cots_ref.at[n, k, 1], t_send.at[1, n, k], t_recv.at[1, n, k], core)

    def start_cot():
        for n in range(I):
            for k in range(1, NX):
                cot_x(n, k).start()

    def land_cot():
        for n in range(I):
            for k in range(1, NX):
                cot_x(n, k).wait_recv()
                cot_core(n, k).start()

    def where(tt):
        out = 0
        for r in range(NP):
            out = out + jnp.where(p == r, xor(tt // SUB, r), 0)
        return out * SUB + tt % SUB

    def hop(k, d, side):
        block = where(ring.tok(q - (d - 1) if side == 0 else q + (d - 1)))
        dst = full_ref.at[k, :, block]
        src = late_ref.at[k] if d == 1 else dst
        if d == NT // 2:
            src, dst = src.at[side], dst.at[side]
        return copy_to(src, dst, l_send.at[k, side, d], l_recv.at[k, side, d], left if side else right)

    def keep(k):
        return pltpu.make_async_copy(late_ref.at[k], full_ref.at[k, :, where(t)], local_sem.at[k])

    def start_hop(k, d):
        for side in range(2):
            hop(k, d, side).start()

    def land_hop(k, d):
        for side in range(2):
            hop(k, d, side).wait_recv()
        if d < NT // 2:
            start_hop(k, d + 1)

    def core_copy(i):
        return copy_to(core_out.at[i], core_in.at[i], c_send.at[i], c_recv.at[i], core)

    def x_copy(i, k):
        return copy_to(
            x_out.at[i, k], x_in.at[i, k], x_send.at[i, k], x_recv.at[i, k], (t, xor(p, 2 * k))
        )

    def back_copy(i):
        return copy_to(total_ref.at[i], branch_ref.at[i, 1], b_send.at[i], b_recv.at[i], core)

    def back_keep(i):
        return pltpu.make_async_copy(total_ref.at[i], branch_ref.at[i, 0], local_sem.at[NX + i])

    def add_core(i):
        core_copy(i).wait_recv()
        for f in range(NX):
            for k in range(NX):
                cols = slice(k * T, (k + 1) * T)
                v = own_ref[f, :, cols] + core_in[i, f, :, cols].astype(f32)
                if k == 0:
                    total_ref[i, f] = v
                else:
                    x_out[i, k, f] = v.astype(bf16)
        for k in range(1, NX):
            x_copy(i, k).start()

    def add_x(i):
        for k in range(1, NX):
            x_copy(i, k).wait_recv()
        for f in range(NX):
            v = total_ref[i, f]
            for k in range(1, NX):
                v = v + x_in[i, k, f ^ k].astype(f32)
            total_ref[i, f] = v
        back_copy(i).start()
        back_keep(i).start()

    @at(0)
    def _():
        barrier = pltpu.get_barrier_semaphore()
        peers = [right, left, core] + [(t, xor(p, 2 * k)) for k in range(1, NX)]
        for peer in peers:
            pl.semaphore_signal(barrier, inc=1, device_id=peer, device_id_type=MESH)
        pl.semaphore_wait(barrier, len(peers))
        if I > 1:
            images.start(1)
        for k in range(NX):
            start_hop(k, 1)
        for n in range(I):
            cot_keep(n).start()
            cot_core(n, 0).start()
        for k in range(NX):
            keep(k).start()
        wt_ref[...] = w_ref[:, :QKV].T

    for n in range(I):
        if n:

            @at((n - 1) * steps + HL)
            def _(n=n):
                images.land(n)
                if n + 1 < I:
                    images.start(n + 1)
                else:
                    start_cot()

        at(n * steps)(functools.partial(load_rows, n))

    @pl.when(s == 0)
    def _():
        for r in range(NP):
            rows = [(pl.ds(i, 1), 0), (pl.ds(i, 1), ML)]
            mcol_ref[r * CB : (r + 1) * CB] = spread(mod_ref, r, rows, CB)
        width = 256
        for j in range(LEN // width):
            cols = slice(j * width, (j + 1) * width)
            v = rows_buf[:, :, cols].reshape(D, width).astype(f32)
            centre = jnp.sum(v, axis=0, keepdims=True) * (1.0 / D)
            square = jnp.sum(v * v, axis=0, keepdims=True) * (1.0 / D)
            inverse = lax.rsqrt(square - centre * centre + EPS)
            stats_ref[0, 0:1, cols] = centre
            stats_ref[0, 1:2, cols] = inverse
            n = (v - centre) * inverse
            a = (n * (1.0 + mcol_ref[:, 1:2]) + mcol_ref[:, 0:1]).astype(bf16)
            attn_ref[0, :, cols] = a
            out = jnp.dot(wt_ref[...], a, preferred_element_type=f32) + bias_ref[...]
            qkv_ref[0, :, cols] = out.astype(bf16)

    @pl.when((s > 0) & (s <= HL))
    def _():
        h = s - 1
        gate = gate_ref[i * HL + h]

        def head(k):
            return pl.ds(pl.multiple_of((k * HL + h) * HP, HP), HP)

        keys = qkv_ref[0, head(1)].T
        sc = jnp.dot(keys, qkv_ref[0, head(0)], preferred_element_type=f32)
        top = jnp.max(sc, axis=0, keepdims=True)
        pr = jnp.exp2((sc - top) * SCALE2).astype(bf16)
        out = jnp.dot(qkv_ref[0, head(2)], pr, preferred_element_type=f32)
        total = out[HD : HD + 1]
        mixed = out * (1.0 / total)
        mixed_ref[0, head(0)] = mixed
        concat_ref[0, head(0)] = (mixed * gate).astype(bf16)
        lse_ref[0, pl.ds(h, 1)] = top * SCALE2 + jnp.log2(total)

    @pl.when(s == HL + 1)
    def _():
        for r in range(NP):
            w = w_ref[r * CB : (r + 1) * CB, w_ref.shape[1] - HL * HP :]
            part = jnp.dot(w, concat_ref[0], preferred_element_type=f32)
            if r % 2 == 0:
                own_ref[r // 2] = part
            else:
                core_out[i, r // 2] = part.astype(bf16)
        core_copy(i).start()

    for n in range(I - 1):
        at((n + 1) * steps + 1)(functools.partial(add_core, n))
        at((n + 1) * steps + HL + 1)(functools.partial(add_x, n))

    events = [(k, d) for d in range(1, NT // 2 + 1) for k in range(NX)]
    early = [6, 7, 13, 14] if I > 2 else []
    for n, (k, d) in zip(early, events):
        at(n)(functools.partial(land_hop, k, d))

    @at(I * steps - 1)
    def _():
        if I == 1:
            start_cot()
        add_core(I - 1)
        land_cot()
        rest = events[len(early) :]
        for n, (k, d) in enumerate(rest):
            land_hop(k, d)
            if n == 0:
                add_x(I - 1)
        for n in range(I):
            back_copy(n).wait_recv()
        if I == 1:
            first_keep().wait()
        for n in range(I):
            if n:
                images.left(n)
            cot_keep(n).wait()
            for k in range(NX):
                cot_core(n, k).wait_recv()
                cot_core(n, k).wait_send()
                if k:
                    cot_x(n, k).wait_send()
        for n in range(I):
            core_copy(n).wait_send()
            back_copy(n).wait_send()
            back_keep(n).wait()
            for k in range(1, NX):
                x_copy(n, k).wait_send()
        for k in range(NX):
            keep(k).wait()
            for d in range(1, NT // 2 + 1):
                for side in range(2):
                    hop(k, d, side).wait_send()


def fwd_call(NT, NP, gate, x, cot, first, w, mods, bias, late):
    I, _, length = x.shape
    NX = NP // 2
    CB, T = D // NP, length // NX
    HL = gate.shape[0] // I
    QKV = 3 * HL * HP
    RB, FL = late.shape[2:]
    hbm = pl.BlockSpec(memory_space=pl.ANY)
    vmem = pl.BlockSpec(memory_space=pltpu.VMEM)
    dma = pltpu.SemaphoreType.DMA

    def image(*shape):
        return pl.BlockSpec((1,) + shape, lambda i, s: (i,) + (0,) * len(shape))

    return pl.pallas_call(
        functools.partial(fwd_kernel, NT, NP),
        grid=(I, HL + 2),
        in_specs=[
            pl.BlockSpec(memory_space=pltpu.SMEM),
            vmem,
            vmem,
            hbm,
            vmem,
            vmem,
            vmem,
            vmem,
        ],
        out_specs=[
            image(D, length),
            image(QKV, length),
            image(HL * HP, length),
            image(HL * HP, length),
            image(HL, length),
            image(8, length),
            hbm,
            hbm,
            hbm,
            hbm,
        ],
        out_shape=[
            jax.ShapeDtypeStruct((I, D, length), bf16),
            jax.ShapeDtypeStruct((I, QKV, length), bf16),
            jax.ShapeDtypeStruct((I, HL * HP, length), f32),
            jax.ShapeDtypeStruct((I, HL * HP, length), bf16),
            jax.ShapeDtypeStruct((I, HL, length), f32),
            jax.ShapeDtypeStruct((I, 8, length), f32),
            jax.ShapeDtypeStruct((I, 2, NX, CB, T), f32),
            jax.ShapeDtypeStruct((NX, 2, NT, RB, FL), bf16),
            jax.ShapeDtypeStruct((I, NP, CB, length), bf16),
            jax.ShapeDtypeStruct((I, NX, 2, CB, T), bf16),
        ],
        scratch_shapes=[
            pltpu.VMEM((QKV, D), bf16),
            pltpu.VMEM((NX, CB, length), f32),
            pltpu.VMEM((I, NX, CB, length), bf16),
            pltpu.VMEM((I, NX, CB, length), bf16),
            pltpu.VMEM((I, NX, NX, CB, T), bf16),
            pltpu.VMEM((I, NX, NX, CB, T), bf16),
            pltpu.VMEM((I, NX, CB, T), f32),
            pltpu.VMEM((D, 8), f32),
            dma((NX, 2, NT // 2 + 1)),
            dma((NX, 2, NT // 2 + 1)),
            dma((I,)),
            dma((I,)),
            dma((I, NX)),
            dma((I, NX)),
            dma((I,)),
            dma((I,)),
            dma((NX + I,)),
            pltpu.VMEM((NP, CB, length), bf16),
            dma((I, NX, NX)),
            dma((I, NX, NX)),
            dma((I, NX, NX)),
            dma((I, NX, NX)),
            dma((I + 1, NX)),
            dma((2, I, NX)),
            dma((2, I, NX)),
            dma((I,)),
        ],
        compiler_params=pltpu.CompilerParams(
            collective_id=2, has_side_effects=True, vmem_limit_bytes=60 * 2**20
        ),
        name="forward",
    )(gate, x, cot, first, w, mods, bias, late)


def lane_sum(v):
    total = v[:, :128]
    for j in range(1, v.shape[1] // 128):
        total = total + v[:, j * 128 : (j + 1) * 128]
    return jnp.sum(total.T, axis=0, keepdims=True)


def mlp_kernel(
    NT, NP, branch_ref, rows_ref, cot_ref, mods_ref, gate_ref, w_ref,
    lhs_ref, rhs_ref, go_ref, gms_ref, gm_ref, sums_ref, fsums_ref, out_ref, go0_ref,
    mid_ref, gn_ref, b2_ref, st_ref, gn_out, gn_in, b2_out, b2_in, o_buf,
    mcol_ref, g_send, g_recv, b_send, b_recv, x_send, x_recv, local_sem, go_buf, f_send, f_recv,
):
    NX = NP // 2
    _, _, D_, T = lhs_ref.shape
    CB = D // NP
    I = pl.num_programs(0)
    FL = w_ref.shape[3]
    i = pl.program_id(0)
    slot = i % 2
    t, p = lax.axis_index("tok"), lax.axis_index("tp")
    xi = p // 2
    core = (t, xor(p, 1))

    def gn_copy(n):
        return copy_to(gn_out, gn_in.at[n % 2], g_send.at[n], g_recv.at[n], core)

    def b2_copy(n):
        return copy_to(b2_out, b2_in.at[n % 2], b_send.at[n], b_recv.at[n], core)

    def place(n):
        return out_ref.at[n, :, pl.ds(pl.multiple_of(xi * T, T), T)]

    def out_copy(n, k):
        return copy_to(
            o_buf.at[n % 2, k], place(n), x_send.at[n, k], x_recv.at[n, k], (t, xor(p, 2 * k))
        )

    def out_keep(n):
        return pltpu.make_async_copy(o_buf.at[n % 2, 0], place(n), local_sem.at[n])

    def out_left(n):
        out_keep(n).wait()
        for k in range(1, NX):
            out_copy(n, k).wait_send()

    def go_x(k, f):
        return copy_to(
            go_buf.at[f], go0_ref.at[k, f ^ k, 0], f_send.at[0, k, f], f_recv.at[0, k, f],
            (t, xor(p, 2 * k)),
        )

    def go_core(k, f):
        return copy_to(
            go0_ref.at[k, f, 0], go0_ref.at[k, f, 1], f_send.at[1, k, f], f_recv.at[1, k, f], core
        )

    @pl.when(i == 0)
    def _():
        barrier = pltpu.get_barrier_semaphore()
        peers = [core] + [(t, xor(p, 2 * k)) for k in range(1, NX)]
        for peer in peers:
            pl.semaphore_signal(barrier, inc=1, device_id=peer, device_id_type=MESH)
        pl.semaphore_wait(barrier, len(peers))

    count = out_ref.shape[0]
    for r in range(NP):
        rows = [(pl.ds(i, 1), k * ML) for k in range(6)]
        rows += [(slice(count, count + 1), 0), (slice(count, count + 1), ML)]
        mcol_ref[r * CB : (r + 1) * CB] = spread(mods_ref, r, rows, CB)

    def col(k):
        return mcol_ref[:, k : k + 1]

    width = min(256, T)
    chunks = [slice(j * width, (j + 1) * width) for j in range(T // width)]

    def branch_one(cols):
        parts = [branch_ref[0, r % 2, r // 2, :, cols] for r in range(NP)]
        return jnp.concatenate(parts, axis=0) + col(6)

    for cols in chunks:
        x = jnp.concatenate([rows_ref[0, r, :, cols] for r in range(NP)], axis=0).astype(f32)
        mid = x + col(2) * branch_one(cols)
        mid_ref[:, cols] = mid
        centre = jnp.sum(mid, axis=0, keepdims=True) * (1.0 / D)
        square = jnp.sum(mid * mid, axis=0, keepdims=True) * (1.0 / D)
        inverse = lax.rsqrt(square - centre * centre + EPS)
        st_ref[0:1, cols] = centre
        st_ref[1:2, cols] = inverse
        n = (mid - centre) * inverse
        lhs_ref[0, 0, :, cols] = (n * (1.0 + col(4)) + col(3)).astype(bf16)
        lhs_ref[0, 1, :, cols] = (col(5) * cot_ref[0, :, cols].astype(f32)).astype(bf16)

    root = math.sqrt(2.0 / math.pi)
    tile = 384
    for k in range(NX):
        for at in range(0, FL, tile):
            rows = slice(at, min(at + tile, FL))
            size = rows.stop - rows.start
            vec = [gate_ref[k, pl.ds(i, 1), rows], mods_ref[2 * k, count + 1 : count + 2, rows]]
            vec = jnp.concatenate(vec + [jnp.zeros((6, size), f32)], axis=0).T
            pre = dot(w_ref[k, 0, :, rows], lhs_ref[0, 0], 0, 0) + vec[:, 1:2]
            grad_hid = dot(w_ref[k, 1, :, rows], lhs_ref[0, 1], 0, 0)
            gate = vec[:, 0:1]
            square = pre * pre
            inner = jnp.tanh(pre * (root + (root * 0.044715) * square))
            half = 0.5 * (1.0 + inner)
            act = pre * half
            slope = half + (0.5 * pre) * (1.0 - inner * inner) * (root + (3.0 * root * 0.044715) * square)
            rhs_ref[0, 1, k, rows] = (act * gate).astype(bf16)
            grad_pre = (slope * gate * grad_hid).astype(bf16)
            rhs_ref[0, 0, k, rows] = grad_pre
            to = slice(k * FL + rows.start, k * FL + rows.stop)
            fsums_ref[0, 0:1, to] = lane_sum(grad_pre.astype(f32))
            fsums_ref[0, 1:2, to] = lane_sum(grad_hid * act)

    def product(u, r):
        total = 0.0
        for k in range(NX):
            w = w_ref[k, u, r * CB : (r + 1) * CB]
            total = total + jnp.dot(w, rhs_ref[0, u, k], preferred_element_type=f32)
        return total

    for r in range(NP):
        v = product(0, r)
        gn_ref[r * CB : (r + 1) * CB] = v
        gn_out[r * CB : (r + 1) * CB] = v.astype(bf16)
    gn_copy(i).start()
    for r in range(NP):
        v = product(1, r)
        if r % 2:
            b2_out[r // 2] = v.astype(bf16)
        else:
            b2_ref[r // 2] = v
    b2_copy(i).start()

    gn_copy(i).wait_recv()
    gn_copy(i).wait_send()
    for r in range(NP):
        mine, theirs = slice(r * CB, (r + 1) * CB), slice((r ^ 1) * CB, ((r ^ 1) + 1) * CB)
        gn_ref[mine] = gn_ref[mine] + gn_in[slot, theirs].astype(f32)
    totals = [0.0] * 5

    def fold(v):
        total = v[:, :128]
        for j in range(1, v.shape[1] // 128):
            total = total + v[:, j * 128 : (j + 1) * 128]
        return total

    for cols in chunks:
        gnorm = gn_ref[:, cols]
        inverse = st_ref[1:2, cols]
        n = (mid_ref[:, cols] - st_ref[0:1, cols]) * inverse
        g = gnorm * (1.0 + col(4))
        mean_g = jnp.sum(g, axis=0, keepdims=True) * (1.0 / D)
        mean_gn = jnp.sum(g * n, axis=0, keepdims=True) * (1.0 / D)
        grad_mid = cot_ref[0, :, cols].astype(f32) + inverse * (g - mean_g - n * mean_gn)
        grad_one = (col(2) * grad_mid).astype(bf16)
        go_ref[0, :, cols] = grad_one
        gm_ref[0, :, cols] = grad_mid[:CB]
        for k in range(NX):
            gms_ref[0, k, :, cols] = grad_mid[2 * k * CB : (2 * k + 1) * CB].astype(bf16)
        terms = (
            grad_mid * branch_one(cols),
            gnorm,
            gnorm * n,
            grad_one.astype(f32),
            lhs_ref[0, 1, :, cols].astype(f32),
        )
        totals = [a + fold(b) for a, b in zip(totals, terms)]
    @pl.when(i == 0)
    def _():
        for f in range(NX):
            go_buf[f] = go_ref[0, 2 * f * CB : (2 * f + 1) * CB]
        for k in range(1, NX):
            for f in range(NX):
                go_x(k, f).start()

    for row, v in enumerate(totals):
        sums_ref[0, row : row + 1, :] = jnp.sum(v.T, axis=0, keepdims=True)

    @pl.when(i >= 2)
    def _():
        out_left(i - 2)

    b2_copy(i).wait_recv()
    b2_copy(i).wait_send()
    for f in range(NX):
        rows = slice(2 * f * CB, (2 * f + 1) * CB)
        v = b2_ref[f] + b2_in[slot, f].astype(f32) + mcol_ref[rows, 7:8]
        sums_ref[0, 5 : 6, f * CB : (f + 1) * CB] = lane_sum(cot_ref[0, rows].astype(f32) * v)
        o_buf[slot, f] = (mid_ref[rows] + mcol_ref[rows, 5:6] * v).astype(bf16)
    out_keep(i).start()
    for k in range(1, NX):
        out_copy(i, k).start()

    @pl.when(i == I - 1)
    def _():
        for k in range(1, NX):
            for f in range(NX):
                go_x(k, f ^ k).wait_recv()
                go_core(k, f).start()
        for n in range(x_send.shape[0]):
            for k in range(1, NX):
                out_copy(n, k).wait_recv()
            if n >= x_send.shape[0] - 2:
                out_left(n)
        for k in range(1, NX):
            for f in range(NX):
                go_core(k, f).wait_recv()
                go_core(k, f).wait_send()
                go_x(k, f).wait_send()


def mlp_call(NT, NP, branch, rows, cot, mods, gates, w):
    I, NX = branch.shape[0], NP // 2
    CB, T = branch.shape[3:]
    FL = w.shape[3]
    hbm = pl.BlockSpec(memory_space=pl.ANY)
    vmem = pl.BlockSpec(memory_space=pltpu.VMEM)
    dma = pltpu.SemaphoreType.DMA

    def image(*shape):
        return pl.BlockSpec((1,) + shape, lambda i: (i,) + (0,) * len(shape))

    return pl.pallas_call(
        functools.partial(mlp_kernel, NT, NP),
        grid=(I,),
        in_specs=[
            pl.BlockSpec(
                (1, 2, NX, CB, T), lambda i: (i, 0, 0, 0, 0), pipeline_mode=pl.Buffered(buffer_count=1)
            ),
            image(NP, CB, T),
            image(D, T),
            vmem,
            vmem,
            vmem,
        ],
        out_specs=[
            image(2, D, T),
            image(2, NX, FL, T),
            image(D, T),
            image(NX, CB, T),
            image(CB, T),
            image(8, D),
            image(8, NX * FL),
            hbm,
            hbm,
        ],
        out_shape=[
            jax.ShapeDtypeStruct((I, 2, D, T), bf16),
            jax.ShapeDtypeStruct((I, 2, NX, FL, T), bf16),
            jax.ShapeDtypeStruct((I, D, T), bf16),
            jax.ShapeDtypeStruct((I, NX, CB, T), bf16),
            jax.ShapeDtypeStruct((I, CB, T), f32),
            jax.ShapeDtypeStruct((I, 8, D), f32),
            jax.ShapeDtypeStruct((I, 8, NX * FL), f32),
            jax.ShapeDtypeStruct((I, CB, NX * T), bf16),
            jax.ShapeDtypeStruct((NX, NX, 2, CB, T), bf16),
        ],
        scratch_shapes=[
            pltpu.VMEM((D, T), f32),
            pltpu.VMEM((D, T), f32),
            pltpu.VMEM((NX, CB, T), f32),
            pltpu.VMEM((8, T), f32),
            pltpu.VMEM((D, T), bf16),
            pltpu.VMEM((2, D, T), bf16),
            pltpu.VMEM((NX, CB, T), bf16),
            pltpu.VMEM((2, NX, CB, T), bf16),
            pltpu.VMEM((2, NX, CB, T), bf16),
            pltpu.VMEM((D, 8), f32),
            dma((I,)),
            dma((I,)),
            dma((I,)),
            dma((I,)),
            dma((I, NX)),
            dma((I, NX)),
            dma((I,)),
            pltpu.VMEM((NX, CB, T), bf16),
            dma((2, NX, NX)),
            dma((2, NX, NX)),
        ],
        compiler_params=pltpu.CompilerParams(
            collective_id=3, has_side_effects=True, vmem_limit_bytes=60 * 2**20
        ),
        name="feed_forward",
    )(branch, rows, cot, mods, gates, w)


def grads_kernel(lhs_ref, rhs_ref, out_ref):
    I, _, rows, _ = lhs_ref.shape
    NT, RB = out_ref.shape[2:4]
    for b in range(0, NT, 2):
        total = 0.0
        for i in range(I):
            a = lhs_ref[i, 0, b * RB : (b + 2) * RB]
            total = total + dot(a, rhs_ref[i, 0, 0], 1, 1)
        out_ref[0, 0, b : b + 2] = total.astype(bf16).reshape(2, RB, -1)


def grads_call(NT, lhs, rhs):
    I, _, NX, FL, T = rhs.shape
    RB = D // NT
    return pl.pallas_call(
        grads_kernel,
        grid=(2, NX),
        in_specs=[
            pl.BlockSpec((I, 1, D, T), lambda u, k: (0, u, 0, 0)),
            pl.BlockSpec((I, 1, 1, FL, T), lambda u, k: (0, u, k, 0, 0)),
        ],
        out_specs=pl.BlockSpec((1, 1, NT, RB, FL), lambda u, k: (k, u, 0, 0, 0)),
        out_shape=jax.ShapeDtypeStruct((NX, 2, NT, RB, FL), bf16),
        compiler_params=pltpu.CompilerParams(vmem_limit_bytes=48 * 2**20),
        name="late_grads",
    )(lhs, rhs)


def bwd_kernel(
    NT, NP, gate_ref, go_ref, go0_ref, gms_ref, gm_ref, qkv_ref, mixed_ref, lse_ref, concat_ref, attn_ref,
    rows_ref, stats_ref, scale_ref, w_ref, late_ref, base_ref, factor_ref, ada_ref,
    gin_ref, late_out, gqkv_ref, gout_ref, lasts_ref, cond_ref, gox_ref,
    go_buf, gmx_ref, own_ref, core_out, core_in, x_out, x_in, gn_ref, accq_ref, acco_ref, wt_ref,
    gc_ref, dqkv_ref, rows_buf, gin_buf, st_out, st_in, msg_ref, heads_ref, qv_ref,
    l_own, l_out, l_in, lx_out, lx_in, q_out, q_in, part_ref, sum_ref, lasts_buf,
    g_send, g_recv, c_send, c_recv, x_send, x_recv, t_send, t_recv, l_send, l_recv, lx_send, lx_recv,
    q_send, q_recv, s_send, s_recv, m_send, m_recv, m2_send, m2_recv, local_sem, own_sem,
):
    NX, SUB = NP // 2, NT // NP
    I, CB, T = gm_ref.shape
    HL = gate_ref.shape[0] // I
    QKV, HO = 3 * HL * HP, HL * HP
    RB = D // NT
    HOPS = NT // 2
    steps = HL + 2
    i, s = pl.program_id(0), pl.program_id(1)
    flat = i * steps + s
    t, p = lax.axis_index("tok"), lax.axis_index("tp")
    xi = p // 2
    ring = Ring(NT)
    q = ring.place(t)
    right, left = (ring.tok(q + 1), p), (ring.tok(q - 1), p)
    core = (t, xor(p, 1))

    def at(n):
        return pl.when(flat == n)

    def partner(k):
        return (t, xor(p, 2 * k))

    def where(tt):
        out = 0
        for r in range(NP):
            out = out + jnp.where(p == r, xor(tt // SUB, r), 0)
        return out * SUB + tt % SUB

    def go_x(n, k, f):
        return copy_to(
            go_ref.at[n, f, 0], gox_ref.at[n, k, f ^ k, 0], g_send.at[0, n, k, f],
            g_recv.at[0, n, k, f], partner(k),
        )

    def go_core(n, k, f):
        return copy_to(
            gox_ref.at[n, k, f, 0], gox_ref.at[n, k, f, 1], g_send.at[1, n, k, f],
            g_recv.at[1, n, k, f], core,
        )

    def gm_x(n, k):
        return copy_to(gms_ref.at[n, k], gmx_ref.at[n, k - 1], m_send.at[n, k], m_recv.at[n, k], partner(k))

    def send_go(n):
        for k in range(1, NX):
            for f in range(NX):
                go_x(n, k, f).start()

    def pass_go(n):
        for k in range(1, NX):
            for f in range(NX):
                go_x(n, k, f ^ k).wait_recv()
                go_core(n, k, f).start()
        if n + 1 < I:
            send_go(n + 1)
        for m in [n - 1] if n + 1 < I else [n - 1, n]:
            if m >= 0:
                for k in range(1, NX):
                    gm_x(m, k).start()

    def load_go(n):
        def load(k):
            src = go_ref.at[n] if k == 0 else gox_ref.at[n, k] if n else go0_ref.at[k]
            return pltpu.make_async_copy(src, go_buf.at[k], local_sem.at[k])

        load(0).start()
        for k in range(1, NX):
            for f in range(NX if n else 0):
                go_core(n, k, f).wait_recv()
            load(k).start()
        for k in range(NX):
            load(k).wait()

    def rows_copy(n):
        return pltpu.make_async_copy(rows_ref.at[n, 0], rows_buf.at[n], local_sem.at[NX + n])

    def core_copy(n):
        return copy_to(core_out, core_in.at[n % 2], c_send.at[n], c_recv.at[n], core)

    def x_copy(n, k):
        return copy_to(
            x_out.at[n % 2, k - 1], x_in.at[n % 2, k - 1], x_send.at[n, k], x_recv.at[n, k], partner(k)
        )

    def st_copy(n, r):
        return copy_to(
            st_out.at[n], st_in.at[n, r], t_send.at[n, r], t_recv.at[n, r], (t, xor(p, r))
        )

    def gin_copy(n, j):
        to = pl.ds(pl.multiple_of(xor(xi, j) * T, T), T)
        return pltpu.make_async_copy(
            gin_buf.at[n % 2, :, pl.ds(j * T, T)], gin_ref.at[n, :, to], local_sem.at[NX + I + n * NX + j]
        )

    def add_core(n):
        core_copy(n).wait_recv()
        if n >= 2:
            for k in range(1, NX):
                x_copy(n - 2, k).wait_send()
        for f in range(NX):
            v = own_ref[f] + core_in[n % 2, f].astype(f32)
            if f == 0:
                gn_ref[...] = v
            else:
                x_out[n % 2, f - 1] = v.astype(bf16)
        for k in range(1, NX):
            x_copy(n, k).start()

    def tokens(v):
        total = v[:, :128]
        for j in range(1, LEN // 128):
            total = total + v[:, j * 128 : (j + 1) * 128]
        return jnp.sum(total.T, axis=0, keepdims=True)

    def own_scale(n):
        return 1.0 + scale_ref[0, :, ML : 2 * ML].T[:CB, n : n + 1]

    def normed(n):
        return (rows_buf[n].astype(f32) - stats_ref[n, 0:1]) * stats_ref[n, 1:2]

    def add_x(n):
        for k in range(1, NX):
            x_copy(n, k).wait_recv()
        for j in range(NX):
            v = gn_ref[:, j * T : (j + 1) * T]
            for k in range(1, NX):
                v = v + x_in[n % 2, k - 1, :, (j ^ k) * T : ((j ^ k) + 1) * T].astype(f32)
            gn_ref[:, j * T : (j + 1) * T] = v
        v = gn_ref[...]
        vn = v * normed(n)
        scale = own_scale(n)
        st_out[n, 0:1] = jnp.sum(v * scale, axis=0, keepdims=True)
        st_out[n, 1:2] = jnp.sum(vn * scale, axis=0, keepdims=True)
        for r in range(1, NP):
            st_copy(n, r).start()
        msg_ref[n : n + 1, :CB] = tokens(v)
        msg_ref[n : n + 1, ML : ML + CB] = tokens(vn)

    def add_stats(n):
        for r in range(1, NP):
            st_copy(n, r).wait_recv()
        if n >= 2:
            for j in range(NX):
                gin_copy(n - 2, j).wait()
        for k in range(1, NX):
            gm_x(n, k).wait_recv()
        for j in range(NX):
            cols = slice(j * T, (j + 1) * T)
            a, b = st_out[n, 0:1, cols], st_out[n, 1:2, cols]
            for r in range(1, NP):
                m = j ^ (r // 2)
                a = a + st_in[n, r, 0:1, m * T : (m + 1) * T]
                b = b + st_in[n, r, 1:2, m * T : (m + 1) * T]
            centre, inverse = stats_ref[n, 0:1, cols], stats_ref[n, 1:2, cols]
            nrm = (rows_buf[n, :, cols].astype(f32) - centre) * inverse
            g = gn_ref[:, cols] * own_scale(n)
            mid = gm_ref[n] if j == 0 else gmx_ref[n, j - 1].astype(f32)
            gin_buf[n % 2, :, cols] = mid + inverse * (g - a * (1.0 / D) - nrm * (b * (1.0 / D)))
        for j in range(NX):
            gin_copy(n, j).start()

    def l_block(side, h):
        d = HOPS - h
        return where(ring.tok(q + d if side == 0 else q - d))

    def l_load(k, side, h):
        return pltpu.make_async_copy(
            late_ref.at[k, :, l_block(side, h)], l_own.at[k, side], own_sem.at[k, side]
        )

    def l_hop(k, side, h):
        to = left if side else right
        if h == 0:
            return copy_to(
                late_ref.at[k, side, l_block(side, 0)], l_in.at[k, side, 0, side],
                l_send.at[k, side, h], l_recv.at[k, side, h], to,
            )
        return copy_to(
            l_out.at[k, side], l_in.at[k, side, h % 2], l_send.at[k, side, h], l_recv.at[k, side, h], to
        )

    def l_event(k, h):
        for side in range(2):
            l_hop(k, side, h - 1).wait_recv()
        for side in range(2):
            if h < HOPS or side == 0:
                l_load(k, side, h).wait()
            if 1 < h < HOPS:
                l_hop(k, side, h - 1).wait_send()
        if h < HOPS:
            for side in range(2):
                for u in range(2):
                    v = l_own[k, side, u]
                    if h > 1 or u == side:
                        v = (v.astype(f32) + l_in[k, side, (h - 1) % 2, u].astype(f32)).astype(bf16)
                    l_out[k, side, u] = v
            for side in range(2):
                l_hop(k, side, h).start()
                if h + 1 < HOPS or side == 0:
                    l_load(k, side, h + 1).start()
        else:
            for u in range(2):
                v = l_own[k, 0, u].astype(f32)
                for side in range(2):
                    if HOPS > 1 or u == side:
                        v = v + l_in[k, side, (h - 1) % 2, u].astype(f32)
                if k == 0:
                    late_out[u] = v
                else:
                    lx_out[k - 1, u] = v.astype(bf16)
            if k:
                lx_copy(k).start()

    def lx_copy(k):
        return copy_to(lx_out.at[k - 1], lx_in.at[k - 1], lx_send.at[k], lx_recv.at[k], partner(k))

    half = (QKV // 2 + 127) // 128 * 128

    def q_block(side, h):
        return l_block(side, h)

    def q_hop(side, h):
        to = left if side else right
        return copy_to(
            q_out.at[side], q_in.at[side, h % 2], q_send.at[side, h], q_recv.at[side, h], to
        )

    def q_event(h):
        if h:
            for side in range(2):
                q_hop(side, h - 1).wait_recv()
        if h < HOPS:
            for side in range(2):
                if h:
                    q_hop(side, h - 1).wait_send()
                block = q_block(side, h)
                a, b = accq_ref[block], acco_ref[block]
                if h:
                    a = a + q_in[side, (h - 1) % 2, :, :QKV].astype(f32)
                    b = b + q_in[side, (h - 1) % 2, :, QWIDE:].astype(f32)
                else:
                    lane = lax.broadcasted_iota(jnp.int32, a.shape, 1)
                    a = jnp.where((lane < half) if side == 0 else (lane >= half), a, 0.0)
                    b = b if side == 0 else jnp.zeros_like(b)
                q_out[side, :, :QKV] = a.astype(bf16)
                q_out[side, :, QWIDE:] = b.astype(bf16)
            for side in range(2):
                q_hop(side, h).start()
        else:
            a, b = accq_ref[q_block(0, h)], acco_ref[q_block(0, h)]
            for side in range(2):
                a = a + q_in[side, (h - 1) % 2, :, :QKV].astype(f32)
                b = b + q_in[side, (h - 1) % 2, :, QWIDE:].astype(f32)
            gqkv_ref[...] = a
            gout_ref[...] = b

    QWIDE = (QKV + 127) // 128 * 128

    pieces = ((1024, 6 * ML - 1024), (0, 1024), (6 * ML, 128))

    def last_copy(k, n):
        lanes = pl.ds(*pieces[n])
        return copy_to(
            msg_ref.at[:, lanes], lasts_buf.at[k, :, lanes], m2_send.at[n, k], m2_recv.at[n, k],
            ((t + k) % NT, p),
        )

    def part_copy(k):
        return copy_to(
            part_ref.at[k], sum_ref.at[0, t], s_send.at[1, k], s_recv.at[1, k], ((t + NT - k) % NT, p)
        )

    def sum_copy(r):
        return copy_to(sum_ref.at[0], sum_ref.at[r], s_send.at[2, r], s_recv.at[2, r], (t, xor(p, r)))

    def cond_first():
        msg_ref[I : I + 1, :QKV] = qv_ref[0:1, :QKV]
        msg_ref[:, 6 * ML :] = msg_ref[:, 6 * ML :] + heads_ref[...] * factor_ref[...]
        for k in range(1, NT):
            last_copy(k, 1).start()
            last_copy(k, 2).start()
        lasts_buf[0] = msg_ref[...]

    def cond_second():
        for k in range(1, NT):
            for n in range(3):
                last_copy(k, n).wait_recv()
        lasts_ref[...] = lasts_buf[...]
        grads = lasts_buf[...].reshape(NT * 8, -1)
        total = 0.0
        for k in range(6):
            g = grads[:, k * ML : (k + 1) * ML]
            high = g.astype(bf16)
            low = (g - high.astype(f32)).astype(bf16)
            total = total + dot(high, ada_ref[k], 1, 1) + dot(low, ada_ref[k], 1, 1)
        part_ref[...] = jnp.zeros_like(part_ref)
        part_ref[:, :, :RB] = total.reshape(NT, 8, RB)
        for k in range(1, NT):
            part_copy(k).start()
        sum_ref[0, t] = part_ref[0]

    def cond_third():
        for k in range(1, NT):
            part_copy(k).wait_recv()
        for r in range(1, NP):
            sum_copy(r).start()

    def cond_last():
        total = sum_ref[0]
        for r in range(1, NP):
            sum_copy(r).wait_recv()
            total = total + sum_ref[r]
        cond_ref[...] = total

    def finish_core():
        if I > 1:
            add_x(I - 2)
            add_stats(I - 2)
        add_core(I - 1)

    @at(0)
    def _():
        greet(t, p, NT, NP)
        if I > 1:
            send_go(1)
        for k in range(NX):
            for side in range(2):
                l_hop(k, side, 0).start()
                l_load(k, side, 1).start()
        for n in range(I):
            rows_copy(n).start()
        msg_ref[...] = base_ref[...]
        for k in range(1, NT):
            last_copy(k, 0).start()
        heads_ref[...] = jnp.zeros_like(heads_ref)
        qv_ref[...] = jnp.zeros_like(qv_ref)
        wt_ref[...] = w_ref[:, w_ref.shape[1] - HO :].T
        accq_ref[...] = jnp.zeros_like(accq_ref)
        acco_ref[...] = jnp.zeros_like(acco_ref)
        for n in range(I):
            rows_copy(n).wait()

    for n in range(I):
        if n:
            at((n - 1) * steps + HL)(functools.partial(pass_go, n))
        at(n * steps)(functools.partial(load_go, n))

    @pl.when(s == 0)
    def _():
        for k in range(NX):
            v = go_buf[k].reshape(D, T)
            gc_ref[:, k * T : (k + 1) * T] = jnp.dot(wt_ref[...], v, preferred_element_type=f32)

    @pl.when((s > 0) & (s <= HL))
    def _():
        h = s - 1
        gate = gate_ref[i * HL + h]

        def head(k):
            return pl.ds(pl.multiple_of((k * HL + h) * HP, HP), HP)

        keys_t = qkv_ref[0, head(1)]
        keys = keys_t.T
        values = qkv_ref[0, head(2)].T
        gc = gc_ref[head(0)]
        inner = jnp.sum(mixed_ref[0, head(0)] * gc, axis=0, keepdims=True)
        lane = lax.broadcasted_iota(jnp.int32, (1, 128), 1)
        row = heads_ref[pl.ds(i, 1)]
        heads_ref[pl.ds(i, 1)] = row + jnp.where(lane == h, jnp.sum(inner), 0.0)
        delta = gate * inner
        grad = (gate * gc).astype(bf16)
        lse = lse_ref[0, pl.ds(h, 1)]
        queries = qkv_ref[0, head(0)]
        dv = jnp.zeros((LEN, HP), f32)
        dk = jnp.zeros((LEN, HP), f32)
        chunk = 256
        for j in range(LEN // chunk):
            part = slice(j * chunk, (j + 1) * chunk)
            qj = queries[:, part]
            do = grad[:, part]
            sc = jnp.dot(keys, qj, preferred_element_type=f32)
            pr = jnp.exp2(sc * SCALE2 - lse[:, part])
            dp = jnp.dot(values, do, preferred_element_type=f32)
            ds = (pr * (dp - delta[:, part])).astype(bf16)
            dv = dv + jnp.dot(pr.astype(bf16), do.T, preferred_element_type=f32)
            dk = dk + jnp.dot(ds, qj.T, preferred_element_type=f32)
            dq = jnp.dot(keys_t, ds, preferred_element_type=f32)
            dqkv_ref[head(0), part] = (dq * SCALE).astype(bf16)
        dqkv_ref[head(1)] = (dk * SCALE).T.astype(bf16)
        dqkv_ref[head(2)] = dv.T.astype(bf16)

    @pl.when(s == HL + 1)
    def _():
        for n in range(1, I):
            at(n * steps + HL + 1)(lambda n=n: core_copy(n - 1).wait_send())
        for r in range(NP):
            w = w_ref[r * CB : (r + 1) * CB, :QKV]
            part = jnp.dot(w, dqkv_ref[...], preferred_element_type=f32)
            if r % 2 == 0:
                own_ref[r // 2] = part
            else:
                core_out[r // 2] = part.astype(bf16)
        for n in range(I):
            at(n * steps + HL + 1)(lambda n=n: core_copy(n).start())
        for b in range(0, NT, 2):
            rows = slice(b * RB, (b + 2) * RB)
            v = dot(attn_ref[0, rows], dqkv_ref[...], 1, 1)
            accq_ref[b : b + 2] = accq_ref[b : b + 2] + v.reshape(2, RB, QKV)
        at(I * steps - 1)(functools.partial(finish_core))
        for b in range(0, NT, 2):
            rows = slice(b * RB, (b + 2) * RB)
            v = 0.0
            for k in range(NX):
                g = go_buf[k].reshape(D, T)[rows]
                v = v + dot(g, concat_ref[0, :, k * T : (k + 1) * T], 1, 1)
            acco_ref[b : b + 2] = acco_ref[b : b + 2] + v.reshape(2, RB, HO)
        qv_ref[0:1, :QKV] = qv_ref[0:1, :QKV] + tokens(dqkv_ref[...].astype(f32))

    for n in range(I - 1):
        at((n + 1) * steps + 1)(functools.partial(add_core, n))
        if n + 2 < I:
            at((n + 1) * steps + HL + 1)(functools.partial(add_x, n))
        if n + 2 < I:
            at((n + 2) * steps)(functools.partial(add_stats, n))

    events = [
        functools.partial(l_event, k, h) for h in range(1, HOPS + 1) for k in reversed(range(NX))
    ]
    early = [2, 3, 8, 9, 13, 14] if I > 2 else []
    early = early[: len(events)]
    for n, event in zip(early, events):
        at(n)(event)

    @at(I * steps - 1)
    def _():
        rest = events[len(early) :]
        q_event(0)
        todo = [functools.partial(add_x, I - 1), cond_first, functools.partial(q_event, 1)]
        todo += [functools.partial(add_stats, I - 1), cond_second]
        todo += rest[:-1] + [functools.partial(q_event, 2), cond_third] + rest[-1:]
        todo += [functools.partial(q_event, h) for h in range(3, HOPS)] + [cond_last]
        todo += [functools.partial(q_event, HOPS)]
        for step in todo:
            step()
        for k in range(1, NX):
            lx_copy(k).wait_recv()
            for u in range(2):
                late_out[u] = late_out[u] + lx_in[k - 1, u].astype(f32)
        core_copy(I - 1).wait_send()
        for n in range(I):
            for k in range(1, NX):
                gm_x(n, k).wait_send()
                for f in range(NX if n else 0):
                    go_x(n, k, f).wait_send()
                    go_core(n, k, f).wait_send()
                if n >= I - 2:
                    x_copy(n, k).wait_send()
            for r in range(1, NP):
                st_copy(n, r).wait_send()
            if n >= I - 2:
                for j in range(NX):
                    gin_copy(n, j).wait()
        for k in range(NX):
            for side in range(2):
                l_hop(k, side, 0).wait_send()
                if HOPS > 1:
                    l_hop(k, side, HOPS - 1).wait_send()
        for side in range(2):
            q_hop(side, HOPS - 1).wait_send()
        for k in range(1, NX):
            lx_copy(k).wait_send()
        for k in range(1, NT):
            for n in range(3):
                last_copy(k, n).wait_send()
            part_copy(k).wait_send()
        for r in range(1, NP):
            sum_copy(r).wait_send()


def bwd_call(
    NT, NP, gate, go, go0, gms, gm, qkv, mixed, lse, concat, attn, rows, stats, scale, w, late, base, factor, ada
):
    I, CB, T = gm.shape
    NX = NP // 2
    length = attn.shape[2]
    HL = gate.shape[0] // I
    QKV, HO = 3 * HL * HP, HL * HP
    QWIDE = (QKV + 127) // 128 * 128
    RB, FL = late.shape[3:]
    HOPS = NT // 2
    hbm = pl.BlockSpec(memory_space=pl.ANY)
    vmem = pl.BlockSpec(memory_space=pltpu.VMEM)
    dma = pltpu.SemaphoreType.DMA
    once = pl.Buffered(buffer_count=1)

    def image(*shape):
        return pl.BlockSpec(
            (1,) + shape, lambda i, s: (i,) + (0,) * len(shape), pipeline_mode=once
        )

    return pl.pallas_call(
        functools.partial(bwd_kernel, NT, NP),
        grid=(I, HL + 2),
        in_specs=[
            pl.BlockSpec(memory_space=pltpu.SMEM),
            hbm,
            hbm,
            hbm,
            vmem,
            image(QKV, length),
            image(HO, length),
            image(HL, length),
            image(HO, length),
            image(D, length),
            hbm,
            vmem,
            vmem,
            vmem,
            hbm,
            vmem,
            vmem,
            vmem,
        ],
        out_specs=[hbm, vmem, vmem, vmem, vmem, vmem, hbm],
        out_shape=[
            jax.ShapeDtypeStruct((I, CB, length), f32),
            jax.ShapeDtypeStruct((2, RB, FL), f32),
            jax.ShapeDtypeStruct((RB, QKV), f32),
            jax.ShapeDtypeStruct((RB, HO), f32),
            jax.ShapeDtypeStruct((NT,) + base.shape, f32),
            jax.ShapeDtypeStruct((NT, 8, 256), f32),
            jax.ShapeDtypeStruct((I, NX, NX, 2, CB, T), bf16),
        ],
        scratch_shapes=[
            pltpu.VMEM((NX, NX, 2, CB, T), bf16),
            pltpu.VMEM((I, NX - 1, CB, T), bf16),
            pltpu.VMEM((NX, CB, length), f32),
            pltpu.VMEM((NX, CB, length), bf16),
            pltpu.VMEM((2, NX, CB, length), bf16),
            pltpu.VMEM((2, NX - 1, CB, length), bf16),
            pltpu.VMEM((2, NX - 1, CB, length), bf16),
            pltpu.VMEM((CB, length), f32),
            pltpu.VMEM((NT, RB, QKV), f32),
            pltpu.VMEM((NT, RB, HO), f32),
            pltpu.VMEM((HO, D), bf16),
            pltpu.VMEM((HO, length), f32),
            pltpu.VMEM((QKV, length), bf16),
            pltpu.VMEM((I, CB, length), bf16),
            pltpu.VMEM((2, CB, length), f32),
            pltpu.VMEM((I, 8, length), f32),
            pltpu.VMEM((I, NP, 8, length), f32),
            pltpu.VMEM(base.shape, f32),
            pltpu.VMEM((8, 128), f32),
            pltpu.VMEM((8, QWIDE), f32),
            pltpu.VMEM((NX, 2, 2, RB, FL), bf16),
            pltpu.VMEM((NX, 2, 2, RB, FL), bf16),
            pltpu.VMEM((NX, 2, 2, 2, RB, FL), bf16),
            pltpu.VMEM((NX - 1, 2, RB, FL), bf16),
            pltpu.VMEM((NX - 1, 2, RB, FL), bf16),
            pltpu.VMEM((2, RB, QWIDE + HO), bf16),
            pltpu.VMEM((2, 2, RB, QWIDE + HO), bf16),
            pltpu.VMEM((NT, 8, 256), f32),
            pltpu.VMEM((NP, NT, 8, 256), f32),
            pltpu.VMEM((NT,) + base.shape, f32),
            dma((2, I, NX, NX)),
            dma((2, I, NX, NX)),
            dma((I,)),
            dma((I,)),
            dma((I, NX)),
            dma((I, NX)),
            dma((I, NP)),
            dma((I, NP)),
            dma((NX, 2, HOPS)),
            dma((NX, 2, HOPS)),
            dma((NX,)),
            dma((NX,)),
            dma((2, HOPS)),
            dma((2, HOPS)),
            dma((3, max(NT, NP))),
            dma((3, max(NT, NP))),
            dma((I, NX)),
            dma((I, NX)),
            dma((3, NT)),
            dma((3, NT)),
            dma((NX + I + I * NX,)),
            dma((NX, 2)),
        ],
        compiler_params=pltpu.CompilerParams(
            collective_id=1, has_side_effects=True, vmem_limit_bytes=63 * 2**20
        ),
        name="backward",
    )(gate, go, go0, gms, gm, qkv, mixed, lse, concat, attn, rows, stats, scale, w, late, base, factor, ada)


def make_body(NT, NP):
    NX = NP // 2
    SUB = NT // NP
    RB = D // NT
    CB = D // NP
    T = LEN // NX

    def tp_xor(v, r):
        return lax.ppermute(v, "tp", [(p, p ^ r) for p in range(NP)])

    def body(
        block_input,
        condition,
        timesteps,
        head_mask,
        group_mask,
        w_ada,
        b_ada,
        w_qkv,
        b_qv,
        w_out,
        b_out,
        w_up,
        b_up,
        w_down,
        b_down,
        w_head,
        b_head,
        w_group,
        b_group,
        cotangent,
    ):
        I = condition.shape[0]
        HL = head_mask.shape[1]
        GL = group_mask.shape[1]
        FL = w_up.shape[1]
        FR = FREQ // NT
        t = lax.axis_index("tok")
        p = lax.axis_index("tp")
        xi = p // 2

        qkv_shard = jnp.pad(
            w_qkv.reshape(RB, 3, HL, HD), ((0, 0), (0, 0), (0, 0), (0, HP - HD))
        ).reshape(RB, 3 * HL * HP)
        out_shard = jnp.pad(w_out.T.reshape(RB, HL, HD), ((0, 0), (0, 0), (0, HP - HD))).reshape(
            RB, HL * HP
        )
        QKV = 3 * HL * HP
        gap = -QKV % 128
        early_shard = jnp.concatenate(
            [qkv_shard, jnp.zeros((RB, gap), bf16), out_shard], axis=1
        )
        late_shard = jnp.stack([w_up, w_down.T])
        late_shards = jnp.stack(
            [late_shard] + [tp_xor(late_shard, 2 * k) for k in range(1, NX)]
        )
        time_feat = embed_time(timesteps).astype(bf16)
        cond_wide = condition.astype(f32)
        cond_act = jax.nn.silu(cond_wide).astype(bf16)
        pad8 = lambda v, width: jnp.pad(v, ((0, 8 - v.shape[0]), (0, width - v.shape[1])))
        message = jnp.concatenate(
            [
                jnp.pad(cond_act.reshape(I, NT, RB), ((0, 0), (0, 0), (0, 256 - RB))),
                jnp.pad(time_feat.reshape(I, NT, FR), ((0, 0), (0, 0), (0, ML - 256 - FR))),
            ],
            axis=2,
        )
        message = jnp.pad(message.transpose(1, 0, 2).astype(f32), ((0, 0), (0, 8 - I), (0, 0)))
        ada = jnp.pad(w_ada.transpose(1, 0, 2), ((0, 0), (0, 0), (0, ML - CB)))
        gates = jnp.concatenate([w_head, w_group], axis=1)
        gates = jnp.pad(gates, ((0, 0), (0, 128 - HL - GL)))
        wide = 6 * ML + 128
        mod_bias = jnp.concatenate(
            [jnp.pad(b_ada, ((0, 0), (0, ML - CB))).reshape(6 * ML), b_head, b_group]
        ).astype(f32)
        bias = jnp.concatenate(
            [
                jnp.broadcast_to(pad8(mod_bias[None], wide)[:1], (I, wide)),
                pad8(jnp.concatenate([jnp.pad(b_out, (0, ML - CB)), b_down]).astype(f32)[None], wide)[:1],
                pad8(b_up.astype(f32)[None], wide)[: 8 - I - 1],
            ],
            axis=0,
        )
        mask = pad8(jnp.concatenate([head_mask, group_mask], axis=1).astype(f32), 128)
        first, early_full, mods, sig, cond_all = start_call(
            NT,
            NP,
            block_input,
            early_shard,
            message,
            ada,
            gates,
            bias,
            mask,
        )
        early_full = early_full.reshape(D, -1)
        head_sig, group_sig = sig[:I, :HL], sig[:I, HL : HL + GL]
        head_gate = mods[0, :I, 6 * ML : 6 * ML + HL]
        group_rows = jnp.stack(
            [
                jnp.repeat(mods[2 * k, :, 6 * ML + HL : 6 * ML + HL + GL], GW, axis=1)
                for k in range(NX)
            ]
        )

        qv = b_qv.astype(f32).reshape(2, HL, HD)
        qv_bias = jnp.stack(
            [
                jnp.pad(qv[0], ((0, 0), (0, HP - HD))),
                jnp.zeros((HL, HP), f32),
                jnp.concatenate(
                    [qv[1], jnp.ones((HL, 1), f32), jnp.zeros((HL, HP - HD - 1), f32)], axis=1
                ),
            ]
        ).reshape(3 * HL * HP, 1)

        attn_all, qkv_all, mixed_all, concat_all, lse_all, stats_all, branch, late_full, rows_all, cots = (
            fwd_call(
                NT,
                NP,
                head_gate.reshape(-1),
                block_input,
                cotangent,
                first,
                early_full,
                mods,
                qv_bias,
                late_shards,
            )
        )
        late_full = late_full.reshape(NX, 2, D, FL)

        lhs, rhs, grad_one, grad_mid_out, grad_mid_own, sums, fsums, block_output, go_first = mlp_call(
            NT,
            NP,
            branch,
            rows_all,
            cots.reshape(I, D, T),
            mods,
            group_rows,
            late_full,
        )
        late_grads = grads_call(NT, lhs, rhs)

        gate_sums = jnp.sum(fsums[:, 1].reshape(I, NX * GL, GW), axis=2)
        up_sums = jnp.sum(fsums[:, 0], axis=0)
        all_sums = jnp.sum(sums[:, 3:5], axis=0)

        def x_message(k):
            mine = slice(2 * k * CB, (2 * k + 1) * CB)
            parts = [
                jnp.concatenate(
                    [
                        sums[:, :3, mine].reshape(I, 3 * CB),
                        sums[:, 5, k * CB : (k + 1) * CB],
                        gate_sums[:, k * GL : (k + 1) * GL],
                    ],
                    axis=1,
                ).reshape(-1),
                all_sums[:, mine].reshape(-1),
                up_sums[k * FL : (k + 1) * FL],
            ]
            return jnp.concatenate(parts)

        x_total = x_message(0)
        for k in range(1, NX):
            x_total = x_total + tp_xor(x_message(k), 2 * k)
        per = 4 * CB + GL
        per_image = x_total[: I * per].reshape(I, per)
        late_mods = per_image[:, : 4 * CB].reshape(I, 4, CB)
        grad_group_gate = per_image[:, 4 * CB :]
        bias_sums = x_total[I * per :]

        head_factor = head_mask.astype(f32) * head_sig * (1.0 - head_sig)
        group_logit = grad_group_gate * group_mask.astype(f32) * group_sig * (1.0 - group_sig)
        image_rows = jnp.concatenate(
            [
                jnp.pad(late_mods, ((0, 0), (2, 0), (0, ML - CB))).reshape(I, 6 * ML),
                jnp.zeros((I, HL), f32),
                group_logit,
                jnp.zeros((I, 128 - HL - GL), f32),
            ],
            axis=1,
        )
        widen = lambda v: jnp.pad(v, (0, wide - v.shape[0]))[None]
        base = jnp.concatenate(
            [
                image_rows,
                jnp.zeros((1, wide), f32),
                widen(bias_sums[: 2 * CB]),
                widen(bias_sums[2 * CB :]),
                jnp.zeros((8 - I - 3, wide), f32),
            ],
            axis=0,
        )
        grad_input, late, grad_qkv, grad_out, lasts, cond_sum, _ = bwd_call(
            NT,
            NP,
            head_gate.reshape(-1),
            grad_one.reshape(I, NX, 2, CB, T),
            go_first,
            grad_mid_out,
            grad_mid_own,
            qkv_all,
            mixed_all,
            lse_all,
            concat_all,
            attn_all,
            rows_all,
            stats_all,
            mods,
            early_full,
            late_grads,
            base,
            pad8(head_factor, 128),
            ada,
        )
        grad_up, grad_down = late[0], late[1]
        mods_all = (
            lasts[:, :I, : 6 * ML].reshape(NT * I, 6, ML)[:, :, :CB].reshape(NT * I, 6 * CB)
        )
        logits_all = lasts[:, :I, 6 * ML : 6 * ML + HL + GL].reshape(NT * I, HL + GL)
        bias_rows = jnp.sum(lasts[:, I : I + 3], axis=0)
        qv_rows = bias_rows[0, :QKV].reshape(3, HL, HP)[:, :, :HD].reshape(3, HL * HD)
        cond_f = cond_all[:, :I, :RB].reshape(NT * I, RB)
        time_f = cond_all[:, :I, 256 : 256 + FR].reshape(NT * I, FR)
        grad_w_ada = lax.dot_general(
            cond_f, mods_all, (((0,), (0,)), ((), ())), precision=exact_mode
        ).reshape(RB, 6, CB)
        grad_b_ada = jnp.sum(mods_all, axis=0).reshape(6, CB)
        grad_w_gates = lax.dot_general(
            time_f, logits_all, (((0,), (0,)), ((), ())), precision=exact_mode
        )
        grad_b_gates = jnp.sum(logits_all, axis=0)
        cond_total = cond_sum[:, :I, :RB].transpose(1, 0, 2).reshape(I, D)
        grad_condition = jax.vjp(jax.nn.silu, cond_wide)[1](cond_total)[0]

        return (
            block_output,
            grad_input,
            grad_condition,
            grad_w_ada,
            grad_b_ada,
            grad_qkv.reshape(RB, 3, HL, HP)[..., :HD].reshape(RB, 3, HL * HD),
            jnp.stack([qv_rows[0], qv_rows[2]]),
            grad_out.reshape(RB, HL, HP)[..., :HD].reshape(RB, HL * HD).T,
            bias_rows[1, :CB],
            grad_up,
            bias_rows[2, :FL],
            grad_down.T,
            bias_rows[1, CB : 2 * CB],
            grad_w_gates[:, :HL],
            grad_b_gates[:HL],
            grad_w_gates[:, HL:],
            grad_b_gates[HL:],
        )

    return body


def solution(mesh):
    return jax.shard_map(
        make_body(mesh.shape["tok"], mesh.shape["tp"]),
        mesh=mesh,
        in_specs=(
            P("tok", "tp", None),
            P("tok", None),
            P("tok"),
            P("tok", "tp"),
            P("tok", "tp"),
            P("tok", None, "tp"),
            P(None, "tp"),
            P("tok", None, "tp"),
            P(None, "tp"),
            P("tp", "tok"),
            P("tp"),
            P("tok", "tp"),
            P("tp"),
            P("tp", "tok"),
            P("tp"),
            P("tok", "tp"),
            P("tp"),
            P("tok", "tp"),
            P("tp"),
            P("tok", "tp", None),
        ),
        out_specs=(
            P("tok", "tp", None),
            P("tok", "tp", None),
            P("tok", None),
            P("tok", None, "tp"),
            P(None, "tp"),
            P("tok", None, "tp"),
            P(None, "tp"),
            P("tp", "tok"),
            P("tp"),
            P("tok", "tp"),
            P("tp"),
            P("tp", "tok"),
            P("tp"),
            P("tok", "tp"),
            P("tp"),
            P("tok", "tp"),
            P("tp"),
        ),
        check_vma=False,
    )
```
